32 devices in a mesh: rep: 8 (over y, x, core), shard: 4 (over z).
Axes of the slice: x: 2, y: 2, z: 4, core: 2. Of those that a mesh axis runs over, the one named last changes fastest.
Arguments:
- tokens: bfloat16 [8192, 1536], P(('rep', 'shard')), may hold values from -6 to 6
- norm_gains: bfloat16 [3200], P('shard'), may hold values from 0.5 to 1.5
- w_query: bfloat16 [1536, 1536], P('shard'), may hold values from -0.15625 to 0.15625
- w_key: bfloat16 [1536, 512], P('shard'), may hold values from -0.15625 to 0.15625
- w_value: bfloat16 [1536, 512], P('shard'), may hold values from -0.15625 to 0.15625
- w_out: bfloat16 [1536, 1536], P('shard'), may hold values from -0.875 to 0.875
- w_gate: bfloat16 [1536, 6912], P('shard'), may hold values from -0.15625 to 0.15625
- w_up: bfloat16 [1536, 6912], P('shard'), may hold values from -0.15625 to 0.15625
- w_down: bfloat16 [6912, 1536], P('shard'), may hold values from -0.078125 to 0.078125
- seq_lengths: int32 [64], replicated, may hold values from 1 to 192, as said below
- seq_device: int32 [64], replicated, may hold values from 0 to 31, as said below
- cotangent: bfloat16 [8192, 1536], P(('rep', 'shard')), may hold values from -6 to 6
Outputs:
- mixed: bfloat16 [8192, 1536], P(('rep', 'shard'))
- grad_tokens: float32 [8192, 1536], P(('rep', 'shard'))
- grad_norm_gains: float32 [3200], P('shard')
- grad_w_query: float32 [1536, 1536], P('shard')
- grad_w_key: float32 [1536, 512], P('shard')
- grad_w_value: float32 [1536, 512], P('shard')
- grad_w_out: float32 [1536, 1536], P('shard')
- grad_w_gate: float32 [1536, 6912], P('shard')
- grad_w_up: float32 [1536, 6912], P('shard')
- grad_w_down: float32 [6912, 1536], P('shard')
The draws below stay inside these ranges and needn't reach their ends.
Inputs may be any that keep to these rules, and one draw needn't show every extreme that they name: `seq_lengths`: every device holds exactly 2 sequences; the sequences of one device hold 256 tokens at most and 128 at least together, and in every draw some device holds exactly 256, one of whose sequences has exactly 192 tokens. `seq_device`: devices are numbered along rep first and shard second, as in the tokens' placement.
All inputs are finite; a program needn't handle non-finite values.
Results may differ from the reference program's by a relative error of at most 0.014.
Values may be sent and summed in bfloat16 or wider, within the bound.
No kernel may reach another device: no remote copies, remote signals or barrier semaphores. Data moves between devices by JAX's collectives and lax.ppermute only.
A program may use at most 512 MiB of HBM per device.

```python
import math
import jax
import jax.numpy as jnp
from jax import lax

D = 1536
HEADS = 24
KV_HEADS = 8
HEAD = 64
FF = 6912
TOK_DEV = 256
SEQ_DEV = 2
TOKENS = 8192
SEQS = 64
GAINS = 3200
DEVICES = 32


def deal_sequences(key):
    device_total = SEQS // SEQ_DEV
    load_key, full_key, split_key, order_key = jax.random.split(key, 4)
    loads = jax.random.randint(load_key, (device_total,), TOK_DEV // 2, TOK_DEV + 1)
    fullest = jax.random.randint(full_key, (), 0, device_total)
    is_fullest = jnp.arange(device_total) == fullest
    loads = jnp.where(is_fullest, TOK_DEV, loads)
    shares = jax.random.randint(split_key, (device_total,), 25, 76)
    shares = jnp.where(is_fullest, 25, shares)
    first_part = jnp.maximum(loads * shares // 100, 1)
    lengths = jnp.stack([first_part, loads - first_part], axis=1).reshape(SEQS)
    owners = jnp.arange(SEQS) // SEQ_DEV
    order = jax.random.permutation(order_key, SEQS)
    return (lengths[order].astype(jnp.int32), owners[order].astype(jnp.int32))


def draw_seq_lengths(key, part):
    shared = deal_sequences(key)
    return shared[0]


def draw_seq_device(key, part):
    shared = deal_sequences(key)
    return shared[1]


def shard_levels(stream_key, extent, cuts, smallest, top_value):
    def one(axis_at, blocks):
        steps = jax.random.uniform(jax.random.fold_in(jax.random.fold_in(stream_key, 6), axis_at), (blocks,), jnp.float32, smallest / len(cuts), top_value / len(cuts))
        return jnp.repeat(jnp.exp(steps), extent[axis_at] // blocks).reshape((-1,) + (1,) * (len(extent) - axis_at - 1))

    loudness = one(*cuts[0])
    for cut in cuts[1:]:
        loudness = loudness * one(*cut)
    return loudness


def scatter_about(rng, shape, scale, bound, shards=(), kind=jnp.bfloat16):
    result = jax.random.normal(rng, shape, jnp.float32) * scale
    if len(shards) > 0:
        result = shard_levels(rng, shape, shards, -0.22, 0.18) * result
    return jnp.clip(result, min=-bound, max=bound).astype(kind)


def setup_inputs(seed: int = 0) -> dict:
    arg_keys = jax.random.split(jax.random.key(seed), 13)
    return {
        "tokens": scatter_about(arg_keys[0], (TOKENS, D), 1.0, 6.0, ((0, 32),)),
        "norm_gains": jnp.clip(1.0 + 0.1 * jax.random.normal(arg_keys[1], (GAINS,), jnp.float32), 0.5, 1.5).astype(jnp.bfloat16),
        "w_query": scatter_about(arg_keys[2], (D, HEADS * HEAD), D ** -0.5, 0.15625, ((0, 4),)),
        "w_key": scatter_about(arg_keys[3], (D, KV_HEADS * HEAD), D ** -0.5, 0.15625, ((0, 4),)),
        "w_value": scatter_about(arg_keys[4], (D, KV_HEADS * HEAD), D ** -0.5, 0.15625, ((0, 4),)),
        "w_out": scatter_about(arg_keys[5], (HEADS * HEAD, D), (HEADS * HEAD * 8 // TOK_DEV) ** -0.5, 0.875, ((0, 4),)),
        "w_gate": scatter_about(arg_keys[6], (D, FF), D ** -0.5, 0.15625, ((0, 4),)),
        "w_up": scatter_about(arg_keys[7], (D, FF), D ** -0.5, 0.15625, ((0, 4),)),
        "w_down": scatter_about(arg_keys[8], (FF, D), FF ** -0.5, 0.078125, ((0, 4),)),
        "seq_lengths": draw_seq_lengths(jax.random.fold_in(arg_keys[12], 71), 0),
        "seq_device": draw_seq_device(jax.random.fold_in(arg_keys[12], 71), 0),
        "cotangent": scatter_about(arg_keys[11], (TOKENS, D), 1.0, 6.0, ((0, 32),)),
    }


epsilon = 1e-05
rope_base = 1000000.0
masked_score = -1e+30

@jax.custom_vjp
def low(v):
    return lax.optimization_barrier(v.astype(jnp.bfloat16)).astype(jnp.float32)

@jax.custom_vjp
def low_back(v):
    return v

def low_keep(v):
    return (low(v), None)

def low_pass(kept, grad):
    return (grad,)

def back_keep(v):
    return (v, None)

def back_low(kept, grad):
    return (low(grad),)
low.defvjp(low_keep, low_pass)
low_back.defvjp(back_keep, back_low)

def matmul(left, right):
    return jnp.dot(left, right, precision=lax.Precision.HIGHEST)

def rms_norm(values, gain):
    return values * lax.rsqrt(lax.optimization_barrier(jnp.mean(values * values, axis=-1, keepdims=True)) + epsilon) * gain

def rotary(values, cosine, sine):
    half_width = values.shape[-1] // 2
    first_half = values[..., :half_width]
    second_half = values[..., half_width:]
    cosine = cosine[:, None, :]
    sine = sine[:, None, :]
    return jnp.concatenate([first_half * cosine - second_half * sine, second_half * cosine + first_half * sine], axis=-1)

def rotary_tables(position, head_width):
    half_width = head_width // 2
    index = jnp.arange(half_width).astype(jnp.float32)
    inverse = jnp.exp(index * (-2.0 * math.log(rope_base) / head_width))
    angle = position.astype(jnp.float32)[:, None] * inverse[None, :]
    return (jnp.cos(angle), jnp.sin(angle))

def layout(seq_lengths, seq_device, device, row_total):
    own_length = jnp.where(seq_device == device, seq_lengths, 0).astype(jnp.int32)
    ends = jnp.cumsum(own_length, dtype=jnp.int32)
    begins = ends - own_length
    slot_index = jnp.arange(row_total, dtype=jnp.int32)
    inside = (slot_index[:, None] >= begins[None, :]) & (slot_index[:, None] < ends[None, :])
    live = jnp.any(inside, axis=1)
    seq_total = seq_lengths.shape[0]
    numbers = jnp.arange(seq_total, dtype=jnp.int32)
    found = lax.optimization_barrier(jnp.sum(jnp.where(inside, numbers[None, :], 0), axis=1, dtype=jnp.int32))
    segment = jnp.where(live, found, seq_total + slot_index).astype(jnp.int32)
    offset = lax.optimization_barrier(jnp.sum(jnp.where(inside, (0 - begins)[None, :], 0), axis=1, dtype=jnp.int32))
    position = jnp.where(live, slot_index + offset, 0).astype(jnp.int32)
    return (live, segment, position)

def block_layer(inputs, gains, w_query, w_key, w_value, w_out, w_gate, w_up, w_down, segment, cosine, sine):
    row_count = inputs.shape[0]
    gain_in = gains[:D]
    gain_query = gains[D:D + HEAD]
    gain_key = gains[D + HEAD:D + 2 * HEAD]
    gain_ff = gains[D + 2 * HEAD:]
    normed_in = low(rms_norm(inputs, gain_in))
    query_proj = low_back(matmul(normed_in, w_query))
    key_proj = low_back(matmul(normed_in, w_key))
    value_proj = low(low_back(matmul(normed_in, w_value)))
    queries = low(rotary(rms_norm(query_proj.reshape(row_count, HEADS, HEAD), gain_query), cosine, sine))
    queries = queries.reshape(row_count, KV_HEADS, HEADS // KV_HEADS, HEAD)
    keys = low(rotary(rms_norm(key_proj.reshape(row_count, KV_HEADS, HEAD), gain_key), cosine, sine))
    values = value_proj.reshape(row_count, KV_HEADS, HEAD)
    scores = jnp.einsum('qkgd,tkd->kgqt', queries, keys, precision=lax.Precision.HIGHEST)
    scores = low_back(scores * HEAD ** (-0.5))
    slot_index = jnp.arange(row_count, dtype=jnp.int32)
    allowed = (segment[:, None] == segment[None, :]) & (slot_index[:, None] >= slot_index[None, :])
    scores = jnp.where(allowed, scores, masked_score)
    highest = lax.optimization_barrier(jnp.max(scores, axis=-1, keepdims=True))
    weights = jnp.exp(scores - highest)
    probs = low(weights / lax.optimization_barrier(jnp.sum(weights, axis=-1, keepdims=True)))
    attended = jnp.einsum('kgqt,tkd->qkgd', probs, values, precision=lax.Precision.HIGHEST)
    attended = low_back(low(attended.reshape(row_count, HEADS * HEAD)))
    hidden = inputs + low_back(matmul(attended, w_out))
    normed_ff = low(rms_norm(hidden, gain_ff))
    gate = low_back(matmul(normed_ff, w_gate))
    upward = low_back(matmul(normed_ff, w_up))
    activated = low(jax.nn.silu(gate) * upward)
    return hidden + matmul(activated, w_down)

def reference(tokens, norm_gains, w_query, w_key, w_value, w_out, w_gate, w_up, w_down, seq_lengths, seq_device, cotangent):
    devices = jnp.arange(DEVICES, dtype=jnp.int32)
    live, segments, positions = jax.vmap(lambda device: layout(seq_lengths, seq_device, device, TOK_DEV))(devices)
    cosines, sines = rotary_tables(positions.reshape(TOKENS), HEAD)
    cosines = cosines.reshape(DEVICES, TOK_DEV, HEAD // 2)
    sines = sines.reshape(DEVICES, TOK_DEV, HEAD // 2)
    inputs = tokens.astype(jnp.float32).reshape(DEVICES, TOK_DEV, D)
    weights = tuple((item.astype(jnp.float32) for item in (norm_gains, w_query, w_key, w_value, w_out, w_gate, w_up, w_down)))

    def whole(block_inputs, gains, query_w, key_w, value_w, out_w, gate_w, up_w, down_w):

        def one_device(items):
            device_rows, segment, cosine, sine = items
            return block_layer(device_rows, gains, query_w, key_w, value_w, out_w, gate_w, up_w, down_w, segment, cosine, sine)
        return lax.map(jax.checkpoint(one_device), (block_inputs, segments, cosines, sines))
    outputs, backward = jax.vjp(whole, inputs, *weights)
    live_rows = live[..., None]
    seed_grad = jnp.where(live_rows, cotangent.astype(jnp.float32).reshape(DEVICES, TOK_DEV, D), jnp.zeros((), jnp.float32))
    grads = backward(seed_grad)
    mixed = jnp.where(live_rows, outputs, jnp.zeros((), jnp.float32)).reshape(TOKENS, D).astype(jnp.bfloat16)
    return (mixed, grads[0].reshape(TOKENS, D), grads[1], grads[2], grads[3], grads[4], grads[5], grads[6], grads[7], grads[8])
```

```python
import math

import jax
import jax.numpy as jnp
from jax import lax
from jax.sharding import PartitionSpec as P

D = 1536
HEADS = 24
KV_HEADS = 8
HEAD = 64
FF = 6912


epsilon = 1e-05
rope_base = 1000000.0
masked_score = -1e30


def plain_product(left, right):
    return jnp.dot(left, right, preferred_element_type=jnp.float32)


def product_over_rows(left, right):
    return lax.dot_general(
        left, right, (((0,), (0,)), ((), ())), preferred_element_type=jnp.float32
    )


def product_with_transpose(left, right):
    return lax.dot_general(
        left, right, (((1,), (1,)), ((), ())), preferred_element_type=jnp.float32
    )


def rms_norm(values, gain):
    return values * lax.rsqrt(jnp.mean(values * values, axis=-1, keepdims=True) + epsilon) * gain


def rotary(values, cosine, sine):
    half_width = values.shape[-1] // 2
    first_half = values[..., :half_width]
    second_half = values[..., half_width:]
    cosine = cosine[:, None, :]
    sine = sine[:, None, :]
    return jnp.concatenate(
        [first_half * cosine - second_half * sine, second_half * cosine + first_half * sine],
        axis=-1,
    )


def head_part(projection, gain, cosine, sine, head_count):
    shaped = projection.reshape(projection.shape[0], head_count, HEAD)
    return rotary(rms_norm(shaped, gain), cosine, sine)


def gated_product(gate, upward):
    return jax.nn.silu(gate) * upward


def rotary_tables(position, head_width):
    half_width = head_width // 2
    index = jnp.arange(half_width).astype(jnp.float32)
    inverse = jnp.exp(index * (-2.0 * math.log(rope_base) / head_width))
    angle = position.astype(jnp.float32)[:, None] * inverse[None, :]
    return (jnp.cos(angle), jnp.sin(angle))


def layout(seq_lengths, seq_device, device, row_total):
    own_length = jnp.where(seq_device == device, seq_lengths, 0)
    ends = jnp.cumsum(own_length, dtype=jnp.int32)
    begins = ends - own_length
    slot_index = jnp.arange(row_total, dtype=jnp.int32)
    inside = (slot_index[:, None] >= begins[None, :]) & (slot_index[:, None] < ends[None, :])
    live = jnp.any(inside, axis=1)
    seq_total = seq_lengths.shape[0]
    numbers = jnp.arange(seq_total, dtype=jnp.int32)
    found = jnp.sum(jnp.where(inside, numbers[None, :], 0), axis=1, dtype=jnp.int32)
    segment = jnp.where(live, found, seq_total + slot_index)
    offset = jnp.sum(jnp.where(inside, (0 - begins)[None, :], 0), axis=1, dtype=jnp.int32)
    position = jnp.where(live, slot_index + offset, 0)
    return (live, segment, position)


def score_block(query_block, keys, segment, block_start):
    row_total = keys.shape[0]
    block_rows = query_block.shape[0]
    scores = jnp.einsum(
        "qkgd,tkd->kgqt", query_block, keys, preferred_element_type=jnp.float32
    ) * HEAD ** (-0.5)
    block_slots = block_start + jnp.arange(block_rows, dtype=jnp.int32)
    all_slots = jnp.arange(row_total, dtype=jnp.int32)
    allowed = (segment[:, None] == segment[None, :]) & (block_slots[:, None] >= all_slots[None, :])
    return jnp.where(allowed, scores, masked_score)


def attend_forward(queries, keys, values, segment):
    row_total = queries.shape[0]
    block_rows = min(row_total, 512)

    def one_block(block_index):
        block_start = block_index * block_rows
        scores = score_block(queries, keys, segment, block_start)
        highest = jnp.max(scores, axis=-1, keepdims=True)
        weights = jnp.exp(scores - highest)
        totals = jnp.sum(weights, axis=-1, keepdims=True)
        probs = (weights / totals).astype(jnp.bfloat16)
        output = jnp.einsum("kgqt,tkd->qkgd", probs, values, preferred_element_type=jnp.float32)
        return (output, (highest + jnp.log(totals))[..., 0])

    outputs, log_totals = lax.map(one_block, jnp.arange(row_total // block_rows))
    return (outputs.reshape(queries.shape), log_totals)


def attend_backward(queries, keys, values, grad_out, log_totals, segment):
    row_total = queries.shape[0]
    block_rows = min(row_total, 512)
    scale = HEAD ** (-0.5)

    def one_block(carry, block_index):
        grad_keys, grad_values = carry
        block_start = block_index * block_rows
        scores = score_block(queries, keys, segment, block_start)
        probs = jnp.exp(scores - log_totals[block_index][..., None])
        grad_probs = jnp.einsum(
            "qkgd,tkd->kgqt", grad_out, values, preferred_element_type=jnp.float32
        )
        inner = jnp.sum(probs * grad_probs, axis=-1, keepdims=True)
        grad_scores = (probs * (grad_probs - inner)).astype(jnp.bfloat16)
        probs_low = probs.astype(jnp.bfloat16)
        grad_query = (
            jnp.einsum("kgqt,tkd->qkgd", grad_scores, keys, preferred_element_type=jnp.float32)
            * scale
        )
        grad_keys = (
            grad_keys
            + jnp.einsum("kgqt,qkgd->tkd", grad_scores, queries, preferred_element_type=jnp.float32)
            * scale
        )
        grad_values = grad_values + jnp.einsum(
            "kgqt,qkgd->tkd", probs_low, grad_out, preferred_element_type=jnp.float32
        )
        return ((grad_keys, grad_values), grad_query)

    zeros = jnp.zeros(keys.shape, jnp.float32)
    (grad_keys, grad_values), grad_queries = lax.scan(
        one_block, (zeros, zeros), jnp.arange(row_total // block_rows)
    )
    return (grad_queries.reshape(queries.shape), grad_keys, grad_values)


def swap(values, offset):
    size = lax.axis_size("rep")
    return lax.ppermute(values, "rep", [(i, i ^ offset) for i in range(size)])


def from_ahead(values, steps):
    size = lax.axis_size("shard")
    return lax.ppermute(values, "shard", [((i + steps) % size, i) for i in range(size)])


def gather_plane(block):
    chips = lax.axis_size("rep") // 2
    mine = [block] + [swap(block, 2 * d) for d in range(1, chips)]
    same_core = jnp.stack(mine)
    return jnp.concatenate([same_core, swap(same_core, 1)], axis=0)


def scatter_plane(blocks):
    chips = lax.axis_size("rep") // 2
    mine = blocks[:chips].astype(jnp.float32) + swap(blocks[chips:], 1).astype(jnp.float32)
    low = mine.astype(jnp.bfloat16)
    total = mine[0]
    for d in range(1, chips):
        total = total + swap(low[d], 2 * d).astype(jnp.float32)
    return total


def place(total, parts, index_of):
    for m, part in enumerate(parts):
        total = lax.dynamic_update_slice_in_dim(total, part[None], index_of(m), 0)
    return total


def plane_order(m):
    chips = lax.axis_size("rep") // 2
    return lax.axis_index("rep") ^ (2 * (m % chips) + m // chips)


def gather_weights(own):
    size, reps = lax.axis_size("shard"), lax.axis_size("rep")
    here, rep = lax.axis_index("shard"), lax.axis_index("rep")
    rows, columns = own.shape
    share = rows // reps
    mine = lax.dynamic_slice_in_dim(own, rep * share, share, 0)
    total = jnp.zeros((size, reps, share, columns), own.dtype)
    total = lax.dynamic_update_slice_in_dim(total, own.reshape(1, reps, share, columns), here, 0)
    arrived = []
    for k in range(1, size):
        slot = from_ahead(mine, k)
        arrived.append(slot)
        blocks = gather_plane(slot)
        at = (here + k) % size
        for m in range(reps):
            total = lax.dynamic_update_slice(
                total, blocks[m][None, None], (at, plane_order(m), 0, 0)
            )
    return total.reshape(size * rows, columns), arrived


def scatter_gradient(partial):
    size, reps = lax.axis_size("shard"), lax.axis_size("rep")
    here, rep = lax.axis_index("shard"), lax.axis_index("rep")
    chips = reps // 2
    rows, columns = partial.shape
    share = rows // size // reps
    cut = partial.reshape(size, chips, 2, share, columns)
    core, chip = rep % 2, rep // 2
    take = lambda array, index, axis: lax.dynamic_index_in_dim(array, index, axis, keepdims=False)
    both = take(cut, core, 2).astype(jnp.float32) + swap(take(cut, 1 - core, 2), 1).astype(
        jnp.float32
    )
    low = both.astype(jnp.bfloat16)
    total = take(both, chip, 1)
    for d in range(1, chips):
        total = total + swap(take(low, chip ^ d, 1), 2 * d).astype(jnp.float32)
    low = total.astype(jnp.bfloat16)
    owned = take(total, here, 0)
    for k in range(1, size):
        owned = owned + from_ahead(take(low, (here + size - k) % size, 0), k).astype(jnp.float32)
    blocks = gather_plane(owned.astype(jnp.bfloat16))
    result = jnp.zeros((reps, share, columns), jnp.bfloat16)
    for m in range(reps):
        result = lax.dynamic_update_slice(result, blocks[m][None], (plane_order(m), 0, 0))
    return result.reshape(reps * share, columns).astype(jnp.float32)


def sum_everywhere(values):
    step = 1
    while step < lax.axis_size("rep"):
        values = values + swap(values, step)
        step *= 2
    step = 1
    size = lax.axis_size("shard")
    while step < size:
        values = values + lax.ppermute(values, "shard", [(i, i ^ step) for i in range(size)])
        step *= 2
    return values


def gather_gains(own):
    size, here = lax.axis_size("shard"), lax.axis_index("shard")
    total = jnp.zeros((size,) + own.shape, own.dtype)
    for k in range(size):
        slot = own if k == 0 else from_ahead(own, k)
        total = lax.dynamic_update_slice(total, slot[None], ((here + k) % size, 0))
    return total.reshape(-1)


def own_columns(weight):
    size, reps = lax.axis_size("shard"), lax.axis_size("rep")
    run = weight.shape[1] // size
    share = run // reps
    rep = lax.axis_index("rep")
    return jnp.concatenate(
        [lax.dynamic_slice_in_dim(weight, z * run + rep * share, share, 1) for z in range(size)],
        axis=1,
    )


def whole_columns(blocks):
    size, reps = lax.axis_size("shard"), lax.axis_size("rep")
    share = blocks.shape[2] // size
    ordered = [
        lax.dynamic_index_in_dim(blocks, plane_order_inverse(j), 0, keepdims=False)
        for j in range(reps)
    ]
    parts = [ordered[j][:, z * share : (z + 1) * share] for z in range(size) for j in range(reps)]
    return jnp.concatenate(parts, axis=1).astype(jnp.float32)


def plane_order_inverse(j):
    chips = lax.axis_size("rep") // 2
    offset = lax.axis_index("rep") ^ j
    return (offset % 2) * chips + offset // 2


def local(
    tokens,
    norm_gains,
    w_query,
    w_key,
    w_value,
    w_out,
    w_gate,
    w_up,
    w_down,
    seq_lengths,
    seq_device,
    cotangent,
):
    row_total = tokens.shape[0]
    size, reps = lax.axis_size("shard"), lax.axis_size("rep")
    rep = lax.axis_index("rep")
    device = rep * size + lax.axis_index("shard")
    group_ratio = HEADS // KV_HEADS
    query_width, key_width = HEADS * HEAD, KV_HEADS * HEAD

    gains = gather_gains(norm_gains)
    joint = jnp.concatenate([w_query, w_key, w_value], axis=1)
    joint_full, joint_slots = gather_weights(joint)
    w_out, joint_slots = lax.optimization_barrier((w_out, joint_slots))
    out_full, out_slots = gather_weights(w_out)
    gate_own, up_own = own_columns(w_gate), own_columns(w_up)
    down_share = w_down.shape[0] // reps
    down_own = lax.dynamic_slice_in_dim(w_down, rep * down_share, down_share, 0)
    gate_own, up_own, down_own, out_slots = lax.optimization_barrier(
        (gate_own, up_own, down_own, out_slots)
    )
    gate_full = lax.all_gather(gate_own, "shard", axis=0, tiled=True)
    up_full = lax.all_gather(up_own, "shard", axis=0, tiled=True)
    down_full = lax.all_gather(down_own, "shard", axis=0, tiled=True)

    live, segment, position = layout(seq_lengths, seq_device, device, row_total)
    cosine, sine = rotary_tables(position, HEAD)
    cotangent_live = jnp.where(live[:, None], cotangent, jnp.zeros_like(cotangent))
    cotangent_group = gather_plane(cotangent_live).reshape(-1, D)

    gains = gains.astype(jnp.float32)
    gain_in = gains[:D]
    gain_query = gains[D : D + HEAD]
    gain_key = gains[D + HEAD : D + 2 * HEAD]
    gain_ff = gains[D + 2 * HEAD :]
    inputs = tokens.astype(jnp.float32)
    normed_in_full, back_in = jax.vjp(rms_norm, inputs, gain_in)
    normed_in = normed_in_full.astype(jnp.bfloat16)
    joint_proj = plain_product(normed_in, joint_full)
    query_proj = joint_proj[:, :query_width]
    key_proj = joint_proj[:, query_width : query_width + key_width]
    value_proj = joint_proj[:, query_width + key_width :]
    query_rot, back_query = jax.vjp(
        lambda proj, gain: head_part(proj, gain, cosine, sine, HEADS), query_proj, gain_query
    )
    key_rot, back_key = jax.vjp(
        lambda proj, gain: head_part(proj, gain, cosine, sine, KV_HEADS), key_proj, gain_key
    )
    queries = query_rot.astype(jnp.bfloat16).reshape(row_total, KV_HEADS, group_ratio, HEAD)
    keys = key_rot.astype(jnp.bfloat16)
    values = value_proj.astype(jnp.bfloat16).reshape(row_total, KV_HEADS, HEAD)
    attended_full, log_totals = attend_forward(queries, keys, values, segment)
    attended = attended_full.reshape(row_total, HEADS * HEAD).astype(jnp.bfloat16)
    hidden = inputs + plain_product(attended, out_full)
    normed_ff_full, back_ff = jax.vjp(rms_norm, hidden, gain_ff)
    normed_ff = gather_plane(normed_ff_full.astype(jnp.bfloat16)).reshape(-1, D)

    gate = plain_product(normed_ff, gate_full)
    upward = plain_product(normed_ff, up_full)
    activated, back_gated = jax.vjp(gated_product, gate, upward)
    activated = activated.astype(jnp.bfloat16)
    grad_down = lax.psum_scatter(
        product_over_rows(activated, cotangent_group).astype(jnp.bfloat16),
        "shard",
        scatter_dimension=0,
        tiled=True,
    )
    grad_act = product_with_transpose(cotangent_group, down_full)
    grad_gate_full, grad_up_full = back_gated(grad_act)
    grad_gate_low = grad_gate_full.astype(jnp.bfloat16)
    grad_up_low = grad_up_full.astype(jnp.bfloat16)
    grad_normed_ff = product_with_transpose(grad_gate_low, gate_full) + product_with_transpose(
        grad_up_low, up_full
    )
    grad_normed_ff = scatter_plane(
        grad_normed_ff.astype(jnp.bfloat16).reshape(reps, row_total, D)
    )
    grad_gate = lax.psum_scatter(
        product_over_rows(normed_ff, grad_gate_low).astype(jnp.bfloat16),
        "shard",
        scatter_dimension=0,
        tiled=True,
    )
    grad_up = lax.psum_scatter(
        product_over_rows(normed_ff, grad_up_low).astype(jnp.bfloat16),
        "shard",
        scatter_dimension=0,
        tiled=True,
    )
    down_term = scatter_plane(
        plain_product(activated, down_full).astype(jnp.bfloat16).reshape(reps, row_total, D)
    )
    mixed_full = hidden + down_term
    mixed = jnp.where(live[:, None], mixed_full, jnp.zeros_like(mixed_full)).astype(jnp.bfloat16)

    grad_hidden_norm, grad_gain_ff = back_ff(grad_normed_ff)
    grad_hidden = cotangent_live.astype(jnp.float32) + grad_hidden_norm
    grad_attn_low = grad_hidden.astype(jnp.bfloat16)
    grad_out_w = scatter_gradient(product_over_rows(attended, grad_attn_low).astype(jnp.bfloat16))
    grad_attended = product_with_transpose(grad_attn_low, out_full).astype(jnp.bfloat16)
    grad_attended = grad_attended.reshape(row_total, KV_HEADS, group_ratio, HEAD)
    grad_queries, grad_keys, grad_values = attend_backward(
        queries, keys, values, grad_attended, log_totals, segment
    )
    grad_query_proj, grad_gain_query = back_query(grad_queries.reshape(row_total, HEADS, HEAD))
    grad_key_proj, grad_gain_key = back_key(grad_keys)
    grad_joint_low = jnp.concatenate(
        [
            grad_query_proj.astype(jnp.bfloat16),
            grad_key_proj.astype(jnp.bfloat16),
            grad_values.reshape(row_total, key_width).astype(jnp.bfloat16),
        ],
        axis=1,
    )
    grad_joint = scatter_gradient(
        product_over_rows(normed_in, grad_joint_low).astype(jnp.bfloat16)
    )
    grad_normed_in = product_with_transpose(grad_joint_low, joint_full)
    grad_input_norm, grad_gain_in = back_in(grad_normed_in)
    grad_tokens = grad_hidden + grad_input_norm
    grad_gains = sum_everywhere(
        jnp.concatenate([grad_gain_in, grad_gain_query, grad_gain_key, grad_gain_ff])
    )
    own_gains = norm_gains.shape[0]
    grad_gains = lax.dynamic_slice_in_dim(grad_gains, lax.axis_index("shard") * own_gains, own_gains, 0)

    down_blocks = gather_plane(grad_down)
    whole_down = jnp.zeros(down_blocks.shape, jnp.float32)
    for m in range(reps):
        whole_down = lax.dynamic_update_slice(
            whole_down, down_blocks[m][None].astype(jnp.float32), (plane_order(m), 0, 0)
        )
    return (
        mixed,
        grad_tokens,
        grad_gains,
        grad_joint[:, :query_width],
        grad_joint[:, query_width : query_width + key_width],
        grad_joint[:, query_width + key_width :],
        grad_out_w,
        whole_columns(gather_plane(grad_gate)),
        whole_columns(gather_plane(grad_up)),
        whole_down.reshape(-1, D),
    )


def solution(mesh):
    return jax.shard_map(
        local,
        mesh=mesh,
        in_specs=(
            P(("rep", "shard"), None),
            P("shard"),
            P("shard", None),
            P("shard", None),
            P("shard", None),
            P("shard", None),
            P("shard", None),
            P("shard", None),
            P("shard", None),
            P(),
            P(),
            P(("rep", "shard"), None),
        ),
        out_specs=(
            P(("rep", "shard"), None),
            P(("rep", "shard"), None),
            P("shard"),
            P("shard", None),
            P("shard", None),
            P("shard", None),
            P("shard", None),
            P("shard", None),
            P("shard", None),
            P("shard", None),
        ),
        check_vma=False,
    )
```

```python
import math

import jax
import jax.numpy as jnp
from jax import lax
from jax.experimental import pallas as pl
from jax.experimental.pallas import tpu as pltpu
from jax.sharding import PartitionSpec as P

D = 1536
HEADS = 24
KV_HEADS = 8
HEAD = 64
FF = 6912


epsilon = 1e-05
rope_base = 1000000.0
masked_score = -1e30


def plain_product(left, right):
    return jnp.dot(left, right, preferred_element_type=jnp.float32)


def product_over_rows(left, right):
    return lax.dot_general(
        left, right, (((0,), (0,)), ((), ())), preferred_element_type=jnp.float32
    )


def product_with_transpose(left, right):
    return lax.dot_general(
        left, right, (((1,), (1,)), ((), ())), preferred_element_type=jnp.float32
    )


def rotary_tables(position, head_width):
    half_width = head_width // 2
    index = jnp.arange(half_width).astype(jnp.float32)
    inverse = jnp.exp(index * (-2.0 * math.log(rope_base) / head_width))
    angle = position.astype(jnp.float32)[:, None] * inverse[None, :]
    return (jnp.cos(angle), jnp.sin(angle))


def layout(seq_lengths, seq_device, device, row_total):
    own_length = jnp.where(seq_device == device, seq_lengths, 0)
    ends = jnp.cumsum(own_length, dtype=jnp.int32)
    begins = ends - own_length
    slot_index = jnp.arange(row_total, dtype=jnp.int32)
    inside = (slot_index[:, None] >= begins[None, :]) & (slot_index[:, None] < ends[None, :])
    live = jnp.any(inside, axis=1)
    seq_total = seq_lengths.shape[0]
    numbers = jnp.arange(seq_total, dtype=jnp.int32)
    found = jnp.sum(jnp.where(inside, numbers[None, :], 0), axis=1, dtype=jnp.int32)
    segment = jnp.where(live, found, seq_total + slot_index)
    offset = jnp.sum(jnp.where(inside, (0 - begins)[None, :], 0), axis=1, dtype=jnp.int32)
    position = jnp.where(live, slot_index + offset, 0)
    return (live, segment, position)


vmem_bytes = 60 * 2**20
low_type = jnp.bfloat16
in_place = pl.BlockSpec(memory_space=pl.ANY)


def swap(values, offset):
    size = lax.axis_size("rep")
    return lax.ppermute(values, "rep", [(i, i ^ offset) for i in range(size)])


def from_ahead(values, steps):
    size = lax.axis_size("shard")
    return lax.ppermute(values, "shard", [((i + steps) % size, i) for i in range(size)])


def from_behind(values, steps):
    size = lax.axis_size("shard")
    return lax.ppermute(values, "shard", [(i, (i + steps) % size) for i in range(size)])


def after(values, *others):
    return lax.optimization_barrier((values, others))[0]


def near_groups(block, unit):
    groups = lax.axis_size("rep") // unit
    return [swap(block, unit * d) for d in range(1, groups if groups != 4 else 3)]


def far_group(near, unit):
    if lax.axis_size("rep") // unit != 4:
        return []
    half = half_rows(near[0].shape[0])
    return [swap(near[1][:half], unit), swap(near[0][half:], 2 * unit)]


def half_rows(rows):
    return rows // 2 // 16 * 16


def piece_rows(groups, rows):
    half = half_rows(rows)
    return [[rows]] * groups if groups != 4 else [[rows]] * 3 + [[half, rows - half]]


def far_terms(blocks, unit):
    return [swap(blocks[3][0], unit), swap(blocks[3][1], 2 * unit)] if len(blocks) == 4 else []


def near_terms(blocks, far, unit):
    if not far:
        return blocks[0] + [swap(block[0], unit * d) for d, block in enumerate(blocks) if d]
    half = blocks[3][0].shape[0]
    one, two = blocks[1][0], blocks[2][0]
    add = lambda left, right: (left.astype(jnp.float32) + right.astype(jnp.float32)).astype(low_type)
    one = jnp.concatenate([one[:half], add(one[half:], far[1])], axis=0)
    two = jnp.concatenate([add(two[:half], far[0]), two[half:]], axis=0)
    return blocks[0] + [swap(one, unit), swap(two, 2 * unit)]


def flat(groups):
    return [piece for group in groups for piece in group]


def piece_copies(rows, refs, target, sems):
    copies, at, n = [], 0, 0
    for i, group in enumerate(rows):
        for count in group:
            copies.append(
                pltpu.make_async_copy(refs[n], target.at[pl.ds(at, count)], sems.at[i])
            )
            at += count
            n += 1
    return copies


def call_kernel(kernel, args, ins, outs, flops, name, grid=None, prefetch=0, scratch=()):
    return pl.pallas_call(
        kernel,
        grid_spec=pltpu.PrefetchScalarGridSpec(
            num_scalar_prefetch=prefetch,
            grid=grid or (1,),
            in_specs=ins,
            out_specs=[spec for spec, _ in outs],
            scratch_shapes=list(scratch),
        ),
        out_shape=[jax.ShapeDtypeStruct(*shape) for _, shape in outs],
        compiler_params=pltpu.CompilerParams(vmem_limit_bytes=vmem_bytes),
        cost_estimate=pl.CostEstimate(flops=flops, bytes_accessed=0, transcendentals=0),
        name=name,
    )(*args)


def resident(shape):
    return pl.BlockSpec(shape, lambda *_: (0,) * len(shape), pipeline_mode=pl.Buffered(1))


def spread(values, shards, members):
    part = values.shape[1] // shards // members
    return [
        jnp.concatenate(
            [values[:, (z * members + p) * part :][:, :part] for z in range(shards)], axis=1
        )
        for p in range(members)
    ]


def unspread(parts, shards):
    part = parts[0].shape[1] // shards
    return jnp.concatenate(
        [run[:, z * part : (z + 1) * part] for z in range(shards) for run in parts], axis=1
    )


def norm_factor(values):
    return lax.rsqrt(jnp.mean(values * values, axis=-1, keepdims=True) + epsilon)


def norm_gradient(values, gain, grad):
    factor = norm_factor(values)
    scaled = grad * gain
    mean = jnp.mean(scaled * values, axis=-1, keepdims=True)
    by_gain = jnp.sum(grad * values * factor, axis=0, keepdims=True)
    return factor * scaled - values * (factor * factor * factor * mean), by_gain


class Tiles:
    def __init__(self, weight):
        reps = lax.axis_size("rep")
        groups = reps // 2
        while weight.shape[1] % (128 * groups):
            groups //= 2
        self.groups, self.members = groups, reps // groups
        self.shards, self.here = lax.axis_size("shard"), lax.axis_index("shard")
        self.group = lax.axis_index("rep") // self.members
        self.member = lax.axis_index("rep") % self.members
        self.rows = weight.shape[0]
        self.part = self.rows // self.members
        self.rest = (self.shards - 1) * self.part
        self.depth = self.shards * self.part
        self.width = weight.shape[1] // groups

    def own(self, weight):
        return lax.dynamic_slice(
            weight, (self.member * self.part, self.group * self.width), (self.part, self.width)
        )

    def across(self, pieces):
        return pieces + [swap(piece, h) for h in range(1, self.members) for piece in pieces]

    def place(self):
        return jnp.stack([self.group, self.member, self.here]).astype(jnp.int32)

    def scratch(self):
        shape = (self.members, self.groups)
        return [
            pltpu.VMEM(shape + (self.depth, self.width), low_type),
            pltpu.SemaphoreType.DMA(shape),
        ]

    def load(self, at, weight_ref, refs, tiles, sems):
        part, shards = self.part, self.shards
        cuts = piece_rows(self.groups, self.rest)
        count = sum(len(group) for group in cuts)

        def to(h, d, z, start, size):
            first = pl.multiple_of(lax.rem(at[2] + z, shards) * part, 16) + start
            return tiles.at[h, d, pl.ds(pl.multiple_of(first, 16), size)]

        n = 0
        for d in range(self.groups):
            for h in range(self.members):
                source = weight_ref.at[
                    pl.ds(pl.multiple_of((at[1] ^ h) * part, 16), part),
                    pl.ds(pl.multiple_of((at[0] ^ d) * self.width, 128), self.width),
                ]
                pltpu.make_async_copy(source, to(h, d, 0, 0, part), sems.at[h, d]).start()
                row = 0
                for i, size in enumerate(cuts[d]):
                    ref, end = refs[h * count + n + i], row + size
                    base = row
                    while row < end:
                        run = min(end, (row // part + 1) * part) - row
                        pltpu.make_async_copy(
                            ref.at[pl.ds(row - base, run)],
                            to(h, d, row // part + 1, row % part, run),
                            sems.at[h, d],
                        ).start()
                        row += run
            n += len(cuts[d])

        def wait(h, d):
            pltpu.make_async_copy(tiles.at[h, d], tiles.at[h, d], sems.at[h, d]).wait()
            return tiles[h, d]

        return wait

    def flops(self, row_total):
        return 2 * row_total * self.shards * self.rows * self.groups * self.width

    def columns(self, at, d):
        return pl.ds(pl.multiple_of((at[0] ^ d) * self.width, 128), self.width)

    def multiply(self, at, wait, x, out):
        for d in range(self.groups):
            total = None
            for h in range(self.members):
                term = plain_product(x[at[1] ^ h], wait(h, d))
                total = term if total is None else total + term
            out[:, self.columns(at, d)] = total

    def multiply_transposed(self, at, wait, grad, out):
        totals = [None] * self.members
        for d in range(self.groups):
            block = grad[:, self.columns(at, d)]
            for h in range(self.members):
                term = product_with_transpose(block, wait(h, d))
                totals[h] = term if totals[h] is None else totals[h] + term
        for h in range(self.members):
            out[at[1] ^ h] = totals[h]

    def call(self, kernel, args, weight, pieces, outs, name, scratch=()):
        given, produced = len(args), len(outs)

        def whole_kernel(at, *refs):
            ins, weight_ref = refs[:given], refs[given]
            rest = refs[given + 1 + len(pieces) :]
            wait = self.load(
                at, weight_ref, refs[given + 1 : given + 1 + len(pieces)], *rest[produced : produced + 2]
            )
            kernel(at, ins, rest[:produced], rest[produced + 2 :], wait)

        return call_kernel(
            whole_kernel,
            [self.place(), *args, weight, *pieces],
            [resident(arg.shape) for arg in args] + [in_place] * (1 + len(pieces)),
            [(resident(shape), (shape, kind)) for shape, kind in outs],
            self.flops(args[0].shape[0]),
            name,
            prefetch=1,
            scratch=self.scratch() + list(scratch),
        )

    def member_rows(self, parts):
        pick = lambda h: lax.dynamic_index_in_dim(parts, self.member ^ h, 0, keepdims=False)
        return [pick(0)] + [swap(pick(h), h) for h in range(1, self.members)]

    def group_columns(self, grad):
        runs = []
        for d in range(self.groups):
            run = lax.dynamic_slice_in_dim(grad, (self.group ^ d) * self.width, self.width, 1)
            runs.append(swap(run, self.members * d) if d else run)
        return runs

    def all_columns(self, runs):
        every = []
        for run in runs:
            every += [run] + [swap(run, h) for h in range(1, self.members)]
        return every

    def tile(self, rows, columns):
        tokens = columns[0].shape[0]
        count, total = len(rows), len(columns) * tokens
        sizes = [piece.shape[0] for piece in rows]

        def kernel(at, *refs):
            outs = refs[count + len(columns) : -4]
            left, right, whole, sems = refs[-4:]
            copies = piece_copies([sizes], refs[:count], left, sems.at[pl.ds(0, 1)])
            copies += piece_copies(
                [[tokens] * len(columns)], refs[count : count + len(columns)], right, sems.at[pl.ds(1, 1)]
            )
            for copy in copies:
                copy.start()
            pltpu.make_async_copy(left, left, sems.at[0]).wait()
            pltpu.make_async_copy(right, right, sems.at[1]).wait()
            whole[...] = product_over_rows(left[...], right[...])
            for k, out in enumerate(outs):
                start = pl.multiple_of(lax.rem(at[2] + k, self.shards) * self.part, 16)
                out[...] = whole[pl.ds(start, self.part), :].astype(out.dtype)

        shape = (self.part, self.width)
        outs = call_kernel(
            kernel,
            [self.place(), *rows, *columns],
            [in_place] * (count + len(columns)),
            [(resident(shape), (shape, low_type if k else jnp.float32)) for k in range(self.shards)],
            2 * total * self.depth * self.width,
            "weight_tile",
            prefetch=1,
            scratch=[
                pltpu.VMEM((total, self.depth), low_type),
                pltpu.VMEM((total, self.width), low_type),
                pltpu.VMEM((self.depth, self.width), jnp.float32),
                pltpu.SemaphoreType.DMA((2,)),
            ],
        )
        return outs[0], [from_behind(outs[k], k) for k in range(1, self.shards)]

    def whole(self, own, sent):
        for part in sent:
            own = own + part.astype(jnp.float32)
        own = own.astype(low_type)
        near = near_groups(own, self.members)
        far = far_group(near, self.members)
        blocks = [own] + near + ([jnp.concatenate(far, axis=0)] if far else [])
        mine = jnp.concatenate(blocks, axis=1)
        every = jnp.stack([mine] + [swap(mine, h) for h in range(1, self.members)])
        ordered = jnp.concatenate(
            [
                lax.dynamic_index_in_dim(every, p ^ self.member, 0, keepdims=False)
                for p in range(self.members)
            ],
            axis=0,
        )
        return jnp.concatenate(
            [
                lax.dynamic_slice_in_dim(ordered, (self.group ^ d) * self.width, self.width, 1)
                for d in range(self.groups)
            ],
            axis=1,
        ).astype(jnp.float32)


def attention_input(tiles, tokens, gain, weight, pieces):
    def kernel(at, ins, outs, scratch, wait):
        x = ins[0][...].astype(jnp.float32)
        normed = (x * norm_factor(x) * ins[1][...]).astype(low_type)
        for p, run in enumerate(spread(normed, tiles.shards, tiles.members)):
            outs[1][p] = run
        tiles.multiply(at, wait, outs[1], outs[0])

    rows = tokens.shape[0]
    return tiles.call(
        kernel,
        [tokens, gain],
        weight,
        pieces,
        [
            ((rows, weight.shape[1]), jnp.float32),
            ((tiles.members, rows, tiles.depth), low_type),
        ],
        "attention_input",
    )


def attention_output(tiles, attended, tokens, gain, weight, pieces):
    def kernel(at, ins, outs, scratch, wait):
        for p, run in enumerate(spread(ins[0][...], tiles.shards, tiles.members)):
            outs[2][p] = run
        tiles.multiply(at, wait, outs[2], outs[0])
        hidden = outs[0][...] + ins[1][...].astype(jnp.float32)
        outs[0][...] = hidden
        outs[1][...] = (hidden * norm_factor(hidden) * ins[2][...]).astype(low_type)

    rows, depth = tokens.shape
    return tiles.call(
        kernel,
        [attended, tokens, gain],
        weight,
        pieces,
        [
            ((rows, depth), jnp.float32),
            ((rows, depth), low_type),
            ((tiles.members, rows, tiles.depth), low_type),
        ],
        "attention_output",
    )


def attention_output_gradient(tiles, terms, grad, hidden, gain, weight, pieces):
    count = len(terms)

    def kernel(at, ins, outs, scratch, wait):
        total = ins[0][...].astype(jnp.float32)
        for term in ins[1:count]:
            total = total + term[...].astype(jnp.float32)
        by_hidden, by_gain = norm_gradient(ins[count + 1][...], ins[count + 2][...], total)
        by_hidden = by_hidden + ins[count][...].astype(jnp.float32)
        outs[0][...] = by_hidden
        outs[1][...] = by_hidden.astype(low_type)
        outs[3][...] = by_gain
        tiles.multiply_transposed(at, wait, outs[1], scratch[0])
        runs = [scratch[0][p].astype(low_type) for p in range(tiles.members)]
        outs[2][...] = unspread(runs, tiles.shards)

    rows, depth = grad.shape
    return tiles.call(
        kernel,
        [*terms, grad, hidden, gain],
        weight,
        pieces,
        [
            ((rows, depth), jnp.float32),
            ((rows, depth), low_type),
            ((rows, depth), low_type),
            ((1, depth), jnp.float32),
        ],
        "attention_output_gradient",
        scratch=[pltpu.VMEM((tiles.members, rows, tiles.depth), jnp.float32)],
    )


def attention_input_gradient(tiles, grad, grad_hidden, tokens, gain, weight, pieces):
    def kernel(at, ins, outs, scratch, wait):
        tiles.multiply_transposed(at, wait, ins[0], scratch[0])
        total = unspread([scratch[0][p] for p in range(tiles.members)], tiles.shards)
        by_tokens, by_gain = norm_gradient(
            ins[2][...].astype(jnp.float32), ins[3][...], total
        )
        outs[0][...] = ins[1][...] + by_tokens
        outs[1][...] = by_gain

    rows, depth = tokens.shape
    return tiles.call(
        kernel,
        [grad, grad_hidden, tokens, gain],
        weight,
        pieces,
        [((rows, depth), jnp.float32), ((1, depth), jnp.float32)],
        "attention_input_gradient",
        scratch=[pltpu.VMEM((tiles.members, rows, tiles.depth), jnp.float32)],
    )


def turn(values):
    half = values.shape[1] // 2
    return jnp.concatenate([values[:, half:], values[:, :half]], axis=1)


def head_of(block, n):
    return block[:, n * HEAD : (n + 1) * HEAD]


def rotated_head(values, gain, cosine, sine):
    normed = values * norm_factor(values) * gain
    return (normed * cosine + turn(normed) * sine).astype(low_type)


def head_gradient(values, gain, cosine, sine, grad):
    return norm_gradient(values, gain, grad * cosine - turn(grad) * sine)


def chunk_of(row_total):
    return min(row_total, 128)


def allowed_scores(rows, columns, start, chunk):
    end = start + chunk
    later = start + lax.broadcasted_iota(jnp.int32, (chunk, end), 0)
    earlier = lax.broadcasted_iota(jnp.int32, (chunk, end), 1)
    return (rows[start:end] == columns[:, :end]) & (later >= earlier)


def head_weights(query, key, allowed):
    scores = product_with_transpose(query, key) * HEAD ** (-0.5)
    return jnp.where(allowed, jnp.exp(scores), 0.0)


def head_specs(row_total):
    pair = 2 * HEADS // KV_HEADS * HEAD
    first_key, first_value = HEADS * HEAD // (2 * HEAD), (HEADS + KV_HEADS) * HEAD // (2 * HEAD)
    blocks = [
        pl.BlockSpec((row_total, pair), lambda i: (0, i)),
        pl.BlockSpec((row_total, 2 * HEAD), lambda i: (0, first_key + i)),
        pl.BlockSpec((row_total, 2 * HEAD), lambda i: (0, first_value + i)),
    ]
    shared = [(1, HEAD), (1, HEAD), (row_total, HEAD), (row_total, HEAD), (row_total, 1), (1, row_total)]
    return pair, blocks, [resident(shape) for shape in shared]


def attend(joint_proj, shared):
    row_total = joint_proj.shape[0]
    ratio, chunk = HEADS // KV_HEADS, chunk_of(joint_proj.shape[0])
    pair, blocks, shared_specs = head_specs(row_total)

    def kernel(query_ref, key_ref, value_ref, query_gain, key_gain, cosine, sine, rows, columns, out, inverse):
        turns = (cosine[...], sine[...])
        heads = [[] for _ in range(2 * ratio)]
        inverses = [[] for _ in range(2 * ratio)]
        for g in range(2):
            key = rotated_head(head_of(key_ref[...], g), key_gain[...], *turns)
            value = head_of(value_ref[...], g).astype(low_type)
            value = jnp.concatenate([value, jnp.ones_like(value)], axis=1)
            queries = [
                rotated_head(head_of(query_ref[...], ratio * g + j), query_gain[...], *turns)
                for j in range(ratio)
            ]
            for start in range(0, row_total, chunk):
                end = start + chunk
                allowed = allowed_scores(rows[...], columns[...], start, chunk)
                for j in range(ratio):
                    weights = head_weights(queries[j][start:end], key[:end], allowed)
                    sums = plain_product(weights.astype(low_type), value[:end])
                    inverted = 1.0 / sums[:, HEAD : HEAD + 1]
                    heads[ratio * g + j].append((sums[:, :HEAD] * inverted).astype(low_type))
                    inverses[ratio * g + j].append(inverted)
        out[...] = jnp.concatenate([jnp.concatenate(head, axis=0) for head in heads], axis=1)
        for n, parts in enumerate(inverses):
            inverse[0, :, n : n + 1] = jnp.concatenate(parts, axis=0)

    steps = KV_HEADS // 2
    return call_kernel(
        kernel,
        [joint_proj] * 3 + list(shared),
        blocks + shared_specs,
        [
            (pl.BlockSpec((row_total, pair), lambda i: (0, i)), ((row_total, HEADS * HEAD), low_type)),
            (
                pl.BlockSpec((1, row_total, 8), lambda i: (i, 0, 0)),
                ((steps, row_total, 8), jnp.float32),
            ),
        ],
        10**10,
        "attend",
        grid=(steps,),
    )


def attend_gradient(joint_proj, attended, inverse, grad, shared):
    row_total = joint_proj.shape[0]
    ratio, chunk = HEADS // KV_HEADS, chunk_of(joint_proj.shape[0])
    pair, blocks, shared_specs = head_specs(row_total)
    query_width, key_width = HEADS * HEAD, KV_HEADS * HEAD
    scale = HEAD ** (-0.5)

    def kernel(
        query_ref,
        key_ref,
        value_ref,
        attended_ref,
        grad_ref,
        inverse_ref,
        query_gain,
        key_gain,
        cosine,
        sine,
        rows,
        columns,
        out,
        gains,
    ):
        step = pl.program_id(0)
        turns = (cosine[...], sine[...])

        @pl.when(step == 0)
        def _():
            gains[...] = jnp.zeros_like(gains)

        by_queries, by_keys, by_values = [], [], []
        for g in range(2):
            key_proj = head_of(key_ref[...], g)
            key = rotated_head(key_proj, key_gain[...], *turns)
            value = head_of(value_ref[...], g).astype(low_type)
            projs = [head_of(query_ref[...], ratio * g + j) for j in range(ratio)]
            queries = [rotated_head(proj, query_gain[...], *turns) for proj in projs]
            grads = [head_of(grad_ref[...], ratio * g + j) for j in range(ratio)]
            inners = [
                jnp.sum(
                    grads[j].astype(jnp.float32)
                    * head_of(attended_ref[...], ratio * g + j).astype(jnp.float32),
                    axis=-1,
                    keepdims=True,
                )
                for j in range(ratio)
            ]
            turned = [[] for _ in range(ratio)]
            by_key = by_value = None
            for start in range(row_total - chunk, -1, -chunk):
                end = start + chunk
                allowed = allowed_scores(rows[...], columns[...], start, chunk)
                all_probs, all_scores = [], []
                for j in range(ratio):
                    weights = head_weights(queries[j][start:end], key[:end], allowed)
                    n = ratio * g + j
                    probs = weights * inverse_ref[0, start:end, n : n + 1]
                    grad_probs = product_with_transpose(grads[j][start:end], value[:end])
                    grad_scores = (probs * (grad_probs - inners[j][start:end])).astype(low_type)
                    all_probs.append(probs.astype(low_type))
                    all_scores.append(grad_scores)
                    turned[j].insert(0, plain_product(grad_scores, key[:end]) * scale)
                stacked = lambda parts: jnp.concatenate([part[start:end] for part in parts], axis=0)
                key_term = (
                    product_over_rows(jnp.concatenate(all_scores, axis=0), stacked(queries)) * scale
                )
                value_term = product_over_rows(jnp.concatenate(all_probs, axis=0), stacked(grads))
                if by_key is None:
                    by_key, by_value = key_term, value_term
                else:
                    by_key = jnp.concatenate([by_key[:end] + key_term, by_key[end:]], axis=0)
                    by_value = jnp.concatenate([by_value[:end] + value_term, by_value[end:]], axis=0)
            for j in range(ratio):
                by_query, by_gain = head_gradient(
                    projs[j], query_gain[...], *turns, jnp.concatenate(turned[j], axis=0)
                )
                by_queries.append(by_query)
                gains[0:1, :] += by_gain
            by_key, by_gain = head_gradient(key_proj, key_gain[...], *turns, by_key)
            by_keys.append(by_key)
            by_values.append(by_value)
            gains[1:2, :] += by_gain
        for first, width, parts in (
            (0, pair, by_queries),
            (query_width, 2 * HEAD, by_keys),
            (query_width + key_width, 2 * HEAD, by_values),
        ):
            start = pl.multiple_of(first + step * width, 128)
            out[:, pl.ds(start, width)] = jnp.concatenate(parts, axis=1).astype(low_type)

    shape = joint_proj.shape
    columns = pl.BlockSpec((row_total, pair), lambda i: (0, i))
    return call_kernel(
        kernel,
        [joint_proj] * 3 + [attended, grad, inverse] + list(shared),
        blocks
        + [columns, columns, pl.BlockSpec((1, row_total, 8), lambda i: (i, 0, 0))]
        + shared_specs,
        [
            (resident(shape), (shape, low_type)),
            (resident((8, HEAD)), ((8, HEAD), jnp.float32)),
        ],
        10**10,
        "attend_gradient",
        grid=(KV_HEADS // 2,),
    )


def token_scratch(chips, rows, depth):
    return [pltpu.VMEM((chips * rows, depth), low_type), pltpu.SemaphoreType.DMA((chips,))]


def token_block(rows, width):
    return pl.BlockSpec((1, rows, width), lambda i: (i, 0, 0))


def load_tokens(chips, rows, refs, target, sems):
    step = pl.program_id(0)

    @pl.when(step == 0)
    def _():
        for copy in piece_copies(piece_rows(chips, rows), refs, target, sems):
            copy.start()

    block = target.at[pl.ds(pl.multiple_of(step * rows, rows), rows)]
    pltpu.make_async_copy(block, block, sems.at[step]).wait()
    return block[...]


def gated_forward(pieces, gate_ws, up_ws):
    chips = lax.axis_size("rep") // 2
    rows, depth = pieces[0].shape
    units = gate_ws[0].shape[1]
    count = len(pieces)

    def kernel(*refs):
        weights, outs, scratch = refs[count : count + 4], refs[count + 4 : -2], refs[-2:]
        x = load_tokens(chips, rows, refs[:count], *scratch)
        outs[0][0] = x
        for n in range(2):
            act, to_gate, to_up = outs[1 + 3 * n : 4 + 3 * n]
            gate = plain_product(x, weights[n][...])
            upward = plain_product(x, weights[2 + n][...])
            sig = 1.0 / (1.0 + jnp.exp(-gate))
            silu = gate * sig
            act[0] = (silu * upward).astype(low_type)
            to_gate[0] = (upward * sig * (1.0 + gate * (1.0 - sig))).astype(low_type)
            to_up[0] = silu.astype(low_type)

    out = (token_block(rows, units), ((chips, rows, units), low_type))
    outs = call_kernel(
        kernel,
        [*pieces, *gate_ws, *up_ws],
        [in_place] * count + [resident((depth, units))] * 4,
        [(token_block(rows, depth), ((chips, rows, depth), low_type))] + [out] * 6,
        8 * chips * rows * depth * units,
        "gated_forward",
        grid=(chips,),
        scratch=token_scratch(chips, rows, depth),
    )
    return outs[0], outs[1:4], outs[4:]


def gated_backward(pieces, to_gate, to_up, down_w, gate_w, up_w, earlier):
    chips, rows, units = to_gate.shape
    depth = pieces[0].shape[1]
    count = len(pieces)
    cuts = piece_rows(chips, rows)

    def kernel(*refs):
        to_gate_ref, to_up_ref, down_ref, gate_ref, up_ref = refs[count : count + 5]
        before = refs[count + 5 : count + 5 + len(earlier)]
        grad_gate, grad_up = refs[count + 5 + len(earlier) : count + 7 + len(earlier)]
        outs, scratch = refs[count + 7 + len(earlier) : -2], refs[-2:]
        grad = load_tokens(chips, rows, refs[:count], *scratch)
        grad_act = product_with_transpose(grad, down_ref[...])
        gate_low = (grad_act * to_gate_ref[0].astype(jnp.float32)).astype(low_type)
        up_low = (grad_act * to_up_ref[0].astype(jnp.float32)).astype(low_type)
        grad_gate[0] = gate_low
        grad_up[0] = up_low
        total = product_with_transpose(gate_low, gate_ref[...]) + product_with_transpose(
            up_low, up_ref[...]
        )
        n = 0
        for i, group in enumerate(cuts):
            start = 0
            for size in group:

                @pl.when(pl.program_id(0) == i)
                def _(n=n, start=start, size=size):
                    part = total[start : start + size]
                    if earlier:
                        part = part + before[n][...].astype(jnp.float32)
                    outs[n][...] = part.astype(low_type)

                start += size
                n += 1

    narrow = token_block(rows, units)
    narrow_out = (narrow, ((chips, rows, units), low_type))
    shapes = [(size, depth) for group in cuts for size in group]
    outs = call_kernel(
        kernel,
        [*pieces, to_gate, to_up, down_w, gate_w, up_w, *earlier],
        [in_place] * count
        + [narrow] * 2
        + [resident(w.shape) for w in (down_w, gate_w, up_w, *earlier)],
        [narrow_out] * 2 + [(resident(shape), (shape, low_type)) for shape in shapes],
        6 * chips * rows * depth * units,
        "gated_backward",
        grid=(chips,),
        scratch=token_scratch(chips, rows, depth),
    )
    return outs[0], outs[1], outs[2:]


def as_groups(pieces, groups, rows):
    cuts = piece_rows(groups, rows)
    result, n = [], 0
    for group in cuts:
        result.append(list(pieces[n : n + len(group)]))
        n += len(group)
    return result


def down_forward(acts, down_ws):
    chips, rows, units = acts[0].shape
    depth = down_ws[0].shape[1]
    cuts = piece_rows(chips, rows)

    def kernel(*refs):
        total = plain_product(refs[0][0], refs[2][...]) + plain_product(refs[1][0], refs[3][...])
        outs, n = refs[4:], 0
        for i, group in enumerate(cuts):
            start = 0
            for size in group:

                @pl.when(pl.program_id(0) == i)
                def _(n=n, start=start, size=size):
                    outs[n][...] = total[start : start + size].astype(low_type)

                start += size
                n += 1

    act = token_block(rows, units)
    shapes = [(size, depth) for group in cuts for size in group]
    return call_kernel(
        kernel,
        [*acts, *down_ws],
        [act, act] + [resident((units, depth))] * 2,
        [(resident(shape), (shape, low_type)) for shape in shapes],
        4 * chips * rows * depth * units,
        "down_forward",
        grid=(chips,),
    )


def weight_gradients(x, grads, steps):
    chips, rows, depth = x.shape
    units = grads[0].shape[2]
    width = depth // steps

    def kernel(x_ref, *refs):
        left = x_ref[...].reshape(chips * rows, width)
        for grad, out in zip(refs[:2], refs[2:], strict=True):
            out[...] = product_over_rows(left, grad[...].reshape(chips * rows, units)).astype(
                low_type
            )

    out = (pl.BlockSpec((width, units), lambda i: (i, 0)), ((depth, units), low_type))
    return call_kernel(
        kernel,
        [x, *grads],
        [pl.BlockSpec((chips, rows, width), lambda i: (0, 0, i))] + [resident(grads[0].shape)] * 2,
        [out] * 2,
        4 * chips * rows * depth * units,
        "weight_gradients",
        grid=(steps,),
    )


def down_gradients(acts, pieces, steps):
    chips, rows, units = acts[0].shape
    depth = pieces[0].shape[1]
    width = depth // steps
    count = len(pieces)

    def kernel(*refs):
        act_refs, outs, (grad, sems) = refs[count : count + 2], refs[count + 2 : -2], refs[-2:]
        step = pl.program_id(0)

        @pl.when(step == 0)
        def _():
            for copy in piece_copies(piece_rows(chips, rows), refs[:count], grad, sems):
                copy.start()
            for i in range(chips):
                block = grad.at[pl.ds(i * rows, rows)]
                pltpu.make_async_copy(block, block, sems.at[i]).wait()

        right = grad[:, pl.ds(pl.multiple_of(step * width, width), width)]
        for act, out in zip(act_refs, outs, strict=True):
            out[...] = product_over_rows(act[...].reshape(chips * rows, units), right).astype(
                low_type
            )

    out = (pl.BlockSpec((units, width), lambda i: (0, i)), ((units, depth), low_type))
    return call_kernel(
        kernel,
        [*pieces, *acts],
        [in_place] * count + [resident(acts[0].shape)] * 2,
        [out] * 2,
        4 * chips * rows * depth * units,
        "down_gradients",
        grid=(steps,),
        scratch=token_scratch(chips, rows, depth),
    )


def plane_place():
    rep = lax.axis_index("rep")
    return jnp.stack([rep // 2, rep % 2]).astype(jnp.int32)


def both_cores(pieces):
    return pieces + [swap(piece, 1) for piece in pieces]


def plane_scratch(chips, rows, width):
    return [
        pltpu.VMEM((2, chips * rows, width), low_type),
        pltpu.SemaphoreType.DMA((2, chips)),
    ]


def load_plane(chips, rows, refs, target, sems):
    half = len(refs) // 2

    @pl.when(pl.program_id(0) == 0)
    def _():
        cuts = piece_rows(chips, rows)
        for core in range(2):
            for copy in piece_copies(
                cuts, refs[core * half : (core + 1) * half], target.at[core], sems.at[core]
            ):
                copy.start()
        for core in range(2):
            for i in range(chips):
                block = target.at[core, pl.ds(i * rows, rows)]
                pltpu.make_async_copy(block, block, sems.at[core, i]).wait()


def whole_columns(pieces, share):
    size, chips = lax.axis_size("shard"), lax.axis_size("rep") // 2
    rows, width = pieces[0].shape
    step_rows = rows // 4

    def kernel(at, *refs):
        out, target, sems = refs[-3:]
        load_plane(chips, rows, refs[:-3], target, sems)
        step = pl.program_id(0)
        for j in range(2 * chips):
            start = (at[0] ^ (j // 2)) * rows + step * step_rows
            own = target[at[1] ^ (j % 2), pl.ds(pl.multiple_of(start, 16), step_rows), :]
            own = own.astype(jnp.float32)
            for z in range(size):
                first = (z * 2 * chips + j) * share
                out[:, first : first + share] = own[:, z * width // size :][:, :share]

    wide = 2 * chips * size * share
    return call_kernel(
        kernel,
        [plane_place(), *pieces],
        [in_place] * len(pieces),
        [(pl.BlockSpec((step_rows, wide), lambda i, at: (i, 0)), ((rows, wide), jnp.float32))],
        10 * 10**9,
        "whole_columns",
        grid=(4,),
        prefetch=1,
        scratch=plane_scratch(chips, rows, width),
    )[0]


def whole_rows(pieces, share):
    chips = lax.axis_size("rep") // 2
    rows, width = pieces[0].shape

    def kernel(at, *refs):
        out, target, sems = refs[-3:]
        load_plane(chips, rows, refs[:-3], target, sems)
        j = pl.program_id(0)
        start = pl.multiple_of((at[0] ^ (j // 2)) * rows, 32)
        own = target[at[1] ^ (j % 2), pl.ds(start, rows), :].astype(jnp.float32)
        out[0] = own[:share]

    shape = (2 * chips, share, width)
    return call_kernel(
        kernel,
        [plane_place(), *pieces],
        [in_place] * len(pieces),
        [(pl.BlockSpec((1, share, width), lambda j, at: (j, 0, 0)), (shape, jnp.float32))],
        10 * 10**9,
        "whole_rows",
        grid=(2 * chips,),
        prefetch=1,
        scratch=plane_scratch(chips, rows, width),
    )[0].reshape(2 * chips * share, width)


def sum_everywhere(values):
    step = 1
    while step < lax.axis_size("rep"):
        values = values + swap(values, step)
        step *= 2
    step = 1
    size = lax.axis_size("shard")
    while step < size:
        values = values + lax.ppermute(values, "shard", [(i, i ^ step) for i in range(size)])
        step *= 2
    return values


def gather_gains(own):
    size, here = lax.axis_size("shard"), lax.axis_index("shard")
    slots = [own] + [from_ahead(own, k) for k in range(1, size)]
    twice = jnp.concatenate(slots + slots)
    return lax.dynamic_slice_in_dim(twice, (size - here) * own.shape[0], size * own.shape[0], 0)


def padded(share):
    return -(-share // 32) * 32


def own_columns(weight):
    size, reps = lax.axis_size("shard"), lax.axis_size("rep")
    run = weight.shape[1] // size
    share = run // reps
    rep = lax.axis_index("rep")
    none = jnp.zeros((weight.shape[0], padded(share) - share), weight.dtype)
    parts = []
    for z in range(size):
        parts += [lax.dynamic_slice_in_dim(weight, z * run + rep * share, share, 1), none]
    return jnp.concatenate(parts, axis=1)


def own_rows(weight):
    share = weight.shape[0] // lax.axis_size("rep")
    own = lax.dynamic_slice_in_dim(weight, lax.axis_index("rep") * share, share, 0)
    return jnp.pad(own, ((0, padded(share) - share), (0, 0)))


def gather_shards(own):
    return lax.all_gather(own, "shard", axis=0, tiled=True)


def with_other(ours, *others):
    return ours, swap(after(ours, *others), 1)


def scatter_group(ours, others):
    total = ours.astype(jnp.float32) + swap(others, 1).astype(jnp.float32)
    return lax.psum_scatter(total.astype(low_type), "shard", scatter_dimension=0, tiled=True)


def local(
    tokens,
    norm_gains,
    w_query,
    w_key,
    w_value,
    w_out,
    w_gate,
    w_up,
    w_down,
    seq_lengths,
    seq_device,
    cotangent,
):
    row_total = tokens.shape[0]
    size, reps = lax.axis_size("shard"), lax.axis_size("rep")
    chips = reps // 2
    rep = lax.axis_index("rep")
    device = rep * size + lax.axis_index("shard")
    query_width, key_width = HEADS * HEAD, KV_HEADS * HEAD

    w_joint = jnp.concatenate([w_query, w_key, w_value], axis=1)
    joint, outer = Tiles(w_joint), Tiles(w_out)
    joint_slots = [from_ahead(joint.own(w_joint), k) for k in range(1, size)]
    gains = gather_gains(norm_gains)
    out_tile = outer.own(w_out)
    out_slots = [from_ahead(out_tile, k) for k in range(1, size)]
    owns = own_columns(w_gate), own_columns(w_up), own_rows(w_down)
    owns = [after(own, joint_slots, out_slots, gains) for own in owns]
    gate_w, up_w, down_w = (gather_shards(own) for own in owns)
    joint_tiles = after(jnp.concatenate(joint_slots, axis=0), gains)
    joint_near = near_groups(joint_tiles, joint.members)
    joint_far = far_group(joint_near, joint.members)
    joint_pieces = joint.across([joint_tiles] + joint_near + joint_far)
    out_tiles = after(jnp.concatenate(out_slots, axis=0), joint_near, joint_far)
    out_near = near_groups(out_tiles, outer.members)

    live, segment, position = layout(seq_lengths, seq_device, device, row_total)
    cosine, sine = rotary_tables(position, HEAD)
    cotangent_live = jnp.where(live[:, None], cotangent, jnp.zeros_like(cotangent))

    gains = gains.astype(jnp.float32)[None]
    gain_in = gains[:, :D]
    gain_ff = gains[:, D + 2 * HEAD :]
    shared = (
        gains[:, D : D + HEAD],
        gains[:, D + HEAD : D + 2 * HEAD],
        jnp.concatenate([cosine, cosine], axis=1),
        jnp.concatenate([0.0 - sine, sine], axis=1),
        segment[:, None],
        segment[None, :],
    )
    joint_proj, normed_in = attention_input(joint, tokens, gain_in, w_joint, joint_pieces)
    normed_runs = joint.member_rows(normed_in)
    joint_proj, out_near, normed_runs = lax.optimization_barrier((joint_proj, out_near, normed_runs))
    out_far = far_group(out_near, outer.members)
    out_pieces = outer.across([out_tiles] + out_near + out_far)
    normed_run = jnp.concatenate(normed_runs, axis=0)
    normed_near = near_groups(normed_run, joint.members)
    attended, inverse = attend(joint_proj, shared)
    hidden, normed_ff, attended_parts = attention_output(
        outer, attended, tokens, gain_ff, w_out, out_pieces
    )
    normed_ff, normed_near = lax.optimization_barrier((normed_ff, normed_near))
    ff_near = near_groups(normed_ff, 2)
    gate_ws, up_ws = with_other(gate_w, ff_near), with_other(up_w, ff_near)
    ff_far = far_group(ff_near, 2)
    ff_near, ff_far, cotangent_live = lax.optimization_barrier((ff_near, ff_far, cotangent_live))
    grad_near = near_groups(cotangent_live, 2)
    normed_far = far_group(after(normed_near, ff_far), joint.members)
    attended_runs = outer.member_rows(after(attended_parts, ff_far))
    group_tokens, first, second = gated_forward([normed_ff] + ff_near + ff_far, gate_ws, up_ws)
    grad_near, group_tokens, normed_far, attended_runs = lax.optimization_barrier(
        (grad_near, group_tokens, normed_far, attended_runs)
    )
    normed_rows = [normed_run] + normed_near + normed_far
    down_ws = with_other(down_w, grad_near)
    grad_far = far_group(grad_near, 2)
    grad_mixed = [cotangent_live] + grad_near + grad_far
    attended_run = jnp.concatenate(attended_runs, axis=0)
    attended_near = near_groups(after(attended_run, grad_far), outer.members)
    grad_downs = down_gradients((first[0], second[0]), grad_mixed, 2)
    grad_down = scatter_group(*grad_downs)
    grad_gate_first, grad_up_first, grad_x = gated_backward(
        after(grad_mixed, grad_downs),
        first[1],
        first[2],
        down_ws[0],
        gate_ws[0],
        up_ws[0],
        [],
    )
    grad_x, attended_near = lax.optimization_barrier((grad_x, attended_near))
    attended_far = far_group(attended_near, outer.members)
    grad_gate_second, grad_up_second, grad_x = gated_backward(
        grad_mixed,
        second[1],
        second[2],
        down_ws[1],
        gate_ws[1],
        up_ws[1],
        grad_x,
    )
    grad_x, attended_far = lax.optimization_barrier((grad_x, attended_far))
    attended_rows = [attended_run] + attended_near + attended_far
    grad_x = as_groups(grad_x, chips, row_total)
    grad_x_far = far_terms(grad_x, 2)
    grad_gates = weight_gradients(group_tokens, (grad_gate_first, grad_gate_second), 4)
    grad_gate = scatter_group(*grad_gates)
    grad_x_far, grad_gates = lax.optimization_barrier((grad_x_far, grad_gates))
    grad_terms = near_terms(grad_x, grad_x_far, 2)
    grad_ups = weight_gradients(after(group_tokens, grad_x_far), (grad_up_first, grad_up_second), 4)
    grad_up = scatter_group(*grad_ups)
    down_parts = down_forward(after((first[0], second[0]), grad_x_far), down_ws)
    grad_terms, down_parts, grad_ups = lax.optimization_barrier((grad_terms, down_parts, grad_ups))
    down_parts = as_groups(down_parts, chips, row_total)
    down_far = far_terms(down_parts, 2)

    grad_hidden, grad_hidden_low, grad_attended, grad_gain_ff = attention_output_gradient(
        outer, grad_terms, cotangent_live, hidden, gain_ff, w_out, out_pieces
    )
    down_far, grad_hidden_low, grad_attended = lax.optimization_barrier(
        (down_far, grad_hidden_low, grad_attended)
    )
    down_terms = near_terms(down_parts, down_far, 2)
    out_runs = outer.group_columns(grad_hidden_low)
    grad_joint_low, grad_head_gains = attend_gradient(
        joint_proj, attended, inverse, grad_attended, shared
    )
    grad_joint_low, down_terms, out_runs = lax.optimization_barrier(
        (grad_joint_low, down_terms, out_runs)
    )
    mixed_full = hidden
    for term in down_terms:
        mixed_full = mixed_full + term.astype(jnp.float32)
    mixed = jnp.where(live[:, None], mixed_full, jnp.zeros_like(mixed_full)).astype(jnp.bfloat16)
    joint_runs = joint.group_columns(grad_joint_low)
    out_own, out_sent = outer.tile(attended_rows, outer.all_columns(out_runs))
    grad_tokens, grad_gain_in = attention_input_gradient(
        joint, grad_joint_low, grad_hidden, tokens, gain_in, w_joint, joint_pieces
    )
    joint_runs, out_sent, grad_gain_in, grad_down, grad_gate, grad_up = lax.optimization_barrier(
        (joint_runs, out_sent, grad_gain_in, grad_down, grad_gate, grad_up)
    )
    joint_own, joint_sent = joint.tile(normed_rows, joint.all_columns(joint_runs))
    grad_joint = joint.whole(joint_own, joint_sent)
    grad_out_w = outer.whole(out_own, out_sent)
    down_near = near_groups(grad_down, 2)
    down_pieces = both_cores([grad_down] + down_near + far_group(down_near, 2))
    gate_near = near_groups(after(grad_gate, down_near), 2)
    gate_pieces = both_cores([grad_gate] + gate_near + far_group(gate_near, 2))
    up_near = near_groups(after(grad_up, gate_near), 2)
    up_pieces = both_cores([grad_up] + up_near + far_group(up_near, 2))
    grad_gains = sum_everywhere(
        jnp.concatenate(
            [grad_gain_in, grad_head_gains[0:1], grad_head_gains[1:2], grad_gain_ff], axis=1
        )[0]
    )
    own_gains = norm_gains.shape[0]
    grad_gains = lax.dynamic_slice_in_dim(
        grad_gains, lax.axis_index("shard") * own_gains, own_gains, 0
    )
    share = w_down.shape[0] // reps
    return (
        mixed,
        grad_tokens,
        grad_gains,
        grad_joint[:, :query_width],
        grad_joint[:, query_width : query_width + key_width],
        grad_joint[:, query_width + key_width :],
        grad_out_w,
        whole_columns(gate_pieces, share),
        whole_columns(up_pieces, share),
        whole_rows(down_pieces, share),
    )


def solution(mesh):
    return jax.shard_map(
        local,
        mesh=mesh,
        in_specs=(
            P(("rep", "shard"), None),
            P("shard"),
            P("shard", None),
            P("shard", None),
            P("shard", None),
            P("shard", None),
            P("shard", None),
            P("shard", None),
            P("shard", None),
            P(),
            P(),
            P(("rep", "shard"), None),
        ),
        out_specs=(
            P(("rep", "shard"), None),
            P(("rep", "shard"), None),
            P("shard"),
            P("shard", None),
            P("shard", None),
            P("shard", None),
            P("shard", None),
            P("shard", None),
            P("shard", None),
            P("shard", None),
        ),
        check_vma=False,
    )
```

```python
import math

import jax
import jax.numpy as jnp
from jax import lax
from jax.experimental import pallas as pl
from jax.experimental.pallas import tpu as pltpu
from jax.sharding import PartitionSpec as P

D = 1536
HEADS = 24
KV_HEADS = 8
HEAD = 64
FF = 6912


epsilon = 1e-05
rope_base = 1000000.0
masked_score = -1e30


def plain_product(left, right):
    return jnp.dot(left, right, preferred_element_type=jnp.float32)


def product_over_rows(left, right):
    return lax.dot_general(
        left, right, (((0,), (0,)), ((), ())), preferred_element_type=jnp.float32
    )


def product_with_transpose(left, right):
    return lax.dot_general(
        left, right, (((1,), (1,)), ((), ())), preferred_element_type=jnp.float32
    )


def rotary_tables(position, head_width):
    half_width = head_width // 2
    index = jnp.arange(half_width).astype(jnp.float32)
    inverse = jnp.exp(index * (-2.0 * math.log(rope_base) / head_width))
    angle = position.astype(jnp.float32)[:, None] * inverse[None, :]
    return (jnp.cos(angle), jnp.sin(angle))


def layout(seq_lengths, seq_device, device, row_total):
    own_length = jnp.where(seq_device == device, seq_lengths, 0)
    ends = jnp.cumsum(own_length, dtype=jnp.int32)
    begins = ends - own_length
    slot_index = jnp.arange(row_total, dtype=jnp.int32)
    inside = (slot_index[:, None] >= begins[None, :]) & (slot_index[:, None] < ends[None, :])
    live = jnp.any(inside, axis=1)
    seq_total = seq_lengths.shape[0]
    numbers = jnp.arange(seq_total, dtype=jnp.int32)
    found = jnp.sum(jnp.where(inside, numbers[None, :], 0), axis=1, dtype=jnp.int32)
    segment = jnp.where(live, found, seq_total + slot_index)
    offset = jnp.sum(jnp.where(inside, (0 - begins)[None, :], 0), axis=1, dtype=jnp.int32)
    position = jnp.where(live, slot_index + offset, 0)
    return (live, segment, position)


vmem_bytes = 60 * 2**20
low_type = jnp.bfloat16
in_place = pl.BlockSpec(memory_space=pl.ANY)


def swap(values, offset):
    size = lax.axis_size("rep")
    return lax.ppermute(values, "rep", [(i, i ^ offset) for i in range(size)])


def from_ahead(values, steps):
    size = lax.axis_size("shard")
    return lax.ppermute(values, "shard", [((i + steps) % size, i) for i in range(size)])


def from_behind(values, steps):
    size = lax.axis_size("shard")
    return lax.ppermute(values, "shard", [(i, (i + steps) % size) for i in range(size)])


def fence(*values):
    return lax.optimization_barrier(values)


def after(values, *others):
    return lax.optimization_barrier((values, others))[0]


def all_groups(block, unit):
    return [block] + [swap(block, unit * d) for d in range(1, lax.axis_size("rep") // unit)]


def sum_terms(blocks, unit):
    return [swap(block, unit * d) if d else block for d, block in enumerate(blocks)]


def near_groups(block, unit):
    groups = lax.axis_size("rep") // unit
    return [swap(block, unit * d) for d in range(1, groups if groups != 4 else 3)]


def far_group(near, unit):
    if lax.axis_size("rep") // unit != 4:
        return []
    half = half_rows(near[0].shape[0])
    return [swap(near[1][:half], unit), swap(near[0][half:], 2 * unit)]


def half_rows(rows):
    return rows // 2 // 16 * 16


def piece_rows(groups, rows, count):
    half = half_rows(rows)
    return [[rows]] * groups if count == groups else [[rows]] * 3 + [[half, rows - half]]


def piece_copies(rows, refs, target, sems):
    copies, at, n = [], 0, 0
    for i, group in enumerate(rows):
        for count in group:
            copies.append(
                pltpu.make_async_copy(refs[n], target.at[pl.ds(at, count)], sems.at[i])
            )
            at += count
            n += 1
    return copies


def call_kernel(kernel, args, ins, outs, micros, name, grid=None, prefetch=0, scratch=()):
    return pl.pallas_call(
        kernel,
        grid_spec=pltpu.PrefetchScalarGridSpec(
            num_scalar_prefetch=prefetch,
            grid=grid or (1,),
            in_specs=ins,
            out_specs=[spec for spec, _ in outs],
            scratch_shapes=list(scratch),
        ),
        out_shape=[jax.ShapeDtypeStruct(*shape) for _, shape in outs],
        compiler_params=pltpu.CompilerParams(vmem_limit_bytes=vmem_bytes),
        cost_estimate=pl.CostEstimate(flops=int(micros * 1.15e9), bytes_accessed=0, transcendentals=0),
        name=name,
    )(*args)


def resident(shape):
    return pl.BlockSpec(shape, lambda *_: (0,) * len(shape), pipeline_mode=pl.Buffered(1))


def spread(values, shards, members):
    part = values.shape[1] // shards // members
    return [
        jnp.concatenate(
            [values[:, (z * members + p) * part :][:, :part] for z in range(shards)], axis=1
        )
        for p in range(members)
    ]


def unspread(parts, shards):
    part = parts[0].shape[1] // shards
    return jnp.concatenate(
        [run[:, z * part : (z + 1) * part] for z in range(shards) for run in parts], axis=1
    )


def norm_factor(values):
    return lax.rsqrt(jnp.mean(values * values, axis=-1, keepdims=True) + epsilon)


def norm_gradient(values, gain, grad):
    factor = norm_factor(values)
    scaled = grad * gain
    mean = jnp.mean(scaled * values, axis=-1, keepdims=True)
    by_gain = jnp.sum(grad * values * factor, axis=0, keepdims=True)
    return factor * scaled - values * (factor * factor * factor * mean), by_gain


def stacked(pieces):
    rows = sum(piece.shape[0] for piece in pieces)

    def kernel(*refs):
        copies, start = [], 0
        for n, piece in enumerate(pieces):
            target = refs[len(pieces)].at[pl.ds(start, piece.shape[0])]
            copies.append(pltpu.make_async_copy(refs[n], target, refs[-1].at[n]))
            start += piece.shape[0]
        for copy in copies:
            copy.start()
        for copy in copies:
            copy.wait()

    shape = (rows, pieces[0].shape[1])
    return call_kernel(
        kernel,
        pieces,
        [in_place] * len(pieces),
        [(resident(shape), (shape, low_type))],
        0,
        "stacked",
        scratch=[pltpu.SemaphoreType.DMA((len(pieces),))],
    )[0]


class Tiles:
    def __init__(self, weight):
        reps = lax.axis_size("rep")
        groups = reps // 2
        while weight.shape[1] % (128 * groups):
            groups //= 2
        self.groups, self.members = groups, reps // groups
        self.shards, self.here = lax.axis_size("shard"), lax.axis_index("shard")
        self.group = lax.axis_index("rep") // self.members
        self.member = lax.axis_index("rep") % self.members
        self.rows = weight.shape[0]
        self.part = self.rows // self.members
        self.rest = (self.shards - 1) * self.part
        self.depth = self.shards * self.part
        self.width = weight.shape[1] // groups

    def own(self, weight):
        return lax.dynamic_slice(
            weight, (self.member * self.part, self.group * self.width), (self.part, self.width)
        )

    def across(self, pieces):
        return pieces + [swap(piece, h) for h in range(1, self.members) for piece in pieces]

    def across_stacked(self, pieces):
        stack = stacked(pieces)
        return pieces + [swap(stack, h) for h in range(1, self.members)]

    def place(self):
        return jnp.stack([self.group, self.member, self.here]).astype(jnp.int32)

    def scratch(self):
        shape = (self.members, self.groups)
        return [
            pltpu.VMEM(shape + (self.depth, self.width), low_type),
            pltpu.SemaphoreType.DMA(shape),
        ]

    def load(self, at, weight_ref, refs, tiles, sems):
        part, shards, groups = self.part, self.shards, self.groups

        def to(h, d, z, start, size):
            first = pl.multiple_of(lax.rem(at[2] + z, shards) * part, 16) + start
            return tiles.at[h, d, pl.ds(pl.multiple_of(first, 16), size)]

        for d in range(groups):
            for h in range(self.members):
                source = weight_ref.at[
                    pl.ds(pl.multiple_of((at[1] ^ h) * part, 16), part),
                    pl.ds(pl.multiple_of((at[0] ^ d) * self.width, 128), self.width),
                ]
                pltpu.make_async_copy(source, to(h, d, 0, 0, part), sems.at[h, d]).start()
                for k in range(shards - 1):
                    pltpu.make_async_copy(
                        refs[h * groups + d].at[pl.ds(k * part, part)],
                        to(h, d, k + 1, 0, part),
                        sems.at[h, d],
                    ).start()

        def wait(h, d):
            pltpu.make_async_copy(tiles.at[h, d], tiles.at[h, d], sems.at[h, d]).wait()
            return tiles[h, d]

        return wait

    def columns(self, at, d):
        return pl.ds(pl.multiple_of((at[0] ^ d) * self.width, 128), self.width)

    def multiply(self, at, wait, x, out):
        for d in range(self.groups):
            total = None
            for h in range(self.members):
                term = plain_product(x[at[1] ^ h], wait(h, d))
                total = term if total is None else total + term
            out[:, self.columns(at, d)] = total

    def multiply_transposed(self, at, wait, grad, out):
        totals = [None] * self.members
        for d in range(self.groups):
            block = grad[:, self.columns(at, d)]
            for h in range(self.members):
                term = product_with_transpose(block, wait(h, d))
                totals[h] = term if totals[h] is None else totals[h] + term
        for h in range(self.members):
            out[at[1] ^ h] = totals[h]

    def call(self, kernel, args, weight, pieces, outs, micros, name, scratch=()):
        given, produced = len(args), len(outs)

        def whole_kernel(at, *refs):
            ins, weight_ref = refs[:given], refs[given]
            rest = refs[given + 1 + len(pieces) :]
            wait = self.load(
                at, weight_ref, refs[given + 1 : given + 1 + len(pieces)], *rest[produced : produced + 2]
            )
            kernel(at, ins, rest[:produced], rest[produced + 2 :], wait)

        return call_kernel(
            whole_kernel,
            [self.place(), *args, weight, *pieces],
            [resident(arg.shape) for arg in args] + [in_place] * (1 + len(pieces)),
            [(resident(shape), (shape, kind)) for shape, kind in outs],
            micros,
            name,
            prefetch=1,
            scratch=self.scratch() + list(scratch),
        )

    def cut_columns(self, grad):
        return [
            lax.dynamic_slice_in_dim(grad, (self.group ^ d) * self.width, self.width, 1)
            for d in range(self.groups)
        ]

    def group_columns(self, cuts):
        return [swap(cut, self.members * d) if d else cut for d, cut in enumerate(cuts)]

    def tile(self, rows, columns, beside=()):
        tokens, members, shards, part = columns[0].shape[0], self.members, self.shards, self.part
        count, total = len(rows), len(columns) * tokens
        sizes = [piece.shape[0] for piece in rows]
        wide = self.width + (beside[0].shape[1] if beside else 0)

        def kernel(at, *refs):
            besides = refs[count + len(columns) : count + len(columns) + len(beside)]
            outs = refs[count + len(columns) + len(beside) : -4]
            left, right, whole, sems = refs[-4:]
            copies = piece_copies([sizes], refs[:count], left, sems.at[pl.ds(0, 1)])
            copies += piece_copies(
                [[tokens] * len(columns)], refs[count : count + len(columns)], right, sems.at[pl.ds(1, 1)]
            )
            for copy in copies:
                copy.start()
            pltpu.make_async_copy(left, left, sems.at[0]).wait()
            pltpu.make_async_copy(right, right, sems.at[1]).wait()
            whole[...] = product_over_rows(left[...], right[...])
            for h in range(members):
                for k in range(shards):
                    start = lax.rem(at[2] + k, shards) * self.rows + (at[1] ^ h) * part
                    block = whole[pl.ds(pl.multiple_of(start, 16), part), :]
                    outs[h][k * part : (k + 1) * part, : self.width] = block.astype(outs[h].dtype)
                if beside:
                    outs[h][:, self.width :] = besides[h][...]

        shape = (shards * part, wide)
        return call_kernel(
            kernel,
            [self.place(), *rows, *columns, *beside],
            [in_place] * (count + len(columns)) + [resident(part.shape) for part in beside],
            [(resident(shape), (shape, low_type if h else jnp.float32)) for h in range(members)],
            7,
            "weight_tile",
            prefetch=1,
            scratch=[
                pltpu.VMEM((total, members * self.depth), low_type),
                pltpu.VMEM((total, self.width), low_type),
                pltpu.VMEM((members * self.depth, self.width), jnp.float32),
                pltpu.SemaphoreType.DMA((2,)),
            ],
        )

    def send(self, tiles, extra):
        total = tiles[0]
        for tile in tiles[1:]:
            total = total + tile.astype(jnp.float32)
        parts = [
            jnp.concatenate([total[k * self.part : (k + 1) * self.part], extra[k]], axis=0)
            for k in range(self.shards)
        ]
        return parts[0], [
            from_behind(parts[k].astype(low_type), k) for k in range(1, self.shards)
        ]

    def extra_rows(self, values, width):
        runs = values.reshape(self.shards, -1)
        block = jnp.stack([rows_of(runs[z], width) for z in range(self.shards)])
        twice = jnp.concatenate([block, block], axis=0)
        return lax.dynamic_slice_in_dim(twice, self.here, self.shards, 0)

    def whole(self, pieces, sections):
        members, groups, part = self.members, self.groups, self.part
        rows, wide = pieces[0].shape
        beneath = rows - part

        def kernel(at, *refs):
            outs, (tiles, sems) = refs[len(pieces) : -2], refs[-2:]
            for h in range(members):
                for d in range(groups):
                    ref = refs[groups + h - 1].at[pl.ds(d * rows, rows)] if h else refs[d]
                    pltpu.make_async_copy(ref, tiles.at[h, d], sems.at[h, d]).start()
            for h in range(members):
                for d in range(groups):
                    pltpu.make_async_copy(tiles.at[h, d], tiles.at[h, d], sems.at[h, d]).wait()
            total = None
            for g in range(groups):
                for p in range(members):
                    block = tiles[at[1] ^ p, at[0] ^ g].astype(jnp.float32)
                    total = block[part:] if total is None else total + block[part:]
                    n, left = 0, 0
                    for widths in sections:
                        width = sum(widths) // groups
                        first = 0
                        for run in widths:
                            low, high = max(first, g * width), min(first + run, (g + 1) * width)
                            if low < high:
                                outs[n][p * part : (p + 1) * part, low - first : high - first] = (
                                    block[:part, left + low - g * width : left + high - g * width]
                                )
                            first += run
                            n += 1
                        left += width
            outs[-1][...] = total

        shapes = [(self.rows, run) for widths in sections for run in widths] + [(beneath, wide)]
        return call_kernel(
            kernel,
            [self.place(), *pieces],
            [in_place] * len(pieces),
            [(resident(shape), (shape, jnp.float32)) for shape in shapes],
            6,
            "whole_tiles",
            prefetch=1,
            scratch=[
                pltpu.VMEM((members, groups, rows, wide), low_type),
                pltpu.SemaphoreType.DMA((members, groups)),
            ],
        )


def attention_input(tiles, tokens, gain, weight, pieces):
    def kernel(at, ins, outs, scratch, wait):
        x = ins[0][...].astype(jnp.float32)
        normed = (x * norm_factor(x) * ins[1][...]).astype(low_type)
        outs[1][...] = normed
        for p, run in enumerate(spread(normed, tiles.shards, tiles.members)):
            scratch[0][p] = run
        tiles.multiply(at, wait, scratch[0], outs[0])

    rows = tokens.shape[0]
    return tiles.call(
        kernel,
        [tokens, gain],
        weight,
        pieces,
        [
            ((rows, weight.shape[1]), jnp.float32),
            (tokens.shape, low_type),
        ],
        0,
        "attention_input",
        scratch=[pltpu.VMEM((tiles.members, rows, tiles.depth), low_type)],
    )


def attention_output(tiles, attended, tokens, gain, weight, pieces):
    def kernel(at, ins, outs, scratch, wait):
        for p, run in enumerate(spread(ins[0][...], tiles.shards, tiles.members)):
            scratch[0][p] = run
        tiles.multiply(at, wait, scratch[0], outs[0])
        hidden = outs[0][...] + ins[1][...].astype(jnp.float32)
        outs[0][...] = hidden
        outs[1][...] = (hidden * norm_factor(hidden) * ins[2][...]).astype(low_type)

    rows, depth = tokens.shape
    return tiles.call(
        kernel,
        [attended, tokens, gain],
        weight,
        pieces,
        [
            ((rows, depth), jnp.float32),
            ((rows, depth), low_type),
        ],
        0,
        "attention_output",
        scratch=[pltpu.VMEM((tiles.members, rows, tiles.depth), low_type)],
    )


def attention_output_gradient(tiles, terms, grad, hidden, gain, weight, pieces):
    count = len(terms)

    def kernel(at, ins, outs, scratch, wait):
        total = ins[0][...].astype(jnp.float32)
        for term in ins[1:count]:
            total = total + term[...].astype(jnp.float32)
        by_hidden, by_gain = norm_gradient(ins[count + 1][...], ins[count + 2][...], total)
        by_hidden = by_hidden + ins[count][...].astype(jnp.float32)
        outs[0][...] = by_hidden
        low = scratch[1]
        low[...] = by_hidden.astype(low_type)
        outs[3][...] = by_gain
        for d in range(tiles.groups):
            outs[1][d] = low[:, tiles.columns(at, d)]
        tiles.multiply_transposed(at, wait, low, scratch[0])
        runs = [scratch[0][p].astype(low_type) for p in range(tiles.members)]
        outs[2][...] = unspread(runs, tiles.shards)

    rows, depth = grad.shape
    return tiles.call(
        kernel,
        [*terms, grad, hidden, gain],
        weight,
        pieces,
        [
            ((rows, depth), jnp.float32),
            ((tiles.groups, rows, tiles.width), low_type),
            ((rows, depth), low_type),
            ((1, depth), jnp.float32),
        ],
        9,
        "attention_output_gradient",
        scratch=[
            pltpu.VMEM((tiles.members, rows, tiles.depth), jnp.float32),
            pltpu.VMEM((rows, depth), low_type),
        ],
    )


def attention_input_gradient(tiles, grad, grad_hidden, tokens, gain, weight, pieces):
    def kernel(at, ins, outs, scratch, wait):
        tiles.multiply_transposed(at, wait, ins[0], scratch[0])
        total = unspread([scratch[0][p] for p in range(tiles.members)], tiles.shards)
        by_tokens, by_gain = norm_gradient(
            ins[2][...].astype(jnp.float32), ins[3][...], total
        )
        outs[0][...] = ins[1][...] + by_tokens
        outs[1][...] = by_gain

    rows, depth = tokens.shape
    return tiles.call(
        kernel,
        [grad, grad_hidden, tokens, gain],
        weight,
        pieces,
        [((rows, depth), jnp.float32), ((1, depth), jnp.float32)],
        10,
        "attention_input_gradient",
        scratch=[pltpu.VMEM((tiles.members, rows, tiles.depth), jnp.float32)],
    )


def turn(values):
    half = values.shape[1] // 2
    return jnp.concatenate([values[:, half:], values[:, :half]], axis=1)


def head_of(block, n):
    return block[:, n * HEAD : (n + 1) * HEAD]


def rotated_head(values, gain, cosine, sine):
    normed = values * norm_factor(values) * gain
    return (normed * cosine + turn(normed) * sine).astype(low_type)


def head_gradient(values, gain, cosine, sine, grad):
    return norm_gradient(values, gain, grad * cosine - turn(grad) * sine)


def chunk_of(row_total):
    return min(row_total, 128)


def allowed_scores(rows, columns, start, chunk):
    end = start + chunk
    later = start + lax.broadcasted_iota(jnp.int32, (chunk, end), 0)
    earlier = lax.broadcasted_iota(jnp.int32, (chunk, end), 1)
    return (rows[start:end] == columns[:, :end]) & (later >= earlier)


def head_weights(query, key, allowed):
    scores = product_with_transpose(query, key) * HEAD ** (-0.5)
    return jnp.where(allowed, jnp.exp(scores), 0.0)


def head_specs(row_total, first_step=0):
    pair = 2 * HEADS // KV_HEADS * HEAD
    first_key, first_value = HEADS * HEAD // (2 * HEAD), (HEADS + KV_HEADS) * HEAD // (2 * HEAD)
    blocks = [
        pl.BlockSpec((row_total, pair), lambda i: (0, first_step + i)),
        pl.BlockSpec((row_total, 2 * HEAD), lambda i: (0, first_key + first_step + i)),
        pl.BlockSpec((row_total, 2 * HEAD), lambda i: (0, first_value + first_step + i)),
    ]
    shared = [(1, HEAD), (1, HEAD), (row_total, HEAD), (row_total, HEAD), (row_total, 1), (1, row_total)]
    return pair, blocks, [resident(shape) for shape in shared]


def attend(joint_proj, shared, first_step, steps):
    row_total = joint_proj.shape[0]
    ratio, chunk = HEADS // KV_HEADS, chunk_of(joint_proj.shape[0])
    pair, blocks, shared_specs = head_specs(row_total, first_step)

    def kernel(query_ref, key_ref, value_ref, query_gain, key_gain, cosine, sine, rows, columns, out, inverse):
        turns = (cosine[...], sine[...])
        heads = [[] for _ in range(2 * ratio)]
        inverses = [[] for _ in range(2 * ratio)]
        for g in range(2):
            key = rotated_head(head_of(key_ref[...], g), key_gain[...], *turns)
            value = head_of(value_ref[...], g).astype(low_type)
            value = jnp.concatenate([value, jnp.ones_like(value)], axis=1)
            queries = [
                rotated_head(head_of(query_ref[...], ratio * g + j), query_gain[...], *turns)
                for j in range(ratio)
            ]
            for start in range(0, row_total, chunk):
                end = start + chunk
                allowed = allowed_scores(rows[...], columns[...], start, chunk)
                for j in range(ratio):
                    weights = head_weights(queries[j][start:end], key[:end], allowed)
                    sums = plain_product(weights.astype(low_type), value[:end])
                    inverted = 1.0 / sums[:, HEAD : HEAD + 1]
                    heads[ratio * g + j].append((sums[:, :HEAD] * inverted).astype(low_type))
                    inverses[ratio * g + j].append(inverted)
        out[...] = jnp.concatenate([jnp.concatenate(head, axis=0) for head in heads], axis=1)
        for n, parts in enumerate(inverses):
            inverse[0, :, n : n + 1] = jnp.concatenate(parts, axis=0)

    return call_kernel(
        kernel,
        [joint_proj] * 3 + list(shared),
        blocks + shared_specs,
        [
            (pl.BlockSpec((row_total, pair), lambda i: (0, i)), ((row_total, steps * pair), low_type)),
            (
                pl.BlockSpec((1, row_total, 8), lambda i: (i, 0, 0)),
                ((steps, row_total, 8), jnp.float32),
            ),
        ],
        0,
        "attend",
        grid=(steps,),
    )


def attend_gradient(joint_proj, attended, inverse, grad, shared, first_step, steps):
    row_total = joint_proj.shape[0]
    ratio, chunk = HEADS // KV_HEADS, chunk_of(joint_proj.shape[0])
    pair, blocks, shared_specs = head_specs(row_total, first_step)
    scale = HEAD ** (-0.5)

    def kernel(
        query_ref,
        key_ref,
        value_ref,
        attended_ref,
        grad_ref,
        inverse_ref,
        query_gain,
        key_gain,
        cosine,
        sine,
        rows,
        columns,
        out_query,
        out_key,
        out_value,
        gains,
    ):
        step = pl.program_id(0)
        turns = (cosine[...], sine[...])

        @pl.when(step == 0)
        def _():
            gains[...] = jnp.zeros_like(gains)

        by_queries, by_keys, by_values = [], [], []
        for g in range(2):
            key_proj = head_of(key_ref[...], g)
            key = rotated_head(key_proj, key_gain[...], *turns)
            value = head_of(value_ref[...], g).astype(low_type)
            projs = [head_of(query_ref[...], ratio * g + j) for j in range(ratio)]
            queries = [rotated_head(proj, query_gain[...], *turns) for proj in projs]
            grads = [head_of(grad_ref[...], ratio * g + j) for j in range(ratio)]
            inners = [
                jnp.sum(
                    grads[j].astype(jnp.float32)
                    * head_of(attended_ref[...], ratio * g + j).astype(jnp.float32),
                    axis=-1,
                    keepdims=True,
                )
                for j in range(ratio)
            ]
            turned = [[] for _ in range(ratio)]
            by_key = by_value = None
            for start in range(row_total - chunk, -1, -chunk):
                end = start + chunk
                allowed = allowed_scores(rows[...], columns[...], start, chunk)
                all_probs, all_scores = [], []
                for j in range(ratio):
                    weights = head_weights(queries[j][start:end], key[:end], allowed)
                    n = ratio * g + j
                    probs = weights * inverse_ref[0, start:end, n : n + 1]
                    grad_probs = product_with_transpose(grads[j][start:end], value[:end])
                    grad_scores = (probs * (grad_probs - inners[j][start:end])).astype(low_type)
                    all_probs.append(probs.astype(low_type))
                    all_scores.append(grad_scores)
                    turned[j].insert(0, plain_product(grad_scores, key[:end]) * scale)
                stacked = lambda parts: jnp.concatenate([part[start:end] for part in parts], axis=0)
                key_term = (
                    product_over_rows(jnp.concatenate(all_scores, axis=0), stacked(queries)) * scale
                )
                value_term = product_over_rows(jnp.concatenate(all_probs, axis=0), stacked(grads))
                if by_key is None:
                    by_key, by_value = key_term, value_term
                else:
                    by_key = jnp.concatenate([by_key[:end] + key_term, by_key[end:]], axis=0)
                    by_value = jnp.concatenate([by_value[:end] + value_term, by_value[end:]], axis=0)
            for j in range(ratio):
                by_query, by_gain = head_gradient(
                    projs[j], query_gain[...], *turns, jnp.concatenate(turned[j], axis=0)
                )
                by_queries.append(by_query)
                gains[0:1, :] += by_gain
            by_key, by_gain = head_gradient(key_proj, key_gain[...], *turns, by_key)
            by_keys.append(by_key)
            by_values.append(by_value)
            gains[1:2, :] += by_gain
        for out, parts in ((out_query, by_queries), (out_key, by_keys), (out_value, by_values)):
            out[...] = jnp.concatenate(parts, axis=1).astype(low_type)

    columns = pl.BlockSpec((row_total, pair), lambda i: (0, first_step + i))
    out = lambda width: (
        pl.BlockSpec((row_total, width), lambda i: (0, i)),
        ((row_total, steps * width), low_type),
    )
    return call_kernel(
        kernel,
        [joint_proj] * 3 + [attended, grad, inverse] + list(shared),
        blocks
        + [
            columns,
            columns,
            pl.BlockSpec((1, row_total, 8), lambda i: (i, 0, 0)),
        ]
        + shared_specs,
        [
            out(pair),
            out(2 * HEAD),
            out(2 * HEAD),
            (resident((8, HEAD)), ((8, HEAD), jnp.float32)),
        ],
        7.5 * steps,
        "attend_gradient",
        grid=(steps,),
    )


def token_scratch(chips, rows, depth):
    return [pltpu.VMEM((chips * rows, depth), low_type), pltpu.SemaphoreType.DMA((chips,))]


def token_block(rows, width):
    return pl.BlockSpec((1, rows, width), lambda i, *_: (i, 0, 0))


def load_tokens(chips, rows, refs, target, sems):
    step = pl.program_id(0)

    @pl.when(step == 0)
    def _():
        for copy in piece_copies(piece_rows(chips, rows, len(refs)), refs, target, sems):
            copy.start()

    block = target.at[pl.ds(pl.multiple_of(step * rows, rows), rows)]
    pltpu.make_async_copy(block, block, sems.at[step]).wait()
    return block[...]


def times_blocks(x, blocks, columns):
    total, start = None, 0
    for block in blocks:
        rows = block.shape[0]
        term = plain_product(x[:, start : start + rows], block[:, columns])
        total = term if total is None else total + term
        start += rows
    return total


def gated_forward(tokens, joint_w, keep):
    chips = lax.axis_size("rep") // 2
    rows, depth = tokens[0].shape
    units = joint_w[0].shape[1] // 2
    count, blocks = len(tokens), len(joint_w)

    def kernel(*refs):
        weight = refs[count : count + blocks]
        act, to_gate, to_up = refs[count + blocks : count + blocks + 3]
        x = load_tokens(chips, rows, refs[:count], *refs[-2:])
        if keep:
            refs[count + blocks + 3][0] = x
        gate = times_blocks(x, weight, slice(0, units))
        upward = times_blocks(x, weight, slice(units, 2 * units))
        sig = 1.0 / (1.0 + jnp.exp(-gate))
        silu = gate * sig
        act[0] = (silu * upward).astype(low_type)
        to_gate[0] = (upward * sig * (1.0 + gate * (1.0 - sig))).astype(low_type)
        to_up[0] = silu.astype(low_type)

    out = (token_block(rows, units), ((chips, rows, units), low_type))
    kept = (token_block(rows, depth), ((chips, rows, depth), low_type))
    return call_kernel(
        kernel,
        [*tokens, *joint_w],
        [in_place] * count + [resident(block.shape) for block in joint_w],
        [out] * 3 + [kept] * keep,
        0,
        "gated_forward",
        grid=(chips,),
        scratch=token_scratch(chips, rows, depth),
    )


def gated_backward(tokens, halves, down_ws, joint_ws):
    chips, rows, units = halves[0][0].shape
    depth = tokens[0].shape[1]
    count = len(tokens)
    firsts = [0, len(joint_ws[0])]
    joint_flat = [*joint_ws[0], *joint_ws[1]]

    def kernel(*refs):
        factors, down_refs = refs[count : count + 4], refs[count + 4 : count + 6]
        joint_refs = refs[count + 6 : count + 6 + len(joint_flat)]
        outs, scratch = refs[count + 6 + len(joint_flat) : -2], refs[-2:]
        grads, outs = outs[:4], outs[4:]
        grad = load_tokens(chips, rows, refs[:count], *scratch)
        total = None
        for n in range(2):
            grad_act = product_with_transpose(grad, down_refs[n][...])
            gate = (grad_act * factors[2 * n][0].astype(jnp.float32)).astype(low_type)
            upward = (grad_act * factors[2 * n + 1][0].astype(jnp.float32)).astype(low_type)
            grads[2 * n][0] = gate
            grads[2 * n + 1][0] = upward
            term = jnp.concatenate(
                [
                    product_with_transpose(gate, block[:, :units])
                    + product_with_transpose(upward, block[:, units:])
                    for block in joint_refs[firsts[n] : firsts[n] + len(joint_ws[n])]
                ],
                axis=1,
            )
            total = term if total is None else total + term
        for i, out in enumerate(outs):

            @pl.when(pl.program_id(0) == i)
            def _(out=out):
                out[...] = total.astype(low_type)

    narrow = token_block(rows, units)
    outs = call_kernel(
        kernel,
        [*tokens, *halves[0], *halves[1], *down_ws, *joint_flat],
        [in_place] * count
        + [narrow] * 4
        + [resident(w.shape) for w in (*down_ws, *joint_flat)],
        [(narrow, ((chips, rows, units), low_type))] * 4
        + [(resident((rows, depth)), ((rows, depth), low_type))] * chips,
        0,
        "gated_backward",
        grid=(chips,),
        scratch=token_scratch(chips, rows, depth),
    )
    return outs[:2], outs[2:4], outs[4:]


def down_forward(acts, down_ws):
    chips, rows, units = acts[0].shape
    depth = down_ws[0].shape[1]

    def kernel(*refs):
        total = plain_product(refs[0][0], refs[2][...]) + plain_product(refs[1][0], refs[3][...])
        for i, out in enumerate(refs[4:]):

            @pl.when(pl.program_id(0) == i)
            def _(out=out):
                out[...] = total.astype(low_type)

    act = token_block(rows, units)
    return call_kernel(
        kernel,
        [*acts, *down_ws],
        [act, act] + [resident((units, depth))] * 2,
        [(resident((rows, depth)), ((rows, depth), low_type))] * chips,
        0,
        "down_forward",
        grid=(chips,),
    )


def weight_gradient(xs, grads, steps):
    chips, rows, depth = xs[0].shape
    units = grads[0].shape[2]
    width = depth // steps

    def kernel(*refs):
        terms = [
            product_over_rows(
                refs[n][...].reshape(chips * rows, width),
                refs[2 + n][...].reshape(chips * rows, units),
            )
            for n in range(2)
        ]
        refs[4][...] = (terms[0] + terms[1]).astype(low_type)

    return call_kernel(
        kernel,
        [*xs, *grads],
        [pl.BlockSpec((chips, rows, width), lambda i: (0, 0, i))] * 2
        + [resident(grads[0].shape)] * 2,
        [(pl.BlockSpec((width, units), lambda i: (i, 0)), ((depth, units), low_type))],
        11,
        "weight_gradient",
        grid=(steps,),
    )[0]


def down_gradients(acts, grads, steps):
    chips, rows, units = acts[0].shape
    depth = grads[0].shape[1]
    width = depth // steps
    count = len(grads)

    def kernel(*refs):
        act_refs, outs, (own, sems) = refs[count : count + 2], refs[count + 2 : -2], refs[-2:]
        step = pl.program_id(0)

        @pl.when(step == 0)
        def _():
            for copy in piece_copies(piece_rows(chips, rows, count), refs[:count], own, sems):
                copy.start()
            for i in range(chips):
                block = own.at[pl.ds(i * rows, rows)]
                pltpu.make_async_copy(block, block, sems.at[i]).wait()

        right = own[:, pl.ds(pl.multiple_of(step * width, width), width)]
        for act, out in zip(act_refs, outs, strict=True):
            out[...] = product_over_rows(act[...].reshape(chips * rows, units), right).astype(
                low_type
            )

    out = (pl.BlockSpec((units, width), lambda i: (0, i)), ((units, depth), low_type))
    return call_kernel(
        kernel,
        [*grads, *acts],
        [in_place] * count + [resident(acts[0].shape)] * 2,
        [out] * 2,
        0,
        "down_gradients",
        grid=(steps,),
        scratch=token_scratch(chips, rows, depth),
    )


def plane_place():
    rep = lax.axis_index("rep")
    return jnp.stack([rep // 2, rep % 2]).astype(jnp.int32)


def both_cores(pieces):
    return pieces + [swap(stacked(pieces), 1)]


def plane_scratch(chips, rows, width):
    return [
        pltpu.VMEM((2, chips * rows, width), low_type),
        pltpu.SemaphoreType.DMA((2, chips)),
    ]


def load_plane(chips, rows, refs, target, sems):
    @pl.when(pl.program_id(0) == 0)
    def _():
        copies = piece_copies(
            piece_rows(chips, rows, len(refs) - 1), refs[:-1], target.at[0], sems.at[0]
        )
        copies.append(pltpu.make_async_copy(refs[-1], target.at[1], sems.at[1, 0]))
        for copy in copies:
            copy.start()
        for i in range(chips):
            block = target.at[0, pl.ds(i * rows, rows)]
            pltpu.make_async_copy(block, block, sems.at[0, i]).wait()
        pltpu.make_async_copy(target.at[1], target.at[1], sems.at[1, 0]).wait()


def whole_columns(pieces, share):
    size, chips = lax.axis_size("shard"), lax.axis_size("rep") // 2
    rows, width = pieces[0].shape
    step_rows = rows // 4

    def kernel(at, *refs):
        out, target, sems = refs[-3:]
        load_plane(chips, rows, refs[:-3], target, sems)
        step = pl.program_id(0)
        for j in range(2 * chips):
            start = (at[0] ^ (j // 2)) * rows + step * step_rows
            own = target[at[1] ^ (j % 2), pl.ds(pl.multiple_of(start, 16), step_rows), :]
            own = own.astype(jnp.float32)
            for z in range(size):
                first = (z * 2 * chips + j) * share
                out[:, first : first + share] = own[:, z * width // size :][:, :share]

    wide = 2 * chips * size * share
    return call_kernel(
        kernel,
        [plane_place(), *pieces],
        [in_place] * len(pieces),
        [(pl.BlockSpec((step_rows, wide), lambda i, at: (i, 0)), ((rows, wide), jnp.float32))],
        8,
        "whole_columns",
        grid=(4,),
        prefetch=1,
        scratch=plane_scratch(chips, rows, width),
    )[0]


def whole_rows(pieces, share):
    chips = lax.axis_size("rep") // 2
    rows, width = pieces[0].shape

    def kernel(at, *refs):
        out, target, sems = refs[-3:]
        load_plane(chips, rows, refs[:-3], target, sems)
        j = pl.program_id(0)
        start = pl.multiple_of((at[0] ^ (j // 2)) * rows, 32)
        own = target[at[1] ^ (j % 2), pl.ds(start, rows), :].astype(jnp.float32)
        out[0] = own[:share]

    shape = (2 * chips, share, width)
    return call_kernel(
        kernel,
        [plane_place(), *pieces],
        [in_place] * len(pieces),
        [(pl.BlockSpec((1, share, width), lambda j, at: (j, 0, 0)), (shape, jnp.float32))],
        8,
        "whole_rows",
        grid=(2 * chips,),
        prefetch=1,
        scratch=plane_scratch(chips, rows, width),
    )[0].reshape(2 * chips * share, width)


def rows_of(values, width):
    rows = -(-values.shape[0] // width)
    block = jnp.pad(values, (0, rows * width - values.shape[0])).reshape(rows, width)
    return jnp.pad(block, ((0, -rows % 16), (0, 0)))


def in_shard_order(parts):
    size, here = lax.axis_size("shard"), lax.axis_index("shard")
    twice = jnp.concatenate(parts + parts)
    run = parts[0].shape[0]
    return lax.dynamic_slice_in_dim(twice, (size - here) * run, size * run, 0)


def padded(share):
    return -(-share // 32) * 32


def own_columns(weight):
    size, reps = lax.axis_size("shard"), lax.axis_size("rep")
    run = weight.shape[1] // size
    share = run // reps
    rep = lax.axis_index("rep")
    none = jnp.zeros((weight.shape[0], padded(share) - share), weight.dtype)
    parts = []
    for z in range(size):
        parts += [lax.dynamic_slice_in_dim(weight, z * run + rep * share, share, 1), none]
    return jnp.concatenate(parts, axis=1)


def own_rows(weight):
    share = weight.shape[0] // lax.axis_size("rep")
    own = lax.dynamic_slice_in_dim(weight, lax.axis_index("rep") * share, share, 0)
    return jnp.pad(own, ((0, padded(share) - share), (0, 0)))


def scatter_group(partial):
    return lax.psum_scatter(partial, "shard", scatter_dimension=0, tiled=True)


def local(
    tokens,
    norm_gains,
    w_query,
    w_key,
    w_value,
    w_out,
    w_gate,
    w_up,
    w_down,
    seq_lengths,
    seq_device,
    cotangent,
):
    row_total = tokens.shape[0]
    size, reps = lax.axis_size("shard"), lax.axis_size("rep")
    chips = reps // 2
    rep = lax.axis_index("rep")
    device = rep * size + lax.axis_index("shard")
    query_width, key_width = HEADS * HEAD, KV_HEADS * HEAD

    w_joint = jnp.concatenate([w_query, w_key, w_value], axis=1)
    joint, outer = Tiles(w_joint), Tiles(w_out)
    own_tiles = jnp.concatenate([joint.own(w_joint), outer.own(w_out)], axis=1)
    own_tiles = jnp.concatenate([own_tiles, rows_of(norm_gains, own_tiles.shape[1])], axis=0)
    slots = [from_ahead(own_tiles, k) for k in range(1, size)]
    gated_own = jnp.concatenate([own_columns(w_gate), own_columns(w_up)], axis=1)
    live, segment, position = layout(seq_lengths, seq_device, device, row_total)
    cotangent_live = jnp.where(live[:, None], cotangent, jnp.zeros_like(cotangent))
    gated_own, down_own, slots = fence(gated_own, own_rows(w_down), slots)
    gather_shards = lambda own: lax.all_gather(own, "shard", axis=0, tiled=True)
    gated_w, down_w = gather_shards(gated_own), gather_shards(down_own)
    part = joint.part
    joint_tiles = jnp.concatenate([slot[:part, : joint.width] for slot in slots], axis=0)
    joint_near = near_groups(joint_tiles, joint.members)

    out_tiles = jnp.concatenate([slot[:part, joint.width :] for slot in slots], axis=0)
    gains = in_shard_order(
        [norm_gains] + [slot[part:].reshape(-1)[: norm_gains.shape[0]] for slot in slots]
    )
    joint_near, out_tiles, gains = fence(joint_near, out_tiles, gains)
    joint_far = far_group(joint_near, joint.members)
    if joint_far:
        joint_far = [jnp.concatenate(joint_far, axis=0)]
    joint_pieces = joint.across([joint_tiles] + joint_near + joint_far)

    cosine, sine = rotary_tables(position, HEAD)
    gains = gains.astype(jnp.float32)[None]
    gain_in = gains[:, :D]
    gain_ff = gains[:, D + 2 * HEAD :]
    shared = (
        gains[:, D : D + HEAD],
        gains[:, D + HEAD : D + 2 * HEAD],
        jnp.concatenate([cosine, cosine], axis=1),
        jnp.concatenate([0.0 - sine, sine], axis=1),
        segment[:, None],
        segment[None, :],
    )
    joint_pieces, shared, out_tiles = fence(joint_pieces, shared, out_tiles)
    out_groups = all_groups(out_tiles, outer.members)
    joint_proj, normed_in = attention_input(joint, tokens, gain_in, w_joint, joint_pieces)

    joint_proj, normed_in = fence(joint_proj, normed_in)
    half_steps = KV_HEADS // 4
    attended_early, inverse_early = attend(joint_proj, shared, 0, half_steps)

    joint_proj, attended_early, out_groups, normed_in = fence(
        joint_proj, attended_early, out_groups, normed_in
    )
    out_pieces = outer.across(out_groups)
    normed_near = near_groups(normed_in, joint.members)
    attended_late, inverse_late = attend(joint_proj, shared, half_steps, half_steps)
    attended = jnp.concatenate([attended_early, attended_late], axis=1)

    attended, out_pieces = fence(attended, out_pieces)
    hidden, normed_ff = attention_output(outer, attended, tokens, gain_ff, w_out, out_pieces)

    normed_ff, normed_near = fence(normed_ff, normed_near)
    ff_near = near_groups(normed_ff, 2)

    ff_near, gated_w = fence(ff_near, gated_w)
    ff_far = far_group(ff_near, 2)
    half = gated_w.shape[0] // 2
    halves = (gated_w[:half], gated_w[half:])
    ff_far, gated_w, halves, cotangent_live, normed_near = fence(
        ff_far, gated_w, halves, cotangent_live, normed_near
    )
    ff_tokens = [normed_ff] + ff_near + ff_far
    gated_ws = ([gated_w], [swap(part, 1) for part in halves])
    grad_mixed = all_groups(cotangent_live, 2)
    *ours, group_tokens = gated_forward(ff_tokens, gated_ws[0], True)

    ours, gated_ws, group_tokens, attended = fence(ours, gated_ws, group_tokens, attended)
    attended_near = near_groups(attended, outer.members)
    theirs = gated_forward(ff_tokens, gated_ws[1], False)

    theirs, grad_mixed, normed_near = fence(theirs, grad_mixed, normed_near)
    normed_far = far_group(normed_near, joint.members)
    normed_rows = [normed_in] + normed_near + normed_far
    grad_downs = down_gradients((ours[0], theirs[0]), grad_mixed, 2)

    grad_downs, down_w, normed_rows, attended_near = fence(
        grad_downs, down_w, normed_rows, attended_near
    )
    attended_far = far_group(attended_near, outer.members)
    attended_rows = [attended] + attended_near + attended_far
    down_ws = (down_w, swap(down_w, 1))
    other_down = swap(grad_downs[1], 1)

    down_ws, ours, theirs = fence(down_ws, ours, theirs)
    down_parts = down_forward((ours[0], theirs[0]), down_ws)

    down_parts, other_down, group_tokens, attended_rows = fence(
        down_parts, other_down, group_tokens, attended_rows
    )
    down_terms = sum_terms(down_parts, 2)
    grad_down = grad_downs[0].astype(jnp.float32) + other_down.astype(jnp.float32)
    grad_down = scatter_group(grad_down.astype(low_type))
    all_tokens = (group_tokens, swap(group_tokens, 1))
    our_grads, their_grads, grad_x = gated_backward(
        grad_mixed, (ours[1:], theirs[1:]), down_ws, gated_ws
    )

    grad_x, our_grads, their_grads, all_tokens, down_terms = fence(
        grad_x, our_grads, their_grads, all_tokens, down_terms
    )
    grad_terms = sum_terms(grad_x, 2)
    grad_terms = sum_terms(grad_x, 2)
    their_grads = [swap(part, 1) for part in their_grads]
    mixed_full = hidden
    for term in down_terms:
        mixed_full = mixed_full + term.astype(jnp.float32)
    mixed = jnp.where(live[:, None], mixed_full, jnp.zeros_like(mixed_full)).astype(jnp.bfloat16)

    their_grads, mixed = fence(their_grads, mixed)
    grad_gate = weight_gradient(all_tokens, (our_grads[0], their_grads[0]), 4)
    grad_up = weight_gradient(all_tokens, (our_grads[1], their_grads[1]), 4)

    grad_terms, grad_gate, grad_up, grad_down = fence(grad_terms, grad_gate, grad_up, grad_down)
    grad_gate = scatter_group(grad_gate)
    down_near = near_groups(grad_down, 2)
    grad_up = scatter_group(grad_up)
    grad_hidden, cuts, grad_attended, grad_gain_ff = attention_output_gradient(
        outer, grad_terms, cotangent_live, hidden, gain_ff, w_out, out_pieces
    )

    cuts, grad_attended, down_near = fence(cuts, grad_attended, down_near)
    down_far = far_group(down_near, 2)
    out_runs = outer.group_columns([cuts[d] for d in range(outer.groups)])
    half_steps = KV_HEADS // 4
    early = attend_gradient(
        joint_proj, attended, inverse_early, grad_attended, shared, 0, half_steps
    )

    early, out_runs, down_far, grad_gate, grad_attended = fence(
        early, out_runs, down_far, grad_gate, grad_attended
    )
    gate_near = near_groups(grad_gate, 2)
    late = attend_gradient(
        joint_proj, attended, inverse_late, grad_attended, shared, half_steps, half_steps
    )

    early, late, gate_near = fence(early, late, gate_near)
    head_gains = early[3] + late[3]
    parts = [part for n in range(3) for part in (early[n], late[n])]
    grad_joint_low = jnp.concatenate(parts, axis=1)
    cuts, grad_joint_low = fence(joint.cut_columns(grad_joint_low), grad_joint_low)
    joint_runs = joint.group_columns(cuts)
    down_pieces = both_cores([grad_down] + down_near + down_far)
    grad_tokens, grad_gain_in = attention_input_gradient(
        joint, grad_joint_low, grad_hidden, tokens, gain_in, w_joint, joint_pieces
    )

    joint_runs, grad_gain_in, out_runs, down_pieces, gate_near = fence(
        joint_runs, grad_gain_in, out_runs, down_pieces, gate_near
    )
    gate_far = far_group(gate_near, 2)
    sums = outer.tile(attended_rows, out_runs)
    sums = joint.tile(normed_rows, joint_runs, sums)
    grad_gains = jnp.concatenate(
        [grad_gain_in, head_gains[0:1], head_gains[1:2], grad_gain_ff], axis=1
    )[0]
    extra = joint.extra_rows(grad_gains, sums[0].shape[1])

    sums, extra, gate_far = fence(sums, extra, gate_far)
    sums = sums[:1] + tuple(swap(part, h) for h, part in enumerate(sums) if h)
    gate_pieces = both_cores([grad_gate] + gate_near + gate_far)

    sums, down_pieces, gate_pieces = fence(sums, down_pieces, gate_pieces)
    own, sent = joint.send(sums, extra)
    up_near = near_groups(grad_up, 2)
    whole_down = whole_rows(down_pieces, w_down.shape[0] // reps)
    whole_gate = whole_columns(gate_pieces, w_down.shape[0] // reps)

    own, sent, whole_down, whole_gate, up_near = fence(own, sent, whole_down, whole_gate, up_near)
    total = own
    for part in sent:
        total = total + part.astype(jnp.float32)
    total_groups = all_groups(total.astype(low_type), joint.members)
    up_far = far_group(up_near, 2)

    total_groups, up_far = fence(total_groups, up_far)
    whole_pieces = joint.across_stacked(total_groups)
    up_pieces = both_cores([grad_up] + up_near + up_far)
    *grad_joint, grad_out_w, beneath = joint.whole(
        whole_pieces, ((query_width, key_width, key_width), (D,))
    )
    grad_gains = beneath.reshape(-1)[: norm_gains.shape[0]]
    share = w_down.shape[0] // reps
    return (
        mixed,
        grad_tokens,
        grad_gains,
        *grad_joint,
        grad_out_w,
        whole_gate,
        whole_columns(up_pieces, share),
        whole_down,
    )


def solution(mesh):
    return jax.shard_map(
        local,
        mesh=mesh,
        in_specs=(
            P(("rep", "shard"), None),
            P("shard"),
            P("shard", None),
            P("shard", None),
            P("shard", None),
            P("shard", None),
            P("shard", None),
            P("shard", None),
            P("shard", None),
            P(),
            P(),
            P(("rep", "shard"), None),
        ),
        out_specs=(
            P(("rep", "shard"), None),
            P(("rep", "shard"), None),
            P("shard"),
            P("shard", None),
            P("shard", None),
            P("shard", None),
            P("shard", None),
            P("shard", None),
            P("shard", None),
            P("shard", None),
        ),
        check_vma=False,
    )
```

```python
import math

import jax
import jax.numpy as jnp
from jax import lax
from jax.experimental import pallas as pl
from jax.experimental.pallas import tpu as pltpu
from jax.sharding import PartitionSpec as P

D = 1536
HEADS = 24
KV_HEADS = 8
HEAD = 64
FF = 6912


epsilon = 1e-05
rope_base = 1000000.0
masked_score = -1e30


def plain_product(left, right):
    return jnp.dot(left, right, preferred_element_type=jnp.float32)


def product_over_rows(left, right):
    return lax.dot_general(
        left, right, (((0,), (0,)), ((), ())), preferred_element_type=jnp.float32
    )


def product_with_transpose(left, right):
    return lax.dot_general(
        left, right, (((1,), (1,)), ((), ())), preferred_element_type=jnp.float32
    )


def rotary_tables(position, head_width):
    half_width = head_width // 2
    index = jnp.arange(half_width).astype(jnp.float32)
    inverse = jnp.exp(index * (-2.0 * math.log(rope_base) / head_width))
    angle = position.astype(jnp.float32)[:, None] * inverse[None, :]
    return (jnp.cos(angle), jnp.sin(angle))


def layout(seq_lengths, seq_device, device, row_total):
    own_length = jnp.where(seq_device == device, seq_lengths, 0)
    ends = jnp.cumsum(own_length, dtype=jnp.int32)
    begins = ends - own_length
    slot_index = jnp.arange(row_total, dtype=jnp.int32)
    inside = (slot_index[:, None] >= begins[None, :]) & (slot_index[:, None] < ends[None, :])
    live = jnp.any(inside, axis=1)
    seq_total = seq_lengths.shape[0]
    numbers = jnp.arange(seq_total, dtype=jnp.int32)
    found = jnp.sum(jnp.where(inside, numbers[None, :], 0), axis=1, dtype=jnp.int32)
    segment = jnp.where(live, found, seq_total + slot_index)
    offset = jnp.sum(jnp.where(inside, (0 - begins)[None, :], 0), axis=1, dtype=jnp.int32)
    position = jnp.where(live, slot_index + offset, 0)
    return (live, segment, position)


vmem_bytes = 60 * 2**20
low_type = jnp.bfloat16
in_place = pl.BlockSpec(memory_space=pl.ANY)


def swap(values, offset):
    size = lax.axis_size("rep")
    return lax.ppermute(values, "rep", [(i, i ^ offset) for i in range(size)])


def from_ahead(values, steps):
    size = lax.axis_size("shard")
    return lax.ppermute(values, "shard", [((i + steps) % size, i) for i in range(size)])


def from_behind(values, steps):
    size = lax.axis_size("shard")
    return lax.ppermute(values, "shard", [(i, (i + steps) % size) for i in range(size)])


def fence(*values):
    return lax.optimization_barrier(values)


def after(values, *others):
    return lax.optimization_barrier((values, others))[0]


def all_groups(block, unit):
    return [block] + [swap(block, unit * d) for d in range(1, lax.axis_size("rep") // unit)]


def sum_terms(blocks, unit):
    return [swap(block, unit * d) if d else block for d, block in enumerate(blocks)]


def near_groups(block, unit):
    groups = lax.axis_size("rep") // unit
    return [swap(block, unit * d) for d in range(1, groups if groups != 4 else 3)]


def far_group(near, unit):
    if lax.axis_size("rep") // unit != 4:
        return []
    half = half_rows(near[0].shape[0])
    return [swap(near[1][:half], unit), swap(near[0][half:], 2 * unit)]


def far_terms(blocks, unit):
    return [swap(blocks[3][0], unit), swap(blocks[3][1], 2 * unit)] if len(blocks) == 4 else []


def near_terms(blocks, far, unit):
    if not far:
        return [swap(block[0], unit * d) if d else block[0] for d, block in enumerate(blocks)]
    half = blocks[3][0].shape[0]
    one, two = blocks[1][0], blocks[2][0]
    add = lambda left, right: (left.astype(jnp.float32) + right.astype(jnp.float32)).astype(low_type)
    one = jnp.concatenate([one[:half], add(one[half:], far[1])], axis=0)
    two = jnp.concatenate([add(two[:half], far[0]), two[half:]], axis=0)
    return [blocks[0][0], swap(one, unit), swap(two, 2 * unit)]


def half_rows(rows):
    return rows // 2 // 16 * 16


def piece_rows(groups, rows, count):
    half = half_rows(rows)
    return [[rows]] * groups if count == groups else [[rows]] * 3 + [[half, rows - half]]


def piece_copies(rows, refs, target, sems):
    copies, at, n = [], 0, 0
    for i, group in enumerate(rows):
        for count in group:
            copies.append(
                pltpu.make_async_copy(refs[n], target.at[pl.ds(at, count)], sems.at[i])
            )
            at += count
            n += 1
    return copies


def call_kernel(kernel, args, ins, outs, micros, name, grid=None, prefetch=0, scratch=()):
    return pl.pallas_call(
        kernel,
        grid_spec=pltpu.PrefetchScalarGridSpec(
            num_scalar_prefetch=prefetch,
            grid=grid or (1,),
            in_specs=ins,
            out_specs=[spec for spec, _ in outs],
            scratch_shapes=list(scratch),
        ),
        out_shape=[jax.ShapeDtypeStruct(*shape) for _, shape in outs],
        compiler_params=pltpu.CompilerParams(vmem_limit_bytes=vmem_bytes),
        cost_estimate=pl.CostEstimate(flops=int(micros * 1.15e9), bytes_accessed=0, transcendentals=0),
        name=name,
    )(*args)


def resident(shape):
    return pl.BlockSpec(shape, lambda *_: (0,) * len(shape), pipeline_mode=pl.Buffered(1))


def spread(values, shards, members):
    part = values.shape[1] // shards // members
    return [
        jnp.concatenate(
            [values[:, (z * members + p) * part :][:, :part] for z in range(shards)], axis=1
        )
        for p in range(members)
    ]


def unspread(parts, shards):
    part = parts[0].shape[1] // shards
    return jnp.concatenate(
        [run[:, z * part : (z + 1) * part] for z in range(shards) for run in parts], axis=1
    )


def norm_factor(values):
    return lax.rsqrt(jnp.mean(values * values, axis=-1, keepdims=True) + epsilon)


def norm_gradient(values, gain, grad):
    factor = norm_factor(values)
    scaled = grad * gain
    mean = jnp.mean(scaled * values, axis=-1, keepdims=True)
    by_gain = jnp.sum(grad * values * factor, axis=0, keepdims=True)
    return factor * scaled - values * (factor * factor * factor * mean), by_gain


def stacked(pieces):
    rows = sum(piece.shape[0] for piece in pieces)

    def kernel(*refs):
        copies, start = [], 0
        for n, piece in enumerate(pieces):
            target = refs[len(pieces)].at[pl.ds(start, piece.shape[0])]
            copies.append(pltpu.make_async_copy(refs[n], target, refs[-1].at[n]))
            start += piece.shape[0]
        for copy in copies:
            copy.start()
        for copy in copies:
            copy.wait()

    shape = (rows, pieces[0].shape[1])
    return call_kernel(
        kernel,
        pieces,
        [in_place] * len(pieces),
        [(resident(shape), (shape, low_type))],
        0,
        "stacked",
        scratch=[pltpu.SemaphoreType.DMA((len(pieces),))],
    )[0]


class Tiles:
    def __init__(self, weight):
        reps = lax.axis_size("rep")
        groups = reps // 2
        while weight.shape[1] % (128 * groups):
            groups //= 2
        self.groups, self.members = groups, reps // groups
        self.shards, self.here = lax.axis_size("shard"), lax.axis_index("shard")
        self.group = lax.axis_index("rep") // self.members
        self.member = lax.axis_index("rep") % self.members
        self.rows = weight.shape[0]
        self.part = self.rows // self.members
        self.rest = (self.shards - 1) * self.part
        self.depth = self.shards * self.part
        self.width = weight.shape[1] // groups

    def own(self, weight):
        return lax.dynamic_slice(
            weight, (self.member * self.part, self.group * self.width), (self.part, self.width)
        )

    def across(self, pieces):
        return pieces + [swap(piece, h) for h in range(1, self.members) for piece in pieces]

    def across_stacked(self, pieces):
        stack = stacked(pieces)
        return pieces + [swap(stack, h) for h in range(1, self.members)]

    def place(self):
        return jnp.stack([self.group, self.member, self.here]).astype(jnp.int32)

    def scratch(self):
        shape = (self.members, self.groups)
        return [
            pltpu.VMEM(shape + (self.depth, self.width), low_type),
            pltpu.SemaphoreType.DMA(shape),
        ]

    def load(self, at, weight_ref, refs, tiles, sems):
        part, shards, groups = self.part, self.shards, self.groups

        def to(h, d, z, start, size):
            first = pl.multiple_of(lax.rem(at[2] + z, shards) * part, 16) + start
            return tiles.at[h, d, pl.ds(pl.multiple_of(first, 16), size)]

        for d in range(groups):
            for h in range(self.members):
                source = weight_ref.at[
                    pl.ds(pl.multiple_of((at[1] ^ h) * part, 16), part),
                    pl.ds(pl.multiple_of((at[0] ^ d) * self.width, 128), self.width),
                ]
                pltpu.make_async_copy(source, to(h, d, 0, 0, part), sems.at[h, d]).start()
                for k in range(shards - 1):
                    pltpu.make_async_copy(
                        refs[h * groups + d].at[pl.ds(k * part, part)],
                        to(h, d, k + 1, 0, part),
                        sems.at[h, d],
                    ).start()

        def wait(h, d):
            pltpu.make_async_copy(tiles.at[h, d], tiles.at[h, d], sems.at[h, d]).wait()
            return tiles[h, d]

        return wait

    def columns(self, at, d):
        return pl.ds(pl.multiple_of((at[0] ^ d) * self.width, 128), self.width)

    def multiply(self, at, wait, x, out):
        for d in range(self.groups):
            total = None
            for h in range(self.members):
                term = plain_product(x[at[1] ^ h], wait(h, d))
                total = term if total is None else total + term
            out[:, self.columns(at, d)] = total

    def multiply_transposed(self, at, wait, grad, out):
        totals = [None] * self.members
        for d in range(self.groups):
            block = grad[:, self.columns(at, d)]
            for h in range(self.members):
                term = product_with_transpose(block, wait(h, d))
                totals[h] = term if totals[h] is None else totals[h] + term
        for h in range(self.members):
            out[at[1] ^ h] = totals[h]

    def call(self, kernel, args, weight, pieces, outs, micros, name, scratch=()):
        given, produced = len(args), len(outs)

        def whole_kernel(at, *refs):
            ins, weight_ref = refs[:given], refs[given]
            rest = refs[given + 1 + len(pieces) :]
            wait = self.load(
                at, weight_ref, refs[given + 1 : given + 1 + len(pieces)], *rest[produced : produced + 2]
            )
            kernel(at, ins, rest[:produced], rest[produced + 2 :], wait)

        return call_kernel(
            whole_kernel,
            [self.place(), *args, weight, *pieces],
            [resident(arg.shape) for arg in args] + [in_place] * (1 + len(pieces)),
            [(resident(shape), (shape, kind)) for shape, kind in outs],
            micros,
            name,
            prefetch=1,
            scratch=self.scratch() + list(scratch),
        )

    def cut_columns(self, grad):
        return [
            lax.dynamic_slice_in_dim(grad, (self.group ^ d) * self.width, self.width, 1)
            for d in range(self.groups)
        ]

    def group_columns(self, cuts):
        return [swap(cut, self.members * d) if d else cut for d, cut in enumerate(cuts)]

    def tile(self, rows, columns, beside=()):
        tokens, members, shards, part = columns[0].shape[0], self.members, self.shards, self.part
        count, total = len(rows), len(columns) * tokens
        sizes = [piece.shape[0] for piece in rows]
        wide = self.width + (beside[0].shape[1] if beside else 0)

        def kernel(at, *refs):
            besides = refs[count + len(columns) : count + len(columns) + len(beside)]
            outs = refs[count + len(columns) + len(beside) : -4]
            left, right, whole, sems = refs[-4:]
            copies = piece_copies([sizes], refs[:count], left, sems.at[pl.ds(0, 1)])
            copies += piece_copies(
                [[tokens] * len(columns)], refs[count : count + len(columns)], right, sems.at[pl.ds(1, 1)]
            )
            for copy in copies:
                copy.start()
            pltpu.make_async_copy(left, left, sems.at[0]).wait()
            pltpu.make_async_copy(right, right, sems.at[1]).wait()
            whole[...] = product_over_rows(left[...], right[...])
            for h in range(members):
                for k in range(shards):
                    start = lax.rem(at[2] + k, shards) * self.rows + (at[1] ^ h) * part
                    block = whole[pl.ds(pl.multiple_of(start, 16), part), :]
                    outs[h][k * part : (k + 1) * part, : self.width] = block.astype(outs[h].dtype)
                if beside:
                    outs[h][:, self.width :] = besides[h][...]

        shape = (shards * part, wide)
        return call_kernel(
            kernel,
            [self.place(), *rows, *columns, *beside],
            [in_place] * (count + len(columns)) + [resident(part.shape) for part in beside],
            [(resident(shape), (shape, low_type if h else jnp.float32)) for h in range(members)],
            7,
            "weight_tile",
            prefetch=1,
            scratch=[
                pltpu.VMEM((total, members * self.depth), low_type),
                pltpu.VMEM((total, self.width), low_type),
                pltpu.VMEM((members * self.depth, self.width), jnp.float32),
                pltpu.SemaphoreType.DMA((2,)),
            ],
        )

    def send(self, tiles, extra):
        total = tiles[0]
        for tile in tiles[1:]:
            total = total + tile.astype(jnp.float32)
        parts = [
            jnp.concatenate([total[k * self.part : (k + 1) * self.part], extra[k]], axis=0)
            for k in range(self.shards)
        ]
        return parts[0], [
            from_behind(parts[k].astype(low_type), k) for k in range(1, self.shards)
        ]

    def extra_rows(self, values, width):
        runs = values.reshape(self.shards, -1)
        block = jnp.stack([rows_of(runs[z], width) for z in range(self.shards)])
        twice = jnp.concatenate([block, block], axis=0)
        return lax.dynamic_slice_in_dim(twice, self.here, self.shards, 0)

    def whole(self, pieces, sections):
        members, groups, part = self.members, self.groups, self.part
        rows, wide = pieces[0].shape
        beneath = rows - part

        def kernel(at, *refs):
            outs, (tiles, sems) = refs[len(pieces) : -2], refs[-2:]
            for h in range(members):
                for d in range(groups):
                    ref = refs[groups + h - 1].at[pl.ds(d * rows, rows)] if h else refs[d]
                    pltpu.make_async_copy(ref, tiles.at[h, d], sems.at[h, d]).start()
            for h in range(members):
                for d in range(groups):
                    pltpu.make_async_copy(tiles.at[h, d], tiles.at[h, d], sems.at[h, d]).wait()
            total = None
            for g in range(groups):
                for p in range(members):
                    block = tiles[at[1] ^ p, at[0] ^ g].astype(jnp.float32)
                    total = block[part:] if total is None else total + block[part:]
                    n, left = 0, 0
                    for widths in sections:
                        width = sum(widths) // groups
                        first = 0
                        for run in widths:
                            low, high = max(first, g * width), min(first + run, (g + 1) * width)
                            if low < high:
                                outs[n][p * part : (p + 1) * part, low - first : high - first] = (
                                    block[:part, left + low - g * width : left + high - g * width]
                                )
                            first += run
                            n += 1
                        left += width
            outs[-1][...] = total

        shapes = [(self.rows, run) for widths in sections for run in widths] + [(beneath, wide)]
        return call_kernel(
            kernel,
            [self.place(), *pieces],
            [in_place] * len(pieces),
            [(resident(shape), (shape, jnp.float32)) for shape in shapes],
            6,
            "whole_tiles",
            prefetch=1,
            scratch=[
                pltpu.VMEM((members, groups, rows, wide), low_type),
                pltpu.SemaphoreType.DMA((members, groups)),
            ],
        )


def attention_input(tiles, tokens, gain, weight, pieces):
    def kernel(at, ins, outs, scratch, wait):
        x = ins[0][...].astype(jnp.float32)
        normed = (x * norm_factor(x) * ins[1][...]).astype(low_type)
        outs[1][...] = normed
        for p, run in enumerate(spread(normed, tiles.shards, tiles.members)):
            scratch[0][p] = run
        tiles.multiply(at, wait, scratch[0], outs[0])

    rows = tokens.shape[0]
    return tiles.call(
        kernel,
        [tokens, gain],
        weight,
        pieces,
        [
            ((rows, weight.shape[1]), jnp.float32),
            (tokens.shape, low_type),
        ],
        0,
        "attention_input",
        scratch=[pltpu.VMEM((tiles.members, rows, tiles.depth), low_type)],
    )


def attention_output(tiles, attended, tokens, gain, weight, pieces):
    def kernel(at, ins, outs, scratch, wait):
        for p, run in enumerate(spread(ins[0][...], tiles.shards, tiles.members)):
            scratch[0][p] = run
        tiles.multiply(at, wait, scratch[0], outs[0])
        hidden = outs[0][...] + ins[1][...].astype(jnp.float32)
        outs[0][...] = hidden
        outs[1][...] = (hidden * norm_factor(hidden) * ins[2][...]).astype(low_type)

    rows, depth = tokens.shape
    return tiles.call(
        kernel,
        [attended, tokens, gain],
        weight,
        pieces,
        [
            ((rows, depth), jnp.float32),
            ((rows, depth), low_type),
        ],
        0,
        "attention_output",
        scratch=[pltpu.VMEM((tiles.members, rows, tiles.depth), low_type)],
    )


def attention_output_gradient(tiles, terms, grad, hidden, gain, weight, pieces):
    count = len(terms)

    def kernel(at, ins, outs, scratch, wait):
        total = ins[0][...].astype(jnp.float32)
        for term in ins[1:count]:
            total = total + term[...].astype(jnp.float32)
        by_hidden, by_gain = norm_gradient(ins[count + 1][...], ins[count + 2][...], total)
        by_hidden = by_hidden + ins[count][...].astype(jnp.float32)
        outs[0][...] = by_hidden
        low = scratch[1]
        low[...] = by_hidden.astype(low_type)
        outs[1][...] = by_gain
        for d in range(tiles.groups):
            outs[3 + d][...] = low[:, tiles.columns(at, d)]
        tiles.multiply_transposed(at, wait, low, scratch[0])
        runs = [scratch[0][p].astype(low_type) for p in range(tiles.members)]
        outs[2][...] = unspread(runs, tiles.shards)

    rows, depth = grad.shape
    return tiles.call(
        kernel,
        [*terms, grad, hidden, gain],
        weight,
        pieces,
        [
            ((rows, depth), jnp.float32),
            ((1, depth), jnp.float32),
            ((rows, depth), low_type),
        ]
        + [((rows, tiles.width), low_type)] * tiles.groups,
        30,
        "attention_output_gradient",
        scratch=[
            pltpu.VMEM((tiles.members, rows, tiles.depth), jnp.float32),
            pltpu.VMEM((rows, depth), low_type),
        ],
    )


def attention_input_gradient(tiles, grad, grad_hidden, tokens, gain, weight, pieces):
    def kernel(at, ins, outs, scratch, wait):
        tiles.multiply_transposed(at, wait, ins[0], scratch[0])
        total = unspread([scratch[0][p] for p in range(tiles.members)], tiles.shards)
        by_tokens, by_gain = norm_gradient(
            ins[2][...].astype(jnp.float32), ins[3][...], total
        )
        outs[0][...] = ins[1][...] + by_tokens
        outs[1][...] = by_gain

    rows, depth = tokens.shape
    return tiles.call(
        kernel,
        [grad, grad_hidden, tokens, gain],
        weight,
        pieces,
        [((rows, depth), jnp.float32), ((1, depth), jnp.float32)],
        10,
        "attention_input_gradient",
        scratch=[pltpu.VMEM((tiles.members, rows, tiles.depth), jnp.float32)],
    )


def turn(values):
    half = values.shape[1] // 2
    return jnp.concatenate([values[:, half:], values[:, :half]], axis=1)


def head_of(block, n):
    return block[:, n * HEAD : (n + 1) * HEAD]


def rotated_head(values, gain, cosine, sine):
    normed = values * norm_factor(values) * gain
    return (normed * cosine + turn(normed) * sine).astype(low_type)


def head_gradient(values, gain, cosine, sine, grad):
    return norm_gradient(values, gain, grad * cosine - turn(grad) * sine)


def chunk_of(row_total):
    return min(row_total, 128)


def allowed_scores(rows, columns, start, chunk):
    end = start + chunk
    later = start + lax.broadcasted_iota(jnp.int32, (chunk, end), 0)
    earlier = lax.broadcasted_iota(jnp.int32, (chunk, end), 1)
    return (rows[start:end] == columns[:, :end]) & (later >= earlier)


def head_weights(query, key, allowed):
    scores = product_with_transpose(query, key) * HEAD ** (-0.5)
    return jnp.where(allowed, jnp.exp(scores), 0.0)


def head_specs(row_total, first_step=0):
    pair = 2 * HEADS // KV_HEADS * HEAD
    first_key, first_value = HEADS * HEAD // (2 * HEAD), (HEADS + KV_HEADS) * HEAD // (2 * HEAD)
    blocks = [
        pl.BlockSpec((row_total, pair), lambda i: (0, first_step + i)),
        pl.BlockSpec((row_total, 2 * HEAD), lambda i: (0, first_key + first_step + i)),
        pl.BlockSpec((row_total, 2 * HEAD), lambda i: (0, first_value + first_step + i)),
    ]
    shared = [(1, HEAD), (1, HEAD), (row_total, HEAD), (row_total, HEAD), (row_total, 1), (1, row_total)]
    return pair, blocks, [resident(shape) for shape in shared]


def attend(joint_proj, shared, first_step, steps):
    row_total = joint_proj.shape[0]
    ratio, chunk = HEADS // KV_HEADS, chunk_of(joint_proj.shape[0])
    pair, blocks, shared_specs = head_specs(row_total, first_step)

    def kernel(query_ref, key_ref, value_ref, query_gain, key_gain, cosine, sine, rows, columns, out, inverse):
        turns = (cosine[...], sine[...])
        heads = [[] for _ in range(2 * ratio)]
        inverses = [[] for _ in range(2 * ratio)]
        for g in range(2):
            key = rotated_head(head_of(key_ref[...], g), key_gain[...], *turns)
            value = head_of(value_ref[...], g).astype(low_type)
            value = jnp.concatenate([value, jnp.ones_like(value)], axis=1)
            queries = [
                rotated_head(head_of(query_ref[...], ratio * g + j), query_gain[...], *turns)
                for j in range(ratio)
            ]
            for start in range(0, row_total, chunk):
                end = start + chunk
                allowed = allowed_scores(rows[...], columns[...], start, chunk)
                batch = jnp.concatenate([query[start:end] for query in queries], axis=0)
                weights = head_weights(
                    batch, key[:end], jnp.concatenate([allowed] * ratio, axis=0)
                )
                sums = plain_product(weights.astype(low_type), value[:end])
                inverted = 1.0 / sums[:, HEAD : HEAD + 1]
                done = (sums[:, :HEAD] * inverted).astype(low_type)
                for j in range(ratio):
                    heads[ratio * g + j].append(done[j * chunk : (j + 1) * chunk])
                    inverses[ratio * g + j].append(inverted[j * chunk : (j + 1) * chunk])
        out[...] = jnp.concatenate([jnp.concatenate(head, axis=0) for head in heads], axis=1)
        for n, parts in enumerate(inverses):
            inverse[0, :, n : n + 1] = jnp.concatenate(parts, axis=0)

    return call_kernel(
        kernel,
        [joint_proj] * 3 + list(shared),
        blocks + shared_specs,
        [
            (pl.BlockSpec((row_total, pair), lambda i: (0, i)), ((row_total, steps * pair), low_type)),
            (
                pl.BlockSpec((1, row_total, 8), lambda i: (i, 0, 0)),
                ((steps, row_total, 8), jnp.float32),
            ),
        ],
        0,
        "attend",
        grid=(steps,),
    )


def attend_gradient(joint_proj, attended, inverse, grad, shared, first_step, steps):
    row_total = joint_proj.shape[0]
    ratio, chunk = HEADS // KV_HEADS, chunk_of(joint_proj.shape[0])
    pair, blocks, shared_specs = head_specs(row_total, first_step)
    scale = HEAD ** (-0.5)

    def kernel(
        query_ref,
        key_ref,
        value_ref,
        attended_ref,
        grad_ref,
        inverse_ref,
        query_gain,
        key_gain,
        cosine,
        sine,
        rows,
        columns,
        out_query,
        out_key,
        out_value,
        gains,
    ):
        step = pl.program_id(0)
        turns = (cosine[...], sine[...])

        @pl.when(step == 0)
        def _():
            gains[...] = jnp.zeros_like(gains)

        by_queries, by_keys, by_values = [], [], []
        for g in range(2):
            key_proj = head_of(key_ref[...], g)
            key = rotated_head(key_proj, key_gain[...], *turns)
            value = head_of(value_ref[...], g).astype(low_type)
            projs = [head_of(query_ref[...], ratio * g + j) for j in range(ratio)]
            queries = [rotated_head(proj, query_gain[...], *turns) for proj in projs]
            grads = [head_of(grad_ref[...], ratio * g + j) for j in range(ratio)]
            inners = [
                jnp.sum(
                    grads[j].astype(jnp.float32)
                    * head_of(attended_ref[...], ratio * g + j).astype(jnp.float32),
                    axis=-1,
                    keepdims=True,
                )
                for j in range(ratio)
            ]
            turned = [[] for _ in range(ratio)]
            by_key = by_value = None
            for start in range(row_total - chunk, -1, -chunk):
                end = start + chunk
                allowed = allowed_scores(rows[...], columns[...], start, chunk)
                stacked_heads = lambda parts: jnp.concatenate(
                    [part[start:end] for part in parts], axis=0
                )
                query_batch, grad_batch = stacked_heads(queries), stacked_heads(grads)
                inverted = jnp.concatenate(
                    [
                        inverse_ref[0, start:end, ratio * g + j : ratio * g + j + 1]
                        for j in range(ratio)
                    ],
                    axis=0,
                )
                weights = head_weights(
                    query_batch, key[:end], jnp.concatenate([allowed] * ratio, axis=0)
                )
                probs = weights * inverted
                grad_probs = product_with_transpose(grad_batch, value[:end])
                grad_scores = (probs * (grad_probs - stacked_heads(inners))).astype(low_type)
                by_batch = plain_product(grad_scores, key[:end]) * scale
                for j in range(ratio):
                    turned[j].insert(0, by_batch[j * chunk : (j + 1) * chunk])
                key_term = product_over_rows(grad_scores, query_batch) * scale
                value_term = product_over_rows(probs.astype(low_type), grad_batch)
                if by_key is None:
                    by_key, by_value = key_term, value_term
                else:
                    by_key = jnp.concatenate([by_key[:end] + key_term, by_key[end:]], axis=0)
                    by_value = jnp.concatenate([by_value[:end] + value_term, by_value[end:]], axis=0)
            for j in range(ratio):
                by_query, by_gain = head_gradient(
                    projs[j], query_gain[...], *turns, jnp.concatenate(turned[j], axis=0)
                )
                by_queries.append(by_query)
                gains[0:1, :] += by_gain
            by_key, by_gain = head_gradient(key_proj, key_gain[...], *turns, by_key)
            by_keys.append(by_key)
            by_values.append(by_value)
            gains[1:2, :] += by_gain
        for out, parts in ((out_query, by_queries), (out_key, by_keys), (out_value, by_values)):
            out[...] = jnp.concatenate(parts, axis=1).astype(low_type)

    columns = pl.BlockSpec((row_total, pair), lambda i: (0, first_step + i))
    out = lambda width: (
        pl.BlockSpec((row_total, width), lambda i: (0, i)),
        ((row_total, steps * width), low_type),
    )
    return call_kernel(
        kernel,
        [joint_proj] * 3 + [attended, grad, inverse] + list(shared),
        blocks
        + [
            columns,
            columns,
            pl.BlockSpec((1, row_total, 8), lambda i: (i, 0, 0)),
        ]
        + shared_specs,
        [
            out(pair),
            out(2 * HEAD),
            out(2 * HEAD),
            (resident((8, HEAD)), ((8, HEAD), jnp.float32)),
        ],
        20 * steps,
        "attend_gradient",
        grid=(steps,),
    )


def token_scratch(chips, rows, depth):
    return [pltpu.VMEM((chips * rows, depth), low_type), pltpu.SemaphoreType.DMA((chips,))]


def token_block(rows, width):
    return pl.BlockSpec((1, rows, width), lambda i, *_: (i, 0, 0))


def load_tokens(chips, rows, refs, target, sems):
    step = pl.program_id(0)

    @pl.when(step == 0)
    def _():
        for copy in piece_copies(piece_rows(chips, rows, len(refs)), refs, target, sems):
            copy.start()

    block = target.at[pl.ds(pl.multiple_of(step * rows, rows), rows)]
    pltpu.make_async_copy(block, block, sems.at[step]).wait()
    return block[...]


def times_blocks(x, blocks, columns):
    total, start = None, 0
    for block in blocks:
        rows = block.shape[0]
        term = plain_product(x[:, start : start + rows], block[:, columns])
        total = term if total is None else total + term
        start += rows
    return total


def gated_forward(tokens, joint_w, keep):
    chips = lax.axis_size("rep") // 2
    rows, depth = tokens[0].shape
    units = joint_w[0].shape[1] // 2
    count, blocks = len(tokens), len(joint_w)

    def kernel(*refs):
        weight = refs[count : count + blocks]
        act, to_gate, to_up = refs[count + blocks : count + blocks + 3]
        x = load_tokens(chips, rows, refs[:count], *refs[-2:])
        if keep:
            refs[count + blocks + 3][0] = x
        gate = times_blocks(x, weight, slice(0, units))
        upward = times_blocks(x, weight, slice(units, 2 * units))
        sig = 1.0 / (1.0 + jnp.exp(-gate))
        silu = gate * sig
        act[0] = (silu * upward).astype(low_type)
        to_gate[0] = (upward * sig * (1.0 + gate * (1.0 - sig))).astype(low_type)
        to_up[0] = silu.astype(low_type)

    out = (token_block(rows, units), ((chips, rows, units), low_type))
    kept = (token_block(rows, depth), ((chips, rows, depth), low_type))
    return call_kernel(
        kernel,
        [*tokens, *joint_w],
        [in_place] * count + [resident(block.shape) for block in joint_w],
        [out] * 3 + [kept] * keep,
        0,
        "gated_forward",
        grid=(chips,),
        scratch=token_scratch(chips, rows, depth),
    )


def gated_backward(tokens, halves, down_ws, joint_ws):
    chips, rows, units = halves[0][0].shape
    depth = tokens[0].shape[1]
    count = len(tokens)
    firsts = [0, len(joint_ws[0])]
    cuts = piece_rows(chips, rows, 5 if chips == 4 else chips)
    joint_flat = [*joint_ws[0], *joint_ws[1]]

    def kernel(*refs):
        factors, down_refs = refs[count : count + 4], refs[count + 4 : count + 6]
        joint_refs = refs[count + 6 : count + 6 + len(joint_flat)]
        outs, scratch = refs[count + 6 + len(joint_flat) : -2], refs[-2:]
        grads, outs = outs[:4], outs[4:]
        grad = load_tokens(chips, rows, refs[:count], *scratch)
        total = None
        for n in range(2):
            grad_act = product_with_transpose(grad, down_refs[n][...])
            gate = (grad_act * factors[2 * n][0].astype(jnp.float32)).astype(low_type)
            upward = (grad_act * factors[2 * n + 1][0].astype(jnp.float32)).astype(low_type)
            grads[2 * n][0] = gate
            grads[2 * n + 1][0] = upward
            term = jnp.concatenate(
                [
                    product_with_transpose(gate, block[:, :units])
                    + product_with_transpose(upward, block[:, units:])
                    for block in joint_refs[firsts[n] : firsts[n] + len(joint_ws[n])]
                ],
                axis=1,
            )
            total = term if total is None else total + term
        n = 0
        for i, group in enumerate(cuts):
            start = 0
            for size in group:

                @pl.when(pl.program_id(0) == i)
                def _(out=outs[n], start=start, size=size):
                    out[...] = total[start : start + size].astype(low_type)

                start += size
                n += 1

    narrow = token_block(rows, units)
    shapes = [(size, depth) for group in cuts for size in group]
    outs = call_kernel(
        kernel,
        [*tokens, *halves[0], *halves[1], *down_ws, *joint_flat],
        [in_place] * count
        + [narrow] * 4
        + [resident(w.shape) for w in (*down_ws, *joint_flat)],
        [(narrow, ((chips, rows, units), low_type))] * 4
        + [(resident(shape), (shape, low_type)) for shape in shapes],
        0,
        "gated_backward",
        grid=(chips,),
        scratch=token_scratch(chips, rows, depth),
    )
    return outs[:2], outs[2:4], as_groups(outs[4:], cuts)


def as_groups(pieces, cuts):
    groups, n = [], 0
    for group in cuts:
        groups.append(list(pieces[n : n + len(group)]))
        n += len(group)
    return groups


def down_forward(acts, down_ws):
    chips, rows, units = acts[0].shape
    depth = down_ws[0].shape[1]

    def kernel(*refs):
        total = plain_product(refs[0][0], refs[2][...]) + plain_product(refs[1][0], refs[3][...])
        for i, out in enumerate(refs[4:]):

            @pl.when(pl.program_id(0) == i)
            def _(out=out):
                out[...] = total.astype(low_type)

    act = token_block(rows, units)
    return call_kernel(
        kernel,
        [*acts, *down_ws],
        [act, act] + [resident((units, depth))] * 2,
        [(resident((rows, depth)), ((rows, depth), low_type))] * chips,
        0,
        "down_forward",
        grid=(chips,),
    )


def weight_gradient(xs, grads, steps):
    chips, rows, depth = xs[0].shape
    units = grads[0].shape[2]
    width = depth // steps

    def kernel(*refs):
        terms = [
            product_over_rows(
                refs[n][...].reshape(chips * rows, width),
                refs[2 + n][...].reshape(chips * rows, units),
            )
            for n in range(2)
        ]
        refs[4][...] = (terms[0] + terms[1]).astype(low_type)

    return call_kernel(
        kernel,
        [*xs, *grads],
        [pl.BlockSpec((chips, rows, width), lambda i: (0, 0, i))] * 2
        + [resident(grads[0].shape)] * 2,
        [(pl.BlockSpec((width, units), lambda i: (i, 0)), ((depth, units), low_type))],
        0,
        "weight_gradient",
        grid=(steps,),
    )[0]


def down_gradients(acts, grads, steps):
    chips, rows, units = acts[0].shape
    depth = grads[0].shape[1]
    width = depth // steps
    count = len(grads)

    def kernel(*refs):
        act_refs, outs, (own, sems) = refs[count : count + 2], refs[count + 2 : -2], refs[-2:]
        step = pl.program_id(0)

        @pl.when(step == 0)
        def _():
            for copy in piece_copies(piece_rows(chips, rows, count), refs[:count], own, sems):
                copy.start()
            for i in range(chips):
                block = own.at[pl.ds(i * rows, rows)]
                pltpu.make_async_copy(block, block, sems.at[i]).wait()

        right = own[:, pl.ds(pl.multiple_of(step * width, width), width)]
        for act, out in zip(act_refs, outs, strict=True):
            out[...] = product_over_rows(act[...].reshape(chips * rows, units), right).astype(
                low_type
            )

    out = (pl.BlockSpec((units, width), lambda i: (0, i)), ((units, depth), low_type))
    return call_kernel(
        kernel,
        [*grads, *acts],
        [in_place] * count + [resident(acts[0].shape)] * 2,
        [out] * 2,
        0,
        "down_gradients",
        grid=(steps,),
        scratch=token_scratch(chips, rows, depth),
    )


def plane_place():
    rep = lax.axis_index("rep")
    return jnp.stack([rep // 2, rep % 2]).astype(jnp.int32)


def both_cores(pieces):
    return pieces + [swap(stacked(pieces), 1)]


def plane_scratch(chips, rows, width):
    return [
        pltpu.VMEM((2, chips * rows, width), low_type),
        pltpu.SemaphoreType.DMA((2, chips)),
    ]


def load_plane(chips, rows, refs, target, sems):
    @pl.when(pl.program_id(0) == 0)
    def _():
        copies = piece_copies(
            piece_rows(chips, rows, len(refs) - 1), refs[:-1], target.at[0], sems.at[0]
        )
        copies.append(pltpu.make_async_copy(refs[-1], target.at[1], sems.at[1, 0]))
        for copy in copies:
            copy.start()
        for i in range(chips):
            block = target.at[0, pl.ds(i * rows, rows)]
            pltpu.make_async_copy(block, block, sems.at[0, i]).wait()
        pltpu.make_async_copy(target.at[1], target.at[1], sems.at[1, 0]).wait()


def whole_columns(pieces, share):
    size, chips = lax.axis_size("shard"), lax.axis_size("rep") // 2
    rows, width = pieces[0].shape
    step_rows = rows // 4

    def kernel(at, *refs):
        out, target, sems = refs[-3:]
        load_plane(chips, rows, refs[:-3], target, sems)
        step = pl.program_id(0)
        for j in range(2 * chips):
            start = (at[0] ^ (j // 2)) * rows + step * step_rows
            own = target[at[1] ^ (j % 2), pl.ds(pl.multiple_of(start, 16), step_rows), :]
            own = own.astype(jnp.float32)
            for z in range(size):
                first = (z * 2 * chips + j) * share
                out[:, first : first + share] = own[:, z * width // size :][:, :share]

    wide = 2 * chips * size * share
    return call_kernel(
        kernel,
        [plane_place(), *pieces],
        [in_place] * len(pieces),
        [(pl.BlockSpec((step_rows, wide), lambda i, at: (i, 0)), ((rows, wide), jnp.float32))],
        8,
        "whole_columns",
        grid=(4,),
        prefetch=1,
        scratch=plane_scratch(chips, rows, width),
    )[0]


def whole_rows(pieces, share):
    chips = lax.axis_size("rep") // 2
    rows, width = pieces[0].shape

    def kernel(at, *refs):
        out, target, sems = refs[-3:]
        load_plane(chips, rows, refs[:-3], target, sems)
        j = pl.program_id(0)
        start = pl.multiple_of((at[0] ^ (j // 2)) * rows, 32)
        own = target[at[1] ^ (j % 2), pl.ds(start, rows), :].astype(jnp.float32)
        out[0] = own[:share]

    shape = (2 * chips, share, width)
    return call_kernel(
        kernel,
        [plane_place(), *pieces],
        [in_place] * len(pieces),
        [(pl.BlockSpec((1, share, width), lambda j, at: (j, 0, 0)), (shape, jnp.float32))],
        8,
        "whole_rows",
        grid=(2 * chips,),
        prefetch=1,
        scratch=plane_scratch(chips, rows, width),
    )[0].reshape(2 * chips * share, width)


def rows_of(values, width):
    rows = -(-values.shape[0] // width)
    block = jnp.pad(values, (0, rows * width - values.shape[0])).reshape(rows, width)
    return jnp.pad(block, ((0, -rows % 16), (0, 0)))


def in_shard_order(parts):
    size, here = lax.axis_size("shard"), lax.axis_index("shard")
    twice = jnp.concatenate(parts + parts)
    run = parts[0].shape[0]
    return lax.dynamic_slice_in_dim(twice, (size - here) * run, size * run, 0)


def padded(share):
    return -(-share // 32) * 32


def own_columns(weight):
    size, reps = lax.axis_size("shard"), lax.axis_size("rep")
    run = weight.shape[1] // size
    share = run // reps
    rep = lax.axis_index("rep")
    none = jnp.zeros((weight.shape[0], padded(share) - share), weight.dtype)
    parts = []
    for z in range(size):
        parts += [lax.dynamic_slice_in_dim(weight, z * run + rep * share, share, 1), none]
    return jnp.concatenate(parts, axis=1)


def own_rows(weight):
    share = weight.shape[0] // lax.axis_size("rep")
    own = lax.dynamic_slice_in_dim(weight, lax.axis_index("rep") * share, share, 0)
    return jnp.pad(own, ((0, padded(share) - share), (0, 0)))


def scatter_group(partial):
    return lax.psum_scatter(partial, "shard", scatter_dimension=0, tiled=True)


def local(
    tokens,
    norm_gains,
    w_query,
    w_key,
    w_value,
    w_out,
    w_gate,
    w_up,
    w_down,
    seq_lengths,
    seq_device,
    cotangent,
):
    row_total = tokens.shape[0]
    size, reps = lax.axis_size("shard"), lax.axis_size("rep")
    chips = reps // 2
    rep = lax.axis_index("rep")
    device = rep * size + lax.axis_index("shard")
    query_width, key_width = HEADS * HEAD, KV_HEADS * HEAD

    w_joint = jnp.concatenate([w_query, w_key, w_value], axis=1)
    joint, outer = Tiles(w_joint), Tiles(w_out)
    joint_tile = jnp.concatenate([joint.own(w_joint), rows_of(norm_gains, joint.width)], axis=0)
    joint_slots = [from_ahead(joint_tile, k) for k in range(1, size)]
    gated_own = jnp.concatenate([own_columns(w_gate), own_columns(w_up)], axis=1)
    live, segment, position = layout(seq_lengths, seq_device, device, row_total)
    cotangent_live = jnp.where(live[:, None], cotangent, jnp.zeros_like(cotangent))
    gated_own, down_own, joint_slots, out_tile = fence(
        gated_own, own_rows(w_down), joint_slots, outer.own(w_out)
    )
    gather_shards = lambda own: lax.all_gather(own, "shard", axis=0, tiled=True)
    gated_w, down_w = gather_shards(gated_own), gather_shards(down_own)
    joint_tiles = jnp.concatenate([slot[: joint.part] for slot in joint_slots], axis=0)
    joint_near = near_groups(joint_tiles, joint.members)
    out_slots = [from_ahead(out_tile, k) for k in range(1, size)]
    gains = in_shard_order(
        [norm_gains]
        + [slot[joint.part :].reshape(-1)[: norm_gains.shape[0]] for slot in joint_slots]
    )
    joint_near, out_slots, gains = fence(joint_near, out_slots, gains)
    out_tiles = jnp.concatenate(out_slots, axis=0)
    joint_far = far_group(joint_near, joint.members)
    if joint_far:
        joint_far = [jnp.concatenate(joint_far, axis=0)]
    joint_pieces = joint.across([joint_tiles] + joint_near + joint_far)

    cosine, sine = rotary_tables(position, HEAD)
    gains = gains.astype(jnp.float32)[None]
    gain_in = gains[:, :D]
    gain_ff = gains[:, D + 2 * HEAD :]
    shared = (
        gains[:, D : D + HEAD],
        gains[:, D + HEAD : D + 2 * HEAD],
        jnp.concatenate([cosine, cosine], axis=1),
        jnp.concatenate([0.0 - sine, sine], axis=1),
        segment[:, None],
        segment[None, :],
    )
    joint_pieces, shared, out_tiles = fence(joint_pieces, shared, out_tiles)
    out_groups = all_groups(out_tiles, outer.members)
    joint_proj, normed_in = attention_input(joint, tokens, gain_in, w_joint, joint_pieces)

    joint_proj, normed_in = fence(joint_proj, normed_in)
    half_steps = KV_HEADS // 4
    attended_early, inverse_early = attend(joint_proj, shared, 0, half_steps)

    joint_proj, attended_early, out_groups, normed_in = fence(
        joint_proj, attended_early, out_groups, normed_in
    )
    out_pieces = outer.across(out_groups)
    normed_near = near_groups(normed_in, joint.members)
    attended_late, inverse_late = attend(joint_proj, shared, half_steps, half_steps)
    attended = jnp.concatenate([attended_early, attended_late], axis=1)

    attended, out_pieces = fence(attended, out_pieces)
    hidden, normed_ff = attention_output(outer, attended, tokens, gain_ff, w_out, out_pieces)

    normed_ff, normed_near = fence(normed_ff, normed_near)
    ff_near = near_groups(normed_ff, 2)

    ff_near, gated_w = fence(ff_near, gated_w)
    ff_far = far_group(ff_near, 2)
    half = gated_w.shape[0] // 2
    halves = (gated_w[:half], gated_w[half:])
    ff_far, gated_w, halves, cotangent_live, normed_near = fence(
        ff_far, gated_w, halves, cotangent_live, normed_near
    )
    ff_tokens = [normed_ff] + ff_near + ff_far
    gated_ws = ([gated_w], [swap(part, 1) for part in halves])
    grad_mixed = all_groups(cotangent_live, 2)
    *ours, group_tokens = gated_forward(ff_tokens, gated_ws[0], True)

    ours, gated_ws, group_tokens, attended = fence(ours, gated_ws, group_tokens, attended)
    theirs = gated_forward(ff_tokens, gated_ws[1], False)

    theirs, grad_mixed, normed_near = fence(theirs, grad_mixed, normed_near)
    normed_far = far_group(normed_near, joint.members)
    normed_rows = [normed_in] + normed_near + normed_far
    grad_downs = down_gradients((ours[0], theirs[0]), grad_mixed, 2)

    grad_downs, down_w, normed_rows = fence(grad_downs, down_w, normed_rows)
    down_ws = (down_w, swap(down_w, 1))
    other_down = swap(grad_downs[1], 1)

    down_ws, ours, theirs, attended, group_tokens = fence(
        down_ws, ours, theirs, attended, group_tokens
    )
    attended_near = near_groups(attended, outer.members)
    all_tokens = (group_tokens, swap(group_tokens, 1))
    down_parts = down_forward((ours[0], theirs[0]), down_ws)

    down_parts, other_down, all_tokens, attended_near = fence(
        down_parts, other_down, all_tokens, attended_near
    )
    attended_far = far_group(attended_near, outer.members)
    attended_rows = [attended] + attended_near + attended_far
    down_terms = sum_terms(down_parts, 2)
    grad_down = grad_downs[0].astype(jnp.float32) + other_down.astype(jnp.float32)
    grad_down = scatter_group(grad_down.astype(low_type))
    our_grads, their_grads, grad_x = gated_backward(
        grad_mixed, (ours[1:], theirs[1:]), down_ws, gated_ws
    )

    grad_x, our_grads, their_grads, attended_rows, down_terms = fence(
        grad_x, our_grads, their_grads, attended_rows, down_terms
    )
    grad_x_far = far_terms(grad_x, 2)
    their_grads = [swap(part, 1) for part in their_grads]
    grad_gate = weight_gradient(all_tokens, (our_grads[0], their_grads[0]), 4)

    grad_x_far, grad_gate, their_grads, down_terms = fence(
        grad_x_far, grad_gate, their_grads, down_terms
    )
    grad_terms = near_terms(grad_x, grad_x_far, 2)
    grad_gate = scatter_group(grad_gate)
    grad_up = weight_gradient(all_tokens, (our_grads[1], their_grads[1]), 4)

    grad_terms, grad_up, grad_down = fence(grad_terms, grad_up, grad_down)
    down_near = near_groups(grad_down, 2)
    grad_up = scatter_group(grad_up)
    grad_hidden, grad_gain_ff, grad_attended, *cuts = attention_output_gradient(
        outer, grad_terms, cotangent_live, hidden, gain_ff, w_out, out_pieces
    )

    cuts, grad_attended, down_near = fence(cuts, grad_attended, down_near)
    down_far = far_group(down_near, 2)
    out_runs = outer.group_columns(cuts)
    half_steps = KV_HEADS // 4
    early = attend_gradient(
        joint_proj, attended, inverse_early, grad_attended, shared, 0, half_steps
    )

    early, out_runs, down_far, grad_gate, grad_attended = fence(
        early, out_runs, down_far, grad_gate, grad_attended
    )
    gate_near = near_groups(grad_gate, 2)
    late = attend_gradient(
        joint_proj, attended, inverse_late, grad_attended, shared, half_steps, half_steps
    )

    early, late, gate_near = fence(early, late, gate_near)
    head_gains = early[3] + late[3]
    parts = [part for n in range(3) for part in (early[n], late[n])]
    grad_joint_low = jnp.concatenate(parts, axis=1)
    cuts, grad_joint_low = fence(joint.cut_columns(grad_joint_low), grad_joint_low)
    joint_runs = joint.group_columns(cuts)
    down_pieces = both_cores([grad_down] + down_near + down_far)
    grad_tokens, grad_gain_in = attention_input_gradient(
        joint, grad_joint_low, grad_hidden, tokens, gain_in, w_joint, joint_pieces
    )

    joint_runs, grad_gain_in, out_runs, down_pieces, gate_near = fence(
        joint_runs, grad_gain_in, out_runs, down_pieces, gate_near
    )
    gate_far = far_group(gate_near, 2)
    sums = outer.tile(attended_rows, out_runs)
    sums = joint.tile(normed_rows, joint_runs, sums)
    grad_gains = jnp.concatenate(
        [grad_gain_in, head_gains[0:1], head_gains[1:2], grad_gain_ff], axis=1
    )[0]
    extra = joint.extra_rows(grad_gains, sums[0].shape[1])

    sums, extra, gate_far = fence(sums, extra, gate_far)
    sums = sums[:1] + tuple(swap(part, h) for h, part in enumerate(sums) if h)
    gate_pieces = both_cores([grad_gate] + gate_near + gate_far)

    sums, down_pieces, gate_pieces, down_terms = fence(sums, down_pieces, gate_pieces, down_terms)
    own, sent = joint.send(sums, extra)
    up_near = near_groups(grad_up, 2)
    whole_down = whole_rows(down_pieces, w_down.shape[0] // reps)
    whole_gate = whole_columns(gate_pieces, w_down.shape[0] // reps)

    mixed_full = hidden
    for term in down_terms:
        mixed_full = mixed_full + term.astype(jnp.float32)
    mixed = jnp.where(live[:, None], mixed_full, jnp.zeros_like(mixed_full)).astype(jnp.bfloat16)

    own, sent, whole_down, whole_gate, up_near, mixed = fence(
        own, sent, whole_down, whole_gate, up_near, mixed
    )
    total = own
    for part in sent:
        total = total + part.astype(jnp.float32)
    total_groups = all_groups(total.astype(low_type), joint.members)
    up_far = far_group(up_near, 2)

    total_groups, up_far = fence(total_groups, up_far)
    whole_pieces = joint.across_stacked(total_groups)
    up_pieces = both_cores(after([grad_up] + up_near + up_far, *whole_pieces[joint.groups :]))
    *grad_joint, grad_out_w, beneath = joint.whole(
        whole_pieces, ((query_width, key_width, key_width), (D,))
    )
    grad_gains = beneath.reshape(-1)[: norm_gains.shape[0]]
    share = w_down.shape[0] // reps
    return (
        mixed,
        grad_tokens,
        grad_gains,
        *grad_joint,
        grad_out_w,
        whole_gate,
        whole_columns(up_pieces, share),
        whole_down,
    )


def solution(mesh):
    return jax.shard_map(
        local,
        mesh=mesh,
        in_specs=(
            P(("rep", "shard"), None),
            P("shard"),
            P("shard", None),
            P("shard", None),
            P("shard", None),
            P("shard", None),
            P("shard", None),
            P("shard", None),
            P("shard", None),
            P(),
            P(),
            P(("rep", "shard"), None),
        ),
        out_specs=(
            P(("rep", "shard"), None),
            P(("rep", "shard"), None),
            P("shard"),
            P("shard", None),
            P("shard", None),
            P("shard", None),
            P("shard", None),
            P("shard", None),
            P("shard", None),
            P("shard", None),
        ),
        check_vma=False,
    )
```

```python
import math

import jax
import jax.numpy as jnp
from jax import lax
from jax.experimental import pallas as pl
from jax.experimental.pallas import tpu as pltpu
from jax.sharding import PartitionSpec as P

D = 1536
HEADS = 24
KV_HEADS = 8
HEAD = 64
FF = 6912


epsilon = 1e-05
rope_base = 1000000.0
masked_score = -1e30


def plain_product(left, right):
    return jnp.dot(left, right, preferred_element_type=jnp.float32)


def product_over_rows(left, right):
    return lax.dot_general(
        left, right, (((0,), (0,)), ((), ())), preferred_element_type=jnp.float32
    )


def product_with_transpose(left, right):
    return lax.dot_general(
        left, right, (((1,), (1,)), ((), ())), preferred_element_type=jnp.float32
    )


def rotary_tables(position, head_width):
    half_width = head_width // 2
    index = jnp.arange(half_width).astype(jnp.float32)
    inverse = jnp.exp(index * (-2.0 * math.log(rope_base) / head_width))
    angle = position.astype(jnp.float32)[:, None] * inverse[None, :]
    return (jnp.cos(angle), jnp.sin(angle))


def layout(seq_lengths, seq_device, device, row_total):
    own_length = jnp.where(seq_device == device, seq_lengths, 0)
    ends = jnp.cumsum(own_length, dtype=jnp.int32)
    begins = ends - own_length
    slot_index = jnp.arange(row_total, dtype=jnp.int32)
    inside = (slot_index[:, None] >= begins[None, :]) & (slot_index[:, None] < ends[None, :])
    live = jnp.any(inside, axis=1)
    seq_total = seq_lengths.shape[0]
    numbers = jnp.arange(seq_total, dtype=jnp.int32)
    found = jnp.sum(jnp.where(inside, numbers[None, :], 0), axis=1, dtype=jnp.int32)
    segment = jnp.where(live, found, seq_total + slot_index)
    offset = jnp.sum(jnp.where(inside, (0 - begins)[None, :], 0), axis=1, dtype=jnp.int32)
    position = jnp.where(live, slot_index + offset, 0)
    return (live, segment, position)


vmem_bytes = 60 * 2**20
low_type = jnp.bfloat16
in_place = pl.BlockSpec(memory_space=pl.ANY)


def swap(values, offset):
    size = lax.axis_size("rep")
    return lax.ppermute(values, "rep", [(i, i ^ offset) for i in range(size)])


def from_ahead(values, steps):
    size = lax.axis_size("shard")
    return lax.ppermute(values, "shard", [((i + steps) % size, i) for i in range(size)])


def from_behind(values, steps):
    size = lax.axis_size("shard")
    return lax.ppermute(values, "shard", [(i, (i + steps) % size) for i in range(size)])


def fence(*values):
    return lax.optimization_barrier(values)


def after(values, *others):
    return lax.optimization_barrier((values, others))[0]


def all_groups(block, unit):
    return [block] + [swap(block, unit * d) for d in range(1, lax.axis_size("rep") // unit)]


def sum_terms(blocks, unit):
    return [swap(block, unit * d) if d else block for d, block in enumerate(blocks)]


def near_groups(block, unit):
    groups = lax.axis_size("rep") // unit
    return [swap(block, unit * d) for d in range(1, groups if groups != 4 else 3)]


def far_group(near, unit):
    if lax.axis_size("rep") // unit != 4:
        return []
    half = half_rows(near[0].shape[0])
    return [swap(near[1][:half], unit), swap(near[0][half:], 2 * unit)]


def far_terms(blocks, unit):
    return [swap(blocks[3][0], unit), swap(blocks[3][1], 2 * unit)] if len(blocks) == 4 else []


def near_terms(blocks, far, unit):
    if not far:
        return [swap(block[0], unit * d) if d else block[0] for d, block in enumerate(blocks)]
    half = blocks[3][0].shape[0]
    one, two = blocks[1][0], blocks[2][0]
    add = lambda left, right: (left.astype(jnp.float32) + right.astype(jnp.float32)).astype(low_type)
    one = jnp.concatenate([one[:half], add(one[half:], far[1])], axis=0)
    two = jnp.concatenate([add(two[:half], far[0]), two[half:]], axis=0)
    return [blocks[0][0], swap(one, unit), swap(two, 2 * unit)]


def half_rows(rows):
    return rows // 2 // 16 * 16


def piece_rows(groups, rows, count):
    half = half_rows(rows)
    return [[rows]] * groups if count == groups else [[rows]] * 3 + [[half, rows - half]]


def piece_copies(rows, refs, target, sems):
    copies, at, n = [], 0, 0
    for i, group in enumerate(rows):
        for count in group:
            copies.append(
                pltpu.make_async_copy(refs[n], target.at[pl.ds(at, count)], sems.at[i])
            )
            at += count
            n += 1
    return copies


def call_kernel(kernel, args, ins, outs, micros, name, grid=None, prefetch=0, scratch=()):
    return pl.pallas_call(
        kernel,
        grid_spec=pltpu.PrefetchScalarGridSpec(
            num_scalar_prefetch=prefetch,
            grid=grid or (1,),
            in_specs=ins,
            out_specs=[spec for spec, _ in outs],
            scratch_shapes=list(scratch),
        ),
        out_shape=[jax.ShapeDtypeStruct(*shape) for _, shape in outs],
        compiler_params=pltpu.CompilerParams(vmem_limit_bytes=vmem_bytes),
        cost_estimate=pl.CostEstimate(flops=int(micros * 1.15e9), bytes_accessed=0, transcendentals=0),
        name=name,
    )(*args)


def resident(shape):
    return pl.BlockSpec(shape, lambda *_: (0,) * len(shape), pipeline_mode=pl.Buffered(1))


def spread(values, shards, members):
    part = values.shape[1] // shards // members
    return [
        jnp.concatenate(
            [values[:, (z * members + p) * part :][:, :part] for z in range(shards)], axis=1
        )
        for p in range(members)
    ]


def unspread(parts, shards):
    part = parts[0].shape[1] // shards
    return jnp.concatenate(
        [run[:, z * part : (z + 1) * part] for z in range(shards) for run in parts], axis=1
    )


def norm_factor(values):
    return lax.rsqrt(jnp.mean(values * values, axis=-1, keepdims=True) + epsilon)


def norm_gradient(values, gain, grad):
    factor = norm_factor(values)
    scaled = grad * gain
    mean = jnp.mean(scaled * values, axis=-1, keepdims=True)
    by_gain = jnp.sum(grad * values * factor, axis=0, keepdims=True)
    return factor * scaled - values * (factor * factor * factor * mean), by_gain


def stacked(pieces):
    rows = sum(piece.shape[0] for piece in pieces)

    def kernel(*refs):
        copies, start = [], 0
        for n, piece in enumerate(pieces):
            target = refs[len(pieces)].at[pl.ds(start, piece.shape[0])]
            copies.append(pltpu.make_async_copy(refs[n], target, refs[-1].at[n]))
            start += piece.shape[0]
        for copy in copies:
            copy.start()
        for copy in copies:
            copy.wait()

    shape = (rows, pieces[0].shape[1])
    return call_kernel(
        kernel,
        pieces,
        [in_place] * len(pieces),
        [(resident(shape), (shape, low_type))],
        0,
        "stacked",
        scratch=[pltpu.SemaphoreType.DMA((len(pieces),))],
    )[0]


class Tiles:
    def __init__(self, weight):
        reps = lax.axis_size("rep")
        groups = reps // 2
        while weight.shape[1] % (128 * groups):
            groups //= 2
        self.groups, self.members = groups, reps // groups
        self.shards, self.here = lax.axis_size("shard"), lax.axis_index("shard")
        self.group = lax.axis_index("rep") // self.members
        self.member = lax.axis_index("rep") % self.members
        self.rows = weight.shape[0]
        self.part = self.rows // self.members
        self.rest = (self.shards - 1) * self.part
        self.depth = self.shards * self.part
        self.width = weight.shape[1] // groups

    def own(self, weight):
        return lax.dynamic_slice(
            weight, (self.member * self.part, self.group * self.width), (self.part, self.width)
        )

    def across(self, pieces):
        return pieces + [swap(piece, h) for h in range(1, self.members) for piece in pieces]

    def across_stacked(self, pieces):
        stack = stacked(pieces)
        return pieces + [swap(stack, h) for h in range(1, self.members)]

    def place(self):
        return jnp.stack([self.group, self.member, self.here]).astype(jnp.int32)

    def scratch(self):
        shape = (self.members, self.groups)
        return [
            pltpu.VMEM(shape + (self.depth, self.width), low_type),
            pltpu.SemaphoreType.DMA(shape),
        ]

    def load(self, at, weight_ref, refs, tiles, sems):
        part, shards, groups = self.part, self.shards, self.groups

        def to(h, d, z, start, size):
            first = pl.multiple_of(lax.rem(at[2] + z, shards) * part, 16) + start
            return tiles.at[h, d, pl.ds(pl.multiple_of(first, 16), size)]

        for d in range(groups):
            for h in range(self.members):
                source = weight_ref.at[
                    pl.ds(pl.multiple_of((at[1] ^ h) * part, 16), part),
                    pl.ds(pl.multiple_of((at[0] ^ d) * self.width, 128), self.width),
                ]
                pltpu.make_async_copy(source, to(h, d, 0, 0, part), sems.at[h, d]).start()
                for k in range(shards - 1):
                    pltpu.make_async_copy(
                        refs[h * groups + d].at[pl.ds(k * part, part)],
                        to(h, d, k + 1, 0, part),
                        sems.at[h, d],
                    ).start()

        def wait(h, d):
            pltpu.make_async_copy(tiles.at[h, d], tiles.at[h, d], sems.at[h, d]).wait()
            return tiles[h, d]

        return wait

    def columns(self, at, d):
        return pl.ds(pl.multiple_of((at[0] ^ d) * self.width, 128), self.width)

    def multiply(self, at, wait, x, out):
        for d in range(self.groups):
            total = None
            for h in range(self.members):
                term = plain_product(x[at[1] ^ h], wait(h, d))
                total = term if total is None else total + term
            out[:, self.columns(at, d)] = total

    def multiply_transposed(self, at, wait, grad, out):
        totals = [None] * self.members
        for d in range(self.groups):
            block = grad[:, self.columns(at, d)]
            for h in range(self.members):
                term = product_with_transpose(block, wait(h, d))
                totals[h] = term if totals[h] is None else totals[h] + term
        for h in range(self.members):
            out[at[1] ^ h] = totals[h]

    def call(self, kernel, args, weight, pieces, outs, micros, name, scratch=()):
        given, produced = len(args), len(outs)

        def whole_kernel(at, *refs):
            ins, weight_ref = refs[:given], refs[given]
            rest = refs[given + 1 + len(pieces) :]
            wait = self.load(
                at, weight_ref, refs[given + 1 : given + 1 + len(pieces)], *rest[produced : produced + 2]
            )
            kernel(at, ins, rest[:produced], rest[produced + 2 :], wait)

        return call_kernel(
            whole_kernel,
            [self.place(), *args, weight, *pieces],
            [resident(arg.shape) for arg in args] + [in_place] * (1 + len(pieces)),
            [(resident(shape), (shape, kind)) for shape, kind in outs],
            micros,
            name,
            prefetch=1,
            scratch=self.scratch() + list(scratch),
        )

    def cut_columns(self, grad):
        return [
            lax.dynamic_slice_in_dim(grad, (self.group ^ d) * self.width, self.width, 1)
            for d in range(self.groups)
        ]

    def group_columns(self, cuts):
        return [swap(cut, self.members * d) if d else cut for d, cut in enumerate(cuts)]

    def tile(self, rows, columns, beside=()):
        tokens, members, shards, part = columns[0].shape[0], self.members, self.shards, self.part
        count, total = len(rows), len(columns) * tokens
        sizes = [piece.shape[0] for piece in rows]
        wide = self.width + (beside[0].shape[1] if beside else 0)

        def kernel(at, *refs):
            besides = refs[count + len(columns) : count + len(columns) + len(beside)]
            outs = refs[count + len(columns) + len(beside) : -4]
            left, right, whole, sems = refs[-4:]
            copies = piece_copies([sizes], refs[:count], left, sems.at[pl.ds(0, 1)])
            copies += piece_copies(
                [[tokens] * len(columns)], refs[count : count + len(columns)], right, sems.at[pl.ds(1, 1)]
            )
            for copy in copies:
                copy.start()
            pltpu.make_async_copy(left, left, sems.at[0]).wait()
            pltpu.make_async_copy(right, right, sems.at[1]).wait()
            whole[...] = product_over_rows(left[...], right[...])
            for h in range(members):
                for k in range(shards):
                    start = lax.rem(at[2] + k, shards) * self.rows + (at[1] ^ h) * part
                    block = whole[pl.ds(pl.multiple_of(start, 16), part), :]
                    outs[h][k * part : (k + 1) * part, : self.width] = block.astype(outs[h].dtype)
                if beside:
                    outs[h][:, self.width :] = besides[h][...]

        shape = (shards * part, wide)
        return call_kernel(
            kernel,
            [self.place(), *rows, *columns, *beside],
            [in_place] * (count + len(columns)) + [resident(part.shape) for part in beside],
            [(resident(shape), (shape, low_type if h else jnp.float32)) for h in range(members)],
            7,
            "weight_tile",
            prefetch=1,
            scratch=[
                pltpu.VMEM((total, members * self.depth), low_type),
                pltpu.VMEM((total, self.width), low_type),
                pltpu.VMEM((members * self.depth, self.width), jnp.float32),
                pltpu.SemaphoreType.DMA((2,)),
            ],
        )

    def send(self, tiles, extra):
        total = tiles[0]
        for tile in tiles[1:]:
            total = total + tile.astype(jnp.float32)
        parts = [
            jnp.concatenate([total[k * self.part : (k + 1) * self.part], extra[k]], axis=0)
            for k in range(self.shards)
        ]
        return parts[0], [
            from_behind(parts[k].astype(low_type), k) for k in range(1, self.shards)
        ]

    def extra_rows(self, values, width):
        run = values.shape[0] // self.shards
        rows = -(-run // width)
        block = jnp.pad(values.reshape(self.shards, run), ((0, 0), (0, rows * width - run)))
        block = block.reshape(self.shards, rows, width)
        block = jnp.pad(block, ((0, 0), (0, -rows % 16), (0, 0)))
        twice = jnp.concatenate([block, block], axis=0)
        return lax.dynamic_slice_in_dim(twice, self.here, self.shards, 0)

    def whole(self, pieces, sections):
        members, groups, part = self.members, self.groups, self.part
        rows, wide = pieces[0].shape
        beneath = rows - part

        def kernel(at, *refs):
            outs, (tiles, sems) = refs[len(pieces) : -2], refs[-2:]
            for h in range(members):
                for d in range(groups):
                    ref = refs[groups + h - 1].at[pl.ds(d * rows, rows)] if h else refs[d]
                    pltpu.make_async_copy(ref, tiles.at[h, d], sems.at[h, d]).start()
            for h in range(members):
                for d in range(groups):
                    pltpu.make_async_copy(tiles.at[h, d], tiles.at[h, d], sems.at[h, d]).wait()
            total = None
            for g in range(groups):
                for p in range(members):
                    block = tiles[at[1] ^ p, at[0] ^ g].astype(jnp.float32)
                    total = block[part:] if total is None else total + block[part:]
                    n, left = 0, 0
                    for widths in sections:
                        width = sum(widths) // groups
                        first = 0
                        for run in widths:
                            low, high = max(first, g * width), min(first + run, (g + 1) * width)
                            if low < high:
                                outs[n][p * part : (p + 1) * part, low - first : high - first] = (
                                    block[:part, left + low - g * width : left + high - g * width]
                                )
                            first += run
                            n += 1
                        left += width
            outs[-1][...] = total

        shapes = [(self.rows, run) for widths in sections for run in widths] + [(beneath, wide)]
        return call_kernel(
            kernel,
            [self.place(), *pieces],
            [in_place] * len(pieces),
            [(resident(shape), (shape, jnp.float32)) for shape in shapes],
            6,
            "whole_tiles",
            prefetch=1,
            scratch=[
                pltpu.VMEM((members, groups, rows, wide), low_type),
                pltpu.SemaphoreType.DMA((members, groups)),
            ],
        )


def attention_input(tiles, tokens, gain, weight, pieces):
    def kernel(at, ins, outs, scratch, wait):
        x = ins[0][...].astype(jnp.float32)
        normed = (x * norm_factor(x) * ins[1][...]).astype(low_type)
        outs[1][...] = normed
        for p, run in enumerate(spread(normed, tiles.shards, tiles.members)):
            scratch[0][p] = run
        tiles.multiply(at, wait, scratch[0], outs[0])

    rows = tokens.shape[0]
    return tiles.call(
        kernel,
        [tokens, gain],
        weight,
        pieces,
        [
            ((rows, weight.shape[1]), jnp.float32),
            (tokens.shape, low_type),
        ],
        0,
        "attention_input",
        scratch=[pltpu.VMEM((tiles.members, rows, tiles.depth), low_type)],
    )


def attention_output(tiles, attended, tokens, gain, weight, pieces):
    def kernel(at, ins, outs, scratch, wait):
        for p, run in enumerate(spread(ins[0][...], tiles.shards, tiles.members)):
            scratch[0][p] = run
        tiles.multiply(at, wait, scratch[0], outs[0])
        hidden = outs[0][...] + ins[1][...].astype(jnp.float32)
        outs[0][...] = hidden
        outs[1][...] = (hidden * norm_factor(hidden) * ins[2][...]).astype(low_type)

    rows, depth = tokens.shape
    return tiles.call(
        kernel,
        [attended, tokens, gain],
        weight,
        pieces,
        [
            ((rows, depth), jnp.float32),
            ((rows, depth), low_type),
        ],
        0,
        "attention_output",
        scratch=[pltpu.VMEM((tiles.members, rows, tiles.depth), low_type)],
    )


def attention_output_gradient(tiles, terms, grad, hidden, gain, weight, pieces):
    count = len(terms)

    def kernel(at, ins, outs, scratch, wait):
        total = ins[0][...].astype(jnp.float32)
        for term in ins[1:count]:
            total = total + term[...].astype(jnp.float32)
        by_hidden, by_gain = norm_gradient(ins[count + 1][...], ins[count + 2][...], total)
        by_hidden = by_hidden + ins[count][...].astype(jnp.float32)
        outs[0][...] = by_hidden
        low = scratch[1]
        low[...] = by_hidden.astype(low_type)
        outs[1][...] = by_gain
        for d in range(tiles.groups):
            outs[3 + d][...] = low[:, tiles.columns(at, d)]
        tiles.multiply_transposed(at, wait, low, scratch[0])
        runs = [scratch[0][p].astype(low_type) for p in range(tiles.members)]
        outs[2][...] = unspread(runs, tiles.shards)

    rows, depth = grad.shape
    return tiles.call(
        kernel,
        [*terms, grad, hidden, gain],
        weight,
        pieces,
        [
            ((rows, depth), jnp.float32),
            ((1, depth), jnp.float32),
            ((rows, depth), low_type),
        ]
        + [((rows, tiles.width), low_type)] * tiles.groups,
        0,
        "attention_output_gradient",
        scratch=[
            pltpu.VMEM((tiles.members, rows, tiles.depth), jnp.float32),
            pltpu.VMEM((rows, depth), low_type),
        ],
    )


def attention_input_gradient(tiles, grad, grad_hidden, tokens, gain, weight, pieces):
    def kernel(at, ins, outs, scratch, wait):
        tiles.multiply_transposed(at, wait, ins[0], scratch[0])
        total = unspread([scratch[0][p] for p in range(tiles.members)], tiles.shards)
        by_tokens, by_gain = norm_gradient(
            ins[2][...].astype(jnp.float32), ins[3][...], total
        )
        outs[0][...] = ins[1][...] + by_tokens
        outs[1][...] = by_gain

    rows, depth = tokens.shape
    return tiles.call(
        kernel,
        [grad, grad_hidden, tokens, gain],
        weight,
        pieces,
        [((rows, depth), jnp.float32), ((1, depth), jnp.float32)],
        10,
        "attention_input_gradient",
        scratch=[pltpu.VMEM((tiles.members, rows, tiles.depth), jnp.float32)],
    )


def turn(values):
    half = values.shape[1] // 2
    return jnp.concatenate([values[:, half:], values[:, :half]], axis=1)


def head_of(block, n):
    return block[:, n * HEAD : (n + 1) * HEAD]


def rotated_head(values, gain, cosine, sine):
    normed = values * norm_factor(values) * gain
    return (normed * cosine + turn(normed) * sine).astype(low_type)


def head_gradient(values, gain, cosine, sine, grad):
    return norm_gradient(values, gain, grad * cosine - turn(grad) * sine)


def chunk_of(row_total):
    return min(row_total, 128)


def allowed_scores(rows, columns, start, chunk):
    end = start + chunk
    later = start + lax.broadcasted_iota(jnp.int32, (chunk, end), 0)
    earlier = lax.broadcasted_iota(jnp.int32, (chunk, end), 1)
    return (rows[start:end] == columns[:, :end]) & (later >= earlier)


def head_weights(query, key, allowed):
    scores = product_with_transpose(query, key) * HEAD ** (-0.5)
    return jnp.where(allowed, jnp.exp(scores), 0.0)


def head_specs(row_total, first_step=0):
    pair = 2 * HEADS // KV_HEADS * HEAD
    first_key, first_value = HEADS * HEAD // (2 * HEAD), (HEADS + KV_HEADS) * HEAD // (2 * HEAD)
    blocks = [
        pl.BlockSpec((row_total, pair), lambda i: (0, first_step + i)),
        pl.BlockSpec((row_total, 2 * HEAD), lambda i: (0, first_key + first_step + i)),
        pl.BlockSpec((row_total, 2 * HEAD), lambda i: (0, first_value + first_step + i)),
    ]
    shared = [(1, HEAD), (1, HEAD), (row_total, HEAD), (row_total, HEAD), (row_total, 1), (1, row_total)]
    return pair, blocks, [resident(shape) for shape in shared]


def attend(joint_proj, shared, first_step, steps):
    row_total = joint_proj.shape[0]
    ratio, chunk = HEADS // KV_HEADS, chunk_of(joint_proj.shape[0])
    pair, blocks, shared_specs = head_specs(row_total, first_step)

    def kernel(query_ref, key_ref, value_ref, query_gain, key_gain, cosine, sine, rows, columns, out, inverse):
        turns = (cosine[...], sine[...])
        heads = [[] for _ in range(2 * ratio)]
        inverses = [[] for _ in range(2 * ratio)]
        for g in range(2):
            key = rotated_head(head_of(key_ref[...], g), key_gain[...], *turns)
            value = head_of(value_ref[...], g).astype(low_type)
            value = jnp.concatenate([value, jnp.ones_like(value)], axis=1)
            queries = [
                rotated_head(head_of(query_ref[...], ratio * g + j), query_gain[...], *turns)
                for j in range(ratio)
            ]
            for start in range(0, row_total, chunk):
                end = start + chunk
                allowed = allowed_scores(rows[...], columns[...], start, chunk)
                batch = jnp.concatenate([query[start:end] for query in queries], axis=0)
                weights = head_weights(
                    batch, key[:end], jnp.concatenate([allowed] * ratio, axis=0)
                )
                sums = plain_product(weights.astype(low_type), value[:end])
                inverted = 1.0 / sums[:, HEAD : HEAD + 1]
                done = (sums[:, :HEAD] * inverted).astype(low_type)
                for j in range(ratio):
                    heads[ratio * g + j].append(done[j * chunk : (j + 1) * chunk])
                    inverses[ratio * g + j].append(inverted[j * chunk : (j + 1) * chunk])
        out[...] = jnp.concatenate([jnp.concatenate(head, axis=0) for head in heads], axis=1)
        for n, parts in enumerate(inverses):
            inverse[0, :, n : n + 1] = jnp.concatenate(parts, axis=0)

    return call_kernel(
        kernel,
        [joint_proj] * 3 + list(shared),
        blocks + shared_specs,
        [
            (pl.BlockSpec((row_total, pair), lambda i: (0, i)), ((row_total, steps * pair), low_type)),
            (
                pl.BlockSpec((1, row_total, 8), lambda i: (i, 0, 0)),
                ((steps, row_total, 8), jnp.float32),
            ),
        ],
        0,
        "attend",
        grid=(steps,),
    )


def attend_gradient(joint_proj, attended, inverse, grad, shared, first_step, steps):
    row_total = joint_proj.shape[0]
    ratio, chunk = HEADS // KV_HEADS, chunk_of(joint_proj.shape[0])
    pair, blocks, shared_specs = head_specs(row_total, first_step)
    scale = HEAD ** (-0.5)

    def kernel(
        query_ref,
        key_ref,
        value_ref,
        attended_ref,
        grad_ref,
        inverse_ref,
        query_gain,
        key_gain,
        cosine,
        sine,
        rows,
        columns,
        out_query,
        out_key,
        out_value,
        gains,
    ):
        step = pl.program_id(0)
        turns = (cosine[...], sine[...])

        @pl.when(step == 0)
        def _():
            gains[...] = jnp.zeros_like(gains)

        by_queries, by_keys, by_values = [], [], []
        for g in range(2):
            key_proj = head_of(key_ref[...], g)
            key = rotated_head(key_proj, key_gain[...], *turns)
            value = head_of(value_ref[...], g).astype(low_type)
            projs = [head_of(query_ref[...], ratio * g + j) for j in range(ratio)]
            queries = [rotated_head(proj, query_gain[...], *turns) for proj in projs]
            grads = [head_of(grad_ref[...], ratio * g + j) for j in range(ratio)]
            inners = [
                jnp.sum(
                    grads[j].astype(jnp.float32)
                    * head_of(attended_ref[...], ratio * g + j).astype(jnp.float32),
                    axis=-1,
                    keepdims=True,
                )
                for j in range(ratio)
            ]
            turned = [[] for _ in range(ratio)]
            by_key = by_value = None
            for start in range(row_total - chunk, -1, -chunk):
                end = start + chunk
                allowed = allowed_scores(rows[...], columns[...], start, chunk)
                stacked_heads = lambda parts: jnp.concatenate(
                    [part[start:end] for part in parts], axis=0
                )
                query_batch, grad_batch = stacked_heads(queries), stacked_heads(grads)
                inverted = jnp.concatenate(
                    [
                        inverse_ref[0, start:end, ratio * g + j : ratio * g + j + 1]
                        for j in range(ratio)
                    ],
                    axis=0,
                )
                weights = head_weights(
                    query_batch, key[:end], jnp.concatenate([allowed] * ratio, axis=0)
                )
                probs = weights * inverted
                grad_probs = product_with_transpose(grad_batch, value[:end])
                grad_scores = (probs * (grad_probs - stacked_heads(inners))).astype(low_type)
                by_batch = plain_product(grad_scores, key[:end]) * scale
                for j in range(ratio):
                    turned[j].insert(0, by_batch[j * chunk : (j + 1) * chunk])
                key_term = product_over_rows(grad_scores, query_batch) * scale
                value_term = product_over_rows(probs.astype(low_type), grad_batch)
                if by_key is None:
                    by_key, by_value = key_term, value_term
                else:
                    by_key = jnp.concatenate([by_key[:end] + key_term, by_key[end:]], axis=0)
                    by_value = jnp.concatenate([by_value[:end] + value_term, by_value[end:]], axis=0)
            for j in range(ratio):
                by_query, by_gain = head_gradient(
                    projs[j], query_gain[...], *turns, jnp.concatenate(turned[j], axis=0)
                )
                by_queries.append(by_query)
                gains[0:1, :] += by_gain
            by_key, by_gain = head_gradient(key_proj, key_gain[...], *turns, by_key)
            by_keys.append(by_key)
            by_values.append(by_value)
            gains[1:2, :] += by_gain
        for out, parts in ((out_query, by_queries), (out_key, by_keys), (out_value, by_values)):
            out[...] = jnp.concatenate(parts, axis=1).astype(low_type)

    columns = pl.BlockSpec((row_total, pair), lambda i: (0, first_step + i))
    out = lambda width: (
        pl.BlockSpec((row_total, width), lambda i: (0, i)),
        ((row_total, steps * width), low_type),
    )
    return call_kernel(
        kernel,
        [joint_proj] * 3 + [attended, grad, inverse] + list(shared),
        blocks
        + [
            columns,
            columns,
            pl.BlockSpec((1, row_total, 8), lambda i: (i, 0, 0)),
        ]
        + shared_specs,
        [
            out(pair),
            out(2 * HEAD),
            out(2 * HEAD),
            (resident((8, HEAD)), ((8, HEAD), jnp.float32)),
        ],
        40 * steps,
        "attend_gradient",
        grid=(steps,),
    )


def token_scratch(chips, rows, depth):
    return [pltpu.VMEM((chips * rows, depth), low_type), pltpu.SemaphoreType.DMA((chips,))]


def token_block(rows, width):
    return pl.BlockSpec((1, rows, width), lambda i, *_: (i, 0, 0))


def load_tokens(chips, rows, refs, target, sems):
    step = pl.program_id(0)

    @pl.when(step == 0)
    def _():
        for copy in piece_copies(piece_rows(chips, rows, len(refs)), refs, target, sems):
            copy.start()

    block = target.at[pl.ds(pl.multiple_of(step * rows, rows), rows)]
    pltpu.make_async_copy(block, block, sems.at[step]).wait()
    return block[...]


def times_blocks(x, blocks, columns):
    total, start = None, 0
    for block in blocks:
        rows = block.shape[0]
        term = plain_product(x[:, start : start + rows], block[:, columns])
        total = term if total is None else total + term
        start += rows
    return total


def gated_forward(tokens, joint_w, keep):
    chips = lax.axis_size("rep") // 2
    rows, depth = tokens[0].shape
    units = joint_w[0].shape[1] // 2
    count, blocks = len(tokens), len(joint_w)

    def kernel(*refs):
        weight = refs[count : count + blocks]
        act, to_gate, to_up = refs[count + blocks : count + blocks + 3]
        x = load_tokens(chips, rows, refs[:count], *refs[-2:])
        if keep:
            refs[count + blocks + 3][0] = x
        gate = times_blocks(x, weight, slice(0, units))
        upward = times_blocks(x, weight, slice(units, 2 * units))
        sig = 1.0 / (1.0 + jnp.exp(-gate))
        silu = gate * sig
        act[0] = (silu * upward).astype(low_type)
        to_gate[0] = (upward * sig * (1.0 + gate * (1.0 - sig))).astype(low_type)
        to_up[0] = silu.astype(low_type)

    out = (token_block(rows, units), ((chips, rows, units), low_type))
    kept = (token_block(rows, depth), ((chips, rows, depth), low_type))
    return call_kernel(
        kernel,
        [*tokens, *joint_w],
        [in_place] * count + [resident(block.shape) for block in joint_w],
        [out] * 3 + [kept] * keep,
        0,
        "gated_forward",
        grid=(chips,),
        scratch=token_scratch(chips, rows, depth),
    )


def gated_backward(tokens, halves, down_ws, joint_ws):
    chips, rows, units = halves[0][0].shape
    depth = tokens[0].shape[1]
    count = len(tokens)
    firsts = [0, len(joint_ws[0])]
    cuts = piece_rows(chips, rows, 5 if chips == 4 else chips)
    joint_flat = [*joint_ws[0], *joint_ws[1]]

    def kernel(*refs):
        factors, down_refs = refs[count : count + 4], refs[count + 4 : count + 6]
        joint_refs = refs[count + 6 : count + 6 + len(joint_flat)]
        outs, scratch = refs[count + 6 + len(joint_flat) : -2], refs[-2:]
        grads, outs = outs[:4], outs[4:]
        grad = load_tokens(chips, rows, refs[:count], *scratch)
        total = None
        for n in range(2):
            grad_act = product_with_transpose(grad, down_refs[n][...])
            gate = (grad_act * factors[2 * n][0].astype(jnp.float32)).astype(low_type)
            upward = (grad_act * factors[2 * n + 1][0].astype(jnp.float32)).astype(low_type)
            grads[2 * n][0] = gate
            grads[2 * n + 1][0] = upward
            term = jnp.concatenate(
                [
                    product_with_transpose(gate, block[:, :units])
                    + product_with_transpose(upward, block[:, units:])
                    for block in joint_refs[firsts[n] : firsts[n] + len(joint_ws[n])]
                ],
                axis=1,
            )
            total = term if total is None else total + term
        n = 0
        for i, group in enumerate(cuts):
            start = 0
            for size in group:

                @pl.when(pl.program_id(0) == i)
                def _(out=outs[n], start=start, size=size):
                    out[...] = total[start : start + size].astype(low_type)

                start += size
                n += 1

    narrow = token_block(rows, units)
    shapes = [(size, depth) for group in cuts for size in group]
    outs = call_kernel(
        kernel,
        [*tokens, *halves[0], *halves[1], *down_ws, *joint_flat],
        [in_place] * count
        + [narrow] * 4
        + [resident(w.shape) for w in (*down_ws, *joint_flat)],
        [(narrow, ((chips, rows, units), low_type))] * 4
        + [(resident(shape), (shape, low_type)) for shape in shapes],
        0,
        "gated_backward",
        grid=(chips,),
        scratch=token_scratch(chips, rows, depth),
    )
    return outs[:2], outs[2:4], as_groups(outs[4:], cuts)


def as_groups(pieces, cuts):
    groups, n = [], 0
    for group in cuts:
        groups.append(list(pieces[n : n + len(group)]))
        n += len(group)
    return groups


def down_forward(acts, down_ws):
    chips, rows, units = acts[0].shape
    depth = down_ws[0].shape[1]

    def kernel(*refs):
        total = plain_product(refs[0][0], refs[2][...]) + plain_product(refs[1][0], refs[3][...])
        for i, out in enumerate(refs[4:]):

            @pl.when(pl.program_id(0) == i)
            def _(out=out):
                out[...] = total.astype(low_type)

    act = token_block(rows, units)
    return call_kernel(
        kernel,
        [*acts, *down_ws],
        [act, act] + [resident((units, depth))] * 2,
        [(resident((rows, depth)), ((rows, depth), low_type))] * chips,
        0,
        "down_forward",
        grid=(chips,),
    )


def weight_gradient(xs, grads, steps):
    chips, rows, depth = xs[0].shape
    units = grads[0].shape[2]
    width = depth // steps

    def kernel(*refs):
        terms = [
            product_over_rows(
                refs[n][...].reshape(chips * rows, width),
                refs[2 + n][...].reshape(chips * rows, units),
            )
            for n in range(2)
        ]
        refs[4][...] = (terms[0] + terms[1]).astype(low_type)

    return call_kernel(
        kernel,
        [*xs, *grads],
        [pl.BlockSpec((chips, rows, width), lambda i: (0, 0, i))] * 2
        + [resident(grads[0].shape)] * 2,
        [(pl.BlockSpec((width, units), lambda i: (i, 0)), ((depth, units), low_type))],
        0,
        "weight_gradient",
        grid=(steps,),
    )[0]


def down_gradients(acts, grads, steps):
    chips, rows, units = acts[0].shape
    depth = grads[0].shape[1]
    width = depth // steps
    count = len(grads)

    def kernel(*refs):
        act_refs, outs, (own, sems) = refs[count : count + 2], refs[count + 2 : -2], refs[-2:]
        step = pl.program_id(0)

        @pl.when(step == 0)
        def _():
            for copy in piece_copies(piece_rows(chips, rows, count), refs[:count], own, sems):
                copy.start()
            for i in range(chips):
                block = own.at[pl.ds(i * rows, rows)]
                pltpu.make_async_copy(block, block, sems.at[i]).wait()

        right = own[:, pl.ds(pl.multiple_of(step * width, width), width)]
        for act, out in zip(act_refs, outs, strict=True):
            out[...] = product_over_rows(act[...].reshape(chips * rows, units), right).astype(
                low_type
            )

    out = (pl.BlockSpec((units, width), lambda i: (0, i)), ((units, depth), low_type))
    return call_kernel(
        kernel,
        [*grads, *acts],
        [in_place] * count + [resident(acts[0].shape)] * 2,
        [out] * 2,
        0,
        "down_gradients",
        grid=(steps,),
        scratch=token_scratch(chips, rows, depth),
    )


def plane_place():
    rep = lax.axis_index("rep")
    return jnp.stack([rep // 2, rep % 2]).astype(jnp.int32)


def both_cores(pieces):
    return pieces + [swap(stacked(pieces), 1)]


def plane_scratch(chips, rows, width):
    return [
        pltpu.VMEM((2, chips * rows, width), low_type),
        pltpu.SemaphoreType.DMA((2, chips)),
    ]


def load_plane(chips, rows, refs, target, sems):
    @pl.when(pl.program_id(0) == 0)
    def _():
        copies = piece_copies(
            piece_rows(chips, rows, len(refs) - 1), refs[:-1], target.at[0], sems.at[0]
        )
        copies.append(pltpu.make_async_copy(refs[-1], target.at[1], sems.at[1, 0]))
        for copy in copies:
            copy.start()
        for i in range(chips):
            block = target.at[0, pl.ds(i * rows, rows)]
            pltpu.make_async_copy(block, block, sems.at[0, i]).wait()
        pltpu.make_async_copy(target.at[1], target.at[1], sems.at[1, 0]).wait()


def whole_columns(pieces, share):
    size, chips = lax.axis_size("shard"), lax.axis_size("rep") // 2
    rows, width = pieces[0].shape
    step_rows = rows // 4

    def kernel(at, *refs):
        out, target, sems = refs[-3:]
        load_plane(chips, rows, refs[:-3], target, sems)
        step = pl.program_id(0)
        for j in range(2 * chips):
            start = (at[0] ^ (j // 2)) * rows + step * step_rows
            own = target[at[1] ^ (j % 2), pl.ds(pl.multiple_of(start, 16), step_rows), :]
            own = own.astype(jnp.float32)
            for z in range(size):
                first = (z * 2 * chips + j) * share
                out[:, first : first + share] = own[:, z * width // size :][:, :share]

    wide = 2 * chips * size * share
    return call_kernel(
        kernel,
        [plane_place(), *pieces],
        [in_place] * len(pieces),
        [(pl.BlockSpec((step_rows, wide), lambda i, at: (i, 0)), ((rows, wide), jnp.float32))],
        0,
        "whole_columns",
        grid=(4,),
        prefetch=1,
        scratch=plane_scratch(chips, rows, width),
    )[0]


def whole_rows(pieces, share):
    chips = lax.axis_size("rep") // 2
    rows, width = pieces[0].shape

    def kernel(at, *refs):
        out, target, sems = refs[-3:]
        load_plane(chips, rows, refs[:-3], target, sems)
        j = pl.program_id(0)
        start = pl.multiple_of((at[0] ^ (j // 2)) * rows, 32)
        own = target[at[1] ^ (j % 2), pl.ds(start, rows), :].astype(jnp.float32)
        out[0] = own[:share]

    shape = (2 * chips, share, width)
    return call_kernel(
        kernel,
        [plane_place(), *pieces],
        [in_place] * len(pieces),
        [(pl.BlockSpec((1, share, width), lambda j, at: (j, 0, 0)), (shape, jnp.float32))],
        0,
        "whole_rows",
        grid=(2 * chips,),
        prefetch=1,
        scratch=plane_scratch(chips, rows, width),
    )[0].reshape(2 * chips * share, width)


def rows_of(values, width):
    rows = -(-values.shape[0] // width)
    block = jnp.pad(values, (0, rows * width - values.shape[0])).reshape(rows, width)
    return jnp.pad(block, ((0, -rows % 16), (0, 0)))


def in_shard_order(parts):
    size, here = lax.axis_size("shard"), lax.axis_index("shard")
    twice = jnp.concatenate(parts + parts)
    run = parts[0].shape[0]
    return lax.dynamic_slice_in_dim(twice, (size - here) * run, size * run, 0)


def padded(share):
    return -(-share // 32) * 32


def own_columns(weight):
    size, reps = lax.axis_size("shard"), lax.axis_size("rep")
    run = weight.shape[1] // size
    share = run // reps
    rep = lax.axis_index("rep")
    none = jnp.zeros((weight.shape[0], padded(share) - share), weight.dtype)
    parts = []
    for z in range(size):
        parts += [lax.dynamic_slice_in_dim(weight, z * run + rep * share, share, 1), none]
    return jnp.concatenate(parts, axis=1)


def own_rows(weight):
    share = weight.shape[0] // lax.axis_size("rep")
    own = lax.dynamic_slice_in_dim(weight, lax.axis_index("rep") * share, share, 0)
    return jnp.pad(own, ((0, padded(share) - share), (0, 0)))


def scatter_group(partial):
    return lax.psum_scatter(partial, "shard", scatter_dimension=0, tiled=True)


def local(
    tokens,
    norm_gains,
    w_query,
    w_key,
    w_value,
    w_out,
    w_gate,
    w_up,
    w_down,
    seq_lengths,
    seq_device,
    cotangent,
):
    row_total = tokens.shape[0]
    size, reps = lax.axis_size("shard"), lax.axis_size("rep")
    chips = reps // 2
    rep = lax.axis_index("rep")
    device = rep * size + lax.axis_index("shard")
    query_width, key_width = HEADS * HEAD, KV_HEADS * HEAD

    w_joint = jnp.concatenate([w_query, w_key, w_value], axis=1)
    joint, outer = Tiles(w_joint), Tiles(w_out)
    joint_tile = jnp.concatenate([joint.own(w_joint), rows_of(norm_gains, joint.width)], axis=0)
    joint_slots = [from_ahead(joint_tile, k) for k in range(1, size)]
    gated_own = jnp.concatenate([own_columns(w_gate), own_columns(w_up)], axis=1)
    live, segment, position = layout(seq_lengths, seq_device, device, row_total)
    cotangent_live = jnp.where(live[:, None], cotangent, jnp.zeros_like(cotangent))
    gated_own, down_own, joint_slots, out_tile = fence(
        gated_own, own_rows(w_down), joint_slots, outer.own(w_out)
    )
    gather_shards = lambda own: lax.all_gather(own, "shard", axis=0, tiled=True)
    gated_w, down_w = gather_shards(gated_own), gather_shards(down_own)
    joint_tiles = jnp.concatenate([slot[: joint.part] for slot in joint_slots], axis=0)
    joint_near = near_groups(joint_tiles, joint.members)
    out_slots = [from_ahead(out_tile, k) for k in range(1, size)]
    gains = in_shard_order(
        [norm_gains]
        + [slot[joint.part :].reshape(-1)[: norm_gains.shape[0]] for slot in joint_slots]
    )
    joint_near, out_slots, gains = fence(joint_near, out_slots, gains)
    out_tiles = jnp.concatenate(out_slots, axis=0)
    joint_far = far_group(joint_near, joint.members)
    if joint_far:
        joint_far = [jnp.concatenate(joint_far, axis=0)]
    joint_pieces = joint.across([joint_tiles] + joint_near + joint_far)

    cosine, sine = rotary_tables(position, HEAD)
    gains = gains.astype(jnp.float32)[None]
    gain_in = gains[:, :D]
    gain_ff = gains[:, D + 2 * HEAD :]
    shared = (
        gains[:, D : D + HEAD],
        gains[:, D + HEAD : D + 2 * HEAD],
        jnp.concatenate([cosine, cosine], axis=1),
        jnp.concatenate([0.0 - sine, sine], axis=1),
        segment[:, None],
        segment[None, :],
    )
    joint_pieces, shared, out_tiles = fence(joint_pieces, shared, out_tiles)
    out_groups = all_groups(out_tiles, outer.members)
    joint_proj, normed_in = attention_input(joint, tokens, gain_in, w_joint, joint_pieces)

    joint_proj, normed_in = fence(joint_proj, normed_in)
    half_steps = KV_HEADS // 4
    attended_early, inverse_early = attend(joint_proj, shared, 0, half_steps)

    joint_proj, attended_early, out_groups, normed_in = fence(
        joint_proj, attended_early, out_groups, normed_in
    )
    out_pieces = outer.across(out_groups)
    normed_near = near_groups(normed_in, joint.members)
    attended_late, inverse_late = attend(joint_proj, shared, half_steps, half_steps)
    attended = jnp.concatenate([attended_early, attended_late], axis=1)

    attended, out_pieces = fence(attended, out_pieces)
    hidden, normed_ff = attention_output(outer, attended, tokens, gain_ff, w_out, out_pieces)

    normed_ff, normed_near = fence(normed_ff, normed_near)
    ff_near = near_groups(normed_ff, 2)

    ff_near, gated_w = fence(ff_near, gated_w)
    ff_far = far_group(ff_near, 2)
    half = gated_w.shape[0] // 2
    halves = (gated_w[:half], gated_w[half:])
    ff_far, gated_w, halves, cotangent_live, normed_near = fence(
        ff_far, gated_w, halves, cotangent_live, normed_near
    )
    ff_tokens = [normed_ff] + ff_near + ff_far
    gated_ws = ([gated_w], [swap(part, 1) for part in halves])
    grad_mixed = all_groups(cotangent_live, 2)
    *ours, group_tokens = gated_forward(ff_tokens, gated_ws[0], True)

    ours, gated_ws, group_tokens, attended = fence(ours, gated_ws, group_tokens, attended)
    attended_near = near_groups(attended, outer.members)
    theirs = gated_forward(ff_tokens, gated_ws[1], False)

    theirs, grad_mixed = fence(theirs, grad_mixed)
    grad_downs = down_gradients((ours[0], theirs[0]), grad_mixed, 2)

    grad_downs, down_w, attended_near = fence(grad_downs, down_w, attended_near)
    down_ws = (down_w, swap(down_w, 1))
    other_down = swap(grad_downs[1], 1)
    attended_far = far_group(attended_near, outer.members)

    down_ws, ours, theirs, normed_near = fence(down_ws, ours, theirs, normed_near)
    normed_far = far_group(normed_near, joint.members)
    down_parts = down_forward((ours[0], theirs[0]), down_ws)

    down_parts, other_down, attended_far, normed_far, group_tokens = fence(
        down_parts, other_down, attended_far, normed_far, group_tokens
    )
    attended_rows = [attended] + attended_near + attended_far
    normed_rows = [normed_in] + normed_near + normed_far
    all_tokens = (group_tokens, swap(group_tokens, 1))
    down_terms = sum_terms(down_parts, 2)
    grad_down = grad_downs[0].astype(jnp.float32) + other_down.astype(jnp.float32)
    grad_down = scatter_group(grad_down.astype(low_type))
    our_grads, their_grads, grad_x = gated_backward(
        grad_mixed, (ours[1:], theirs[1:]), down_ws, gated_ws
    )

    grad_x, our_grads, their_grads, all_tokens, down_terms = fence(
        grad_x, our_grads, their_grads, all_tokens, down_terms
    )
    grad_x_far = far_terms(grad_x, 2)
    their_grads = [swap(part, 1) for part in their_grads]
    grad_gate = weight_gradient(all_tokens, (our_grads[0], their_grads[0]), 4)

    grad_x_far, grad_gate, their_grads, down_terms, grad_down = fence(
        grad_x_far, grad_gate, their_grads, down_terms, grad_down
    )
    grad_terms = near_terms(grad_x, grad_x_far, 2)
    down_near = near_groups(grad_down, 2)
    grad_gate = scatter_group(grad_gate)
    grad_up = weight_gradient(all_tokens, (our_grads[1], their_grads[1]), 4)

    grad_terms, grad_up = fence(grad_terms, grad_up)
    grad_up = scatter_group(grad_up)
    grad_hidden, grad_gain_ff, grad_attended, *cuts = attention_output_gradient(
        outer, grad_terms, cotangent_live, hidden, gain_ff, w_out, out_pieces
    )

    cuts, grad_attended, down_near = fence(cuts, grad_attended, down_near)
    down_far = far_group(down_near, 2)
    out_runs = outer.group_columns(cuts)
    half_steps = KV_HEADS // 4
    early = attend_gradient(
        joint_proj, attended, inverse_early, grad_attended, shared, 0, half_steps
    )

    early, out_runs, down_far, grad_gate, grad_attended = fence(
        early, out_runs, down_far, grad_gate, grad_attended
    )
    gate_near = near_groups(grad_gate, 2)
    late = attend_gradient(
        joint_proj, attended, inverse_late, grad_attended, shared, half_steps, half_steps
    )

    early, late, gate_near = fence(early, late, gate_near)
    head_gains = early[3] + late[3]
    parts = [part for n in range(3) for part in (early[n], late[n])]
    grad_joint_low = jnp.concatenate(parts, axis=1)
    cuts, grad_joint_low = fence(joint.cut_columns(grad_joint_low), grad_joint_low)
    joint_runs = joint.group_columns(cuts)
    down_pieces = both_cores([grad_down] + down_near + down_far)
    grad_tokens, grad_gain_in = attention_input_gradient(
        joint, grad_joint_low, grad_hidden, tokens, gain_in, w_joint, joint_pieces
    )

    joint_runs, grad_gain_in, out_runs, down_pieces, gate_near = fence(
        joint_runs, grad_gain_in, out_runs, down_pieces, gate_near
    )
    gate_far = far_group(gate_near, 2)
    sums = outer.tile(attended_rows, out_runs)
    sums = joint.tile(normed_rows, joint_runs, sums)
    grad_gains = jnp.concatenate(
        [grad_gain_in, head_gains[0:1], head_gains[1:2], grad_gain_ff], axis=1
    )[0]
    extra = joint.extra_rows(grad_gains, sums[0].shape[1])

    sums, gate_far = fence(sums, gate_far)
    sums = sums[:1] + tuple(swap(part, h) for h, part in enumerate(sums) if h)
    gate_pieces = both_cores([grad_gate] + gate_near + gate_far)

    sums, down_pieces, gate_pieces, down_terms = fence(sums, down_pieces, gate_pieces, down_terms)
    own, sent = joint.send(sums, extra)
    up_near = near_groups(grad_up, 2)
    whole_down = whole_rows(down_pieces, w_down.shape[0] // reps)
    whole_gate = whole_columns(gate_pieces, w_down.shape[0] // reps)

    mixed_full = hidden
    for term in down_terms:
        mixed_full = mixed_full + term.astype(jnp.float32)
    mixed = jnp.where(live[:, None], mixed_full, jnp.zeros_like(mixed_full)).astype(jnp.bfloat16)

    whole_down, whole_gate, up_near, mixed = fence(whole_down, whole_gate, up_near, mixed)
    up_far = far_group(up_near, 2)

    own, sent, up_far = fence(own, sent, up_far)
    total = own
    for part in sent:
        total = total + part.astype(jnp.float32)
    total_groups = all_groups(total.astype(low_type), joint.members)
    up_pieces = both_cores([grad_up] + up_near + up_far)

    up_pieces = fence(*up_pieces)
    whole_up = whole_columns(up_pieces, w_down.shape[0] // reps)

    total_groups, whole_up = fence(total_groups, whole_up)
    whole_pieces = joint.across_stacked(total_groups)
    *grad_joint, grad_out_w, beneath = joint.whole(
        whole_pieces, ((query_width, key_width, key_width), (D,))
    )
    grad_gains = beneath.reshape(-1)[: norm_gains.shape[0]]
    share = w_down.shape[0] // reps
    return (
        mixed,
        grad_tokens,
        grad_gains,
        *grad_joint,
        grad_out_w,
        whole_gate,
        whole_up,
        whole_down,
    )


def solution(mesh):
    return jax.shard_map(
        local,
        mesh=mesh,
        in_specs=(
            P(("rep", "shard"), None),
            P("shard"),
            P("shard", None),
            P("shard", None),
            P("shard", None),
            P("shard", None),
            P("shard", None),
            P("shard", None),
            P("shard", None),
            P(),
            P(),
            P(("rep", "shard"), None),
        ),
        out_specs=(
            P(("rep", "shard"), None),
            P(("rep", "shard"), None),
            P("shard"),
            P("shard", None),
            P("shard", None),
            P("shard", None),
            P("shard", None),
            P("shard", None),
            P("shard", None),
            P("shard", None),
        ),
        check_vma=False,
    )
```

```python
import math

import jax
import jax.numpy as jnp
from jax import lax
from jax.experimental import pallas as pl
from jax.experimental.pallas import tpu as pltpu
from jax.sharding import PartitionSpec as P

D = 1536
HEADS = 24
KV_HEADS = 8
HEAD = 64
FF = 6912


epsilon = 1e-05
rope_base = 1000000.0
masked_score = -1e30


def plain_product(left, right):
    return jnp.dot(left, right, preferred_element_type=jnp.float32)


def product_over_rows(left, right):
    return lax.dot_general(
        left, right, (((0,), (0,)), ((), ())), preferred_element_type=jnp.float32
    )


def product_with_transpose(left, right):
    return lax.dot_general(
        left, right, (((1,), (1,)), ((), ())), preferred_element_type=jnp.float32
    )


def rotary_tables(position, head_width):
    half_width = head_width // 2
    index = jnp.arange(half_width).astype(jnp.float32)
    inverse = jnp.exp(index * (-2.0 * math.log(rope_base) / head_width))
    angle = position.astype(jnp.float32)[:, None] * inverse[None, :]
    return (jnp.cos(angle), jnp.sin(angle))


def layout(seq_lengths, seq_device, device, row_total):
    own_length = jnp.where(seq_device == device, seq_lengths, 0)
    ends = jnp.cumsum(own_length, dtype=jnp.int32)
    begins = ends - own_length
    slot_index = jnp.arange(row_total, dtype=jnp.int32)
    inside = (slot_index[:, None] >= begins[None, :]) & (slot_index[:, None] < ends[None, :])
    live = jnp.any(inside, axis=1)
    seq_total = seq_lengths.shape[0]
    numbers = jnp.arange(seq_total, dtype=jnp.int32)
    found = jnp.sum(jnp.where(inside, numbers[None, :], 0), axis=1, dtype=jnp.int32)
    segment = jnp.where(live, found, seq_total + slot_index)
    offset = jnp.sum(jnp.where(inside, (0 - begins)[None, :], 0), axis=1, dtype=jnp.int32)
    position = jnp.where(live, slot_index + offset, 0)
    return (live, segment, position)


vmem_bytes = 60 * 2**20
low_type = jnp.bfloat16
in_place = pl.BlockSpec(memory_space=pl.ANY)


def swap(values, offset):
    size = lax.axis_size("rep")
    return lax.ppermute(values, "rep", [(i, i ^ offset) for i in range(size)])


def from_ahead(values, steps):
    size = lax.axis_size("shard")
    return lax.ppermute(values, "shard", [((i + steps) % size, i) for i in range(size)])


def from_behind(values, steps):
    size = lax.axis_size("shard")
    return lax.ppermute(values, "shard", [(i, (i + steps) % size) for i in range(size)])


def fence(*values):
    return lax.optimization_barrier(values)


def after(values, *others):
    return lax.optimization_barrier((values, others))[0]


def all_groups(block, unit):
    return [block] + [swap(block, unit * d) for d in range(1, lax.axis_size("rep") // unit)]


def sum_terms(blocks, unit):
    return [swap(block, unit * d) if d else block for d, block in enumerate(blocks)]


def near_groups(block, unit):
    groups = lax.axis_size("rep") // unit
    return [swap(block, unit * d) for d in range(1, groups if groups != 4 else 3)]


def far_group(near, unit):
    if lax.axis_size("rep") // unit != 4:
        return []
    half = half_rows(near[0].shape[0])
    return [swap(near[1][:half], unit), swap(near[0][half:], 2 * unit)]


def far_terms(blocks, unit):
    return [swap(blocks[3][0], unit), swap(blocks[3][1], 2 * unit)] if len(blocks) == 4 else []


def near_terms(blocks, far, unit):
    if not far:
        return [swap(block[0], unit * d) if d else block[0] for d, block in enumerate(blocks)]
    half = blocks[3][0].shape[0]
    one, two = blocks[1][0], blocks[2][0]
    add = lambda left, right: (left.astype(jnp.float32) + right.astype(jnp.float32)).astype(low_type)
    one = jnp.concatenate([one[:half], add(one[half:], far[1])], axis=0)
    two = jnp.concatenate([add(two[:half], far[0]), two[half:]], axis=0)
    return [blocks[0][0], swap(one, unit), swap(two, 2 * unit)]


def half_rows(rows):
    return rows // 2 // 16 * 16


def piece_rows(groups, rows, count):
    half = half_rows(rows)
    return [[rows]] * groups if count == groups else [[rows]] * 3 + [[half, rows - half]]


def piece_copies(rows, refs, target, sems):
    copies, at, n = [], 0, 0
    for i, group in enumerate(rows):
        for count in group:
            copies.append(
                pltpu.make_async_copy(refs[n], target.at[pl.ds(at, count)], sems.at[i])
            )
            at += count
            n += 1
    return copies


def call_kernel(kernel, args, ins, outs, micros, name, grid=None, prefetch=0, scratch=()):
    return pl.pallas_call(
        kernel,
        grid_spec=pltpu.PrefetchScalarGridSpec(
            num_scalar_prefetch=prefetch,
            grid=grid or (1,),
            in_specs=ins,
            out_specs=[spec for spec, _ in outs],
            scratch_shapes=list(scratch),
        ),
        out_shape=[jax.ShapeDtypeStruct(*shape) for _, shape in outs],
        compiler_params=pltpu.CompilerParams(vmem_limit_bytes=vmem_bytes),
        cost_estimate=pl.CostEstimate(flops=int(micros * 1.15e9), bytes_accessed=0, transcendentals=0),
        name=name,
    )(*args)


def resident(shape):
    return pl.BlockSpec(shape, lambda *_: (0,) * len(shape), pipeline_mode=pl.Buffered(1))


def spread(values, shards, members):
    part = values.shape[1] // shards // members
    return [
        jnp.concatenate(
            [values[:, (z * members + p) * part :][:, :part] for z in range(shards)], axis=1
        )
        for p in range(members)
    ]


def unspread(parts, shards):
    part = parts[0].shape[1] // shards
    return jnp.concatenate(
        [run[:, z * part : (z + 1) * part] for z in range(shards) for run in parts], axis=1
    )


def norm_factor(values):
    return lax.rsqrt(jnp.mean(values * values, axis=-1, keepdims=True) + epsilon)


def norm_gradient(values, gain, grad):
    factor = norm_factor(values)
    scaled = grad * gain
    mean = jnp.mean(scaled * values, axis=-1, keepdims=True)
    by_gain = jnp.sum(grad * values * factor, axis=0, keepdims=True)
    return factor * scaled - values * (factor * factor * factor * mean), by_gain


def stacked(pieces):
    rows = sum(piece.shape[0] for piece in pieces)

    def kernel(*refs):
        copies, start = [], 0
        for n, piece in enumerate(pieces):
            target = refs[len(pieces)].at[pl.ds(start, piece.shape[0])]
            copies.append(pltpu.make_async_copy(refs[n], target, refs[-1].at[n]))
            start += piece.shape[0]
        for copy in copies:
            copy.start()
        for copy in copies:
            copy.wait()

    shape = (rows, pieces[0].shape[1])
    return call_kernel(
        kernel,
        pieces,
        [in_place] * len(pieces),
        [(resident(shape), (shape, low_type))],
        0,
        "stacked",
        scratch=[pltpu.SemaphoreType.DMA((len(pieces),))],
    )[0]


class Tiles:
    def __init__(self, weight):
        reps = lax.axis_size("rep")
        groups = reps // 2
        while weight.shape[1] % (128 * groups):
            groups //= 2
        self.groups, self.members = groups, reps // groups
        self.shards, self.here = lax.axis_size("shard"), lax.axis_index("shard")
        self.group = lax.axis_index("rep") // self.members
        self.member = lax.axis_index("rep") % self.members
        self.rows = weight.shape[0]
        self.part = self.rows // self.members
        self.rest = (self.shards - 1) * self.part
        self.depth = self.shards * self.part
        self.width = weight.shape[1] // groups

    def own(self, weight):
        return lax.dynamic_slice(
            weight, (self.member * self.part, self.group * self.width), (self.part, self.width)
        )

    def across(self, pieces):
        return pieces + [swap(piece, h) for h in range(1, self.members) for piece in pieces]

    def place(self):
        return jnp.stack([self.group, self.member, self.here]).astype(jnp.int32)

    def scratch(self):
        shape = (self.members, self.groups)
        return [
            pltpu.VMEM(shape + (self.depth, self.width), low_type),
            pltpu.SemaphoreType.DMA(shape),
        ]

    def load(self, at, weight_ref, refs, tiles, sems):
        part, shards, groups = self.part, self.shards, self.groups

        def to(h, d, z, start, size):
            first = pl.multiple_of(lax.rem(at[2] + z, shards) * part, 16) + start
            return tiles.at[h, d, pl.ds(pl.multiple_of(first, 16), size)]

        for d in range(groups):
            for h in range(self.members):
                source = weight_ref.at[
                    pl.ds(pl.multiple_of((at[1] ^ h) * part, 16), part),
                    pl.ds(pl.multiple_of((at[0] ^ d) * self.width, 128), self.width),
                ]
                pltpu.make_async_copy(source, to(h, d, 0, 0, part), sems.at[h, d]).start()
                for k in range(shards - 1):
                    pltpu.make_async_copy(
                        refs[h * groups + d].at[pl.ds(k * part, part)],
                        to(h, d, k + 1, 0, part),
                        sems.at[h, d],
                    ).start()

        def wait(h, d):
            pltpu.make_async_copy(tiles.at[h, d], tiles.at[h, d], sems.at[h, d]).wait()
            return tiles[h, d]

        return wait

    def columns(self, at, d):
        return pl.ds(pl.multiple_of((at[0] ^ d) * self.width, 128), self.width)

    def multiply(self, at, wait, x, out):
        for d in range(self.groups):
            total = None
            for h in range(self.members):
                term = plain_product(x[at[1] ^ h], wait(h, d))
                total = term if total is None else total + term
            out[:, self.columns(at, d)] = total

    def multiply_transposed(self, at, wait, grad, out):
        totals = [None] * self.members
        for d in range(self.groups):
            block = grad[:, self.columns(at, d)]
            for h in range(self.members):
                term = product_with_transpose(block, wait(h, d))
                totals[h] = term if totals[h] is None else totals[h] + term
        for h in range(self.members):
            out[at[1] ^ h] = totals[h]

    def call(self, kernel, args, weight, pieces, outs, micros, name, scratch=()):
        given, produced = len(args), len(outs)

        def whole_kernel(at, *refs):
            ins, weight_ref = refs[:given], refs[given]
            rest = refs[given + 1 + len(pieces) :]
            wait = self.load(
                at, weight_ref, refs[given + 1 : given + 1 + len(pieces)], *rest[produced : produced + 2]
            )
            kernel(at, ins, rest[:produced], rest[produced + 2 :], wait)

        return call_kernel(
            whole_kernel,
            [self.place(), *args, weight, *pieces],
            [resident(arg.shape) for arg in args] + [in_place] * (1 + len(pieces)),
            [(resident(shape), (shape, kind)) for shape, kind in outs],
            micros,
            name,
            prefetch=1,
            scratch=self.scratch() + list(scratch),
        )

    def cut_columns(self, grad):
        return [
            lax.dynamic_slice_in_dim(grad, (self.group ^ d) * self.width, self.width, 1)
            for d in range(self.groups)
        ]

    def group_columns(self, cuts):
        return [swap(cut, self.members * d) if d else cut for d, cut in enumerate(cuts)]

    def tile(self, rows, columns, beside=()):
        tokens, members, shards, part = columns[0].shape[0], self.members, self.shards, self.part
        count, total = len(rows), len(columns) * tokens
        sizes = [piece.shape[0] for piece in rows]
        wide = self.width + (beside[0].shape[1] if beside else 0)

        def kernel(at, *refs):
            besides = refs[count + len(columns) : count + len(columns) + len(beside)]
            outs = refs[count + len(columns) + len(beside) : -4]
            left, right, whole, sems = refs[-4:]
            copies = piece_copies([sizes], refs[:count], left, sems.at[pl.ds(0, 1)])
            copies += piece_copies(
                [[tokens] * len(columns)], refs[count : count + len(columns)], right, sems.at[pl.ds(1, 1)]
            )
            for copy in copies:
                copy.start()
            pltpu.make_async_copy(left, left, sems.at[0]).wait()
            pltpu.make_async_copy(right, right, sems.at[1]).wait()
            whole[...] = product_over_rows(left[...], right[...])
            for h in range(members):
                for k in range(shards):
                    start = lax.rem(at[2] + k, shards) * self.rows + (at[1] ^ h) * part
                    block = whole[pl.ds(pl.multiple_of(start, 16), part), :]
                    outs[h][k * part : (k + 1) * part, : self.width] = block.astype(outs[h].dtype)
                if beside:
                    outs[h][:, self.width :] = besides[h][...]

        shape = (shards * part, wide)
        return call_kernel(
            kernel,
            [self.place(), *rows, *columns, *beside],
            [in_place] * (count + len(columns)) + [resident(part.shape) for part in beside],
            [(resident(shape), (shape, low_type if h else jnp.float32)) for h in range(members)],
            7,
            "weight_tile",
            prefetch=1,
            scratch=[
                pltpu.VMEM((total, members * self.depth), low_type),
                pltpu.VMEM((total, self.width), low_type),
                pltpu.VMEM((members * self.depth, self.width), jnp.float32),
                pltpu.SemaphoreType.DMA((2,)),
            ],
        )

    def send(self, tiles, extra):
        total = tiles[0]
        for tile in tiles[1:]:
            total = total + tile.astype(jnp.float32)
        parts = [
            jnp.concatenate([total[k * self.part : (k + 1) * self.part], extra[k]], axis=0)
            for k in range(self.shards)
        ]
        return parts[0], [
            from_behind(parts[k].astype(low_type), k) for k in range(1, self.shards)
        ]

    def extra_rows(self, values, width):
        run = values.shape[0] // self.shards
        rows = -(-run // width)
        block = jnp.pad(values.reshape(self.shards, run), ((0, 0), (0, rows * width - run)))
        block = block.reshape(self.shards, rows, width)
        block = jnp.pad(block, ((0, 0), (0, -rows % 16), (0, 0)))
        twice = jnp.concatenate([block, block], axis=0)
        return lax.dynamic_slice_in_dim(twice, self.here, self.shards, 0)

    def whole(self, pieces, sections):
        members, groups, part = self.members, self.groups, self.part
        rows, wide = pieces[0].shape
        beneath = rows - part

        def kernel(at, *refs):
            outs, (tiles, sems) = refs[len(pieces) : -2], refs[-2:]
            for h in range(members):
                for d in range(groups):
                    pltpu.make_async_copy(
                        refs[h * groups + d], tiles.at[h, d], sems.at[h, d]
                    ).start()
            for h in range(members):
                for d in range(groups):
                    pltpu.make_async_copy(tiles.at[h, d], tiles.at[h, d], sems.at[h, d]).wait()
            total = None
            for g in range(groups):
                for p in range(members):
                    block = tiles[at[1] ^ p, at[0] ^ g].astype(jnp.float32)
                    total = block[part:] if total is None else total + block[part:]
                    n, left = 0, 0
                    for widths in sections:
                        width = sum(widths) // groups
                        first = 0
                        for run in widths:
                            low, high = max(first, g * width), min(first + run, (g + 1) * width)
                            if low < high:
                                outs[n][p * part : (p + 1) * part, low - first : high - first] = (
                                    block[:part, left + low - g * width : left + high - g * width]
                                )
                            first += run
                            n += 1
                        left += width
            outs[-1][...] = total

        shapes = [(self.rows, run) for widths in sections for run in widths] + [(beneath, wide)]
        return call_kernel(
            kernel,
            [self.place(), *pieces],
            [in_place] * len(pieces),
            [(resident(shape), (shape, jnp.float32)) for shape in shapes],
            6,
            "whole_tiles",
            prefetch=1,
            scratch=[
                pltpu.VMEM((members, groups, rows, wide), low_type),
                pltpu.SemaphoreType.DMA((members, groups)),
            ],
        )


def attention_input(tiles, tokens, gain, weight, pieces):
    def kernel(at, ins, outs, scratch, wait):
        x = ins[0][...].astype(jnp.float32)
        normed = (x * norm_factor(x) * ins[1][...]).astype(low_type)
        outs[1][...] = normed
        for p, run in enumerate(spread(normed, tiles.shards, tiles.members)):
            scratch[0][p] = run
        tiles.multiply(at, wait, scratch[0], outs[0])

    rows = tokens.shape[0]
    return tiles.call(
        kernel,
        [tokens, gain],
        weight,
        pieces,
        [
            ((rows, weight.shape[1]), jnp.float32),
            (tokens.shape, low_type),
        ],
        0,
        "attention_input",
        scratch=[pltpu.VMEM((tiles.members, rows, tiles.depth), low_type)],
    )


def attention_output(tiles, attended, tokens, gain, weight, pieces):
    def kernel(at, ins, outs, scratch, wait):
        for p, run in enumerate(spread(ins[0][...], tiles.shards, tiles.members)):
            scratch[0][p] = run
        tiles.multiply(at, wait, scratch[0], outs[0])
        hidden = outs[0][...] + ins[1][...].astype(jnp.float32)
        outs[0][...] = hidden
        outs[1][...] = (hidden * norm_factor(hidden) * ins[2][...]).astype(low_type)

    rows, depth = tokens.shape
    return tiles.call(
        kernel,
        [attended, tokens, gain],
        weight,
        pieces,
        [
            ((rows, depth), jnp.float32),
            ((rows, depth), low_type),
        ],
        0,
        "attention_output",
        scratch=[pltpu.VMEM((tiles.members, rows, tiles.depth), low_type)],
    )


def attention_output_gradient(tiles, terms, grad, hidden, gain, weight, pieces):
    count = len(terms)

    def kernel(at, ins, outs, scratch, wait):
        total = ins[0][...].astype(jnp.float32)
        for term in ins[1:count]:
            total = total + term[...].astype(jnp.float32)
        by_hidden, by_gain = norm_gradient(ins[count + 1][...], ins[count + 2][...], total)
        by_hidden = by_hidden + ins[count][...].astype(jnp.float32)
        outs[0][...] = by_hidden
        low = scratch[1]
        low[...] = by_hidden.astype(low_type)
        outs[1][...] = by_gain
        for d in range(tiles.groups):
            outs[3 + d][...] = low[:, tiles.columns(at, d)]
        tiles.multiply_transposed(at, wait, low, scratch[0])
        runs = [scratch[0][p].astype(low_type) for p in range(tiles.members)]
        outs[2][...] = unspread(runs, tiles.shards)

    rows, depth = grad.shape
    return tiles.call(
        kernel,
        [*terms, grad, hidden, gain],
        weight,
        pieces,
        [
            ((rows, depth), jnp.float32),
            ((1, depth), jnp.float32),
            ((rows, depth), low_type),
        ]
        + [((rows, tiles.width), low_type)] * tiles.groups,
        0,
        "attention_output_gradient",
        scratch=[
            pltpu.VMEM((tiles.members, rows, tiles.depth), jnp.float32),
            pltpu.VMEM((rows, depth), low_type),
        ],
    )


def attention_input_gradient(tiles, grad, grad_hidden, tokens, gain, weight, pieces):
    def kernel(at, ins, outs, scratch, wait):
        tiles.multiply_transposed(at, wait, ins[0], scratch[0])
        total = unspread([scratch[0][p] for p in range(tiles.members)], tiles.shards)
        by_tokens, by_gain = norm_gradient(
            ins[2][...].astype(jnp.float32), ins[3][...], total
        )
        outs[0][...] = ins[1][...] + by_tokens
        outs[1][...] = by_gain

    rows, depth = tokens.shape
    return tiles.call(
        kernel,
        [grad, grad_hidden, tokens, gain],
        weight,
        pieces,
        [((rows, depth), jnp.float32), ((1, depth), jnp.float32)],
        10,
        "attention_input_gradient",
        scratch=[pltpu.VMEM((tiles.members, rows, tiles.depth), jnp.float32)],
    )


def turn(values):
    half = values.shape[1] // 2
    return jnp.concatenate([values[:, half:], values[:, :half]], axis=1)


def head_of(block, n):
    return block[:, n * HEAD : (n + 1) * HEAD]


def rotated_head(values, gain, cosine, sine):
    normed = values * norm_factor(values) * gain
    return (normed * cosine + turn(normed) * sine).astype(low_type)


def head_gradient(values, gain, cosine, sine, grad):
    return norm_gradient(values, gain, grad * cosine - turn(grad) * sine)


def chunk_of(row_total):
    return min(row_total, 128)


def allowed_scores(rows, columns, start, chunk):
    end = start + chunk
    later = start + lax.broadcasted_iota(jnp.int32, (chunk, end), 0)
    earlier = lax.broadcasted_iota(jnp.int32, (chunk, end), 1)
    return (rows[start:end] == columns[:, :end]) & (later >= earlier)


def head_weights(query, key, allowed):
    scores = product_with_transpose(query, key) * HEAD ** (-0.5)
    return jnp.where(allowed, jnp.exp(scores), 0.0)


def head_specs(row_total, first_step=0):
    pair = 2 * HEADS // KV_HEADS * HEAD
    first_key, first_value = HEADS * HEAD // (2 * HEAD), (HEADS + KV_HEADS) * HEAD // (2 * HEAD)
    blocks = [
        pl.BlockSpec((row_total, pair), lambda i: (0, first_step + i)),
        pl.BlockSpec((row_total, 2 * HEAD), lambda i: (0, first_key + first_step + i)),
        pl.BlockSpec((row_total, 2 * HEAD), lambda i: (0, first_value + first_step + i)),
    ]
    shared = [(1, HEAD), (1, HEAD), (row_total, HEAD), (row_total, HEAD), (row_total, 1), (1, row_total)]
    return pair, blocks, [resident(shape) for shape in shared]


def attend(joint_proj, shared, first_step, steps):
    row_total = joint_proj.shape[0]
    ratio, chunk = HEADS // KV_HEADS, chunk_of(joint_proj.shape[0])
    pair, blocks, shared_specs = head_specs(row_total, first_step)

    def kernel(query_ref, key_ref, value_ref, query_gain, key_gain, cosine, sine, rows, columns, out, inverse):
        turns = (cosine[...], sine[...])
        heads = [[] for _ in range(2 * ratio)]
        inverses = [[] for _ in range(2 * ratio)]
        for g in range(2):
            key = rotated_head(head_of(key_ref[...], g), key_gain[...], *turns)
            value = head_of(value_ref[...], g).astype(low_type)
            value = jnp.concatenate([value, jnp.ones_like(value)], axis=1)
            queries = [
                rotated_head(head_of(query_ref[...], ratio * g + j), query_gain[...], *turns)
                for j in range(ratio)
            ]
            for start in range(0, row_total, chunk):
                end = start + chunk
                allowed = allowed_scores(rows[...], columns[...], start, chunk)
                batch = jnp.concatenate([query[start:end] for query in queries], axis=0)
                weights = head_weights(
                    batch, key[:end], jnp.concatenate([allowed] * ratio, axis=0)
                )
                sums = plain_product(weights.astype(low_type), value[:end])
                inverted = 1.0 / sums[:, HEAD : HEAD + 1]
                done = (sums[:, :HEAD] * inverted).astype(low_type)
                for j in range(ratio):
                    heads[ratio * g + j].append(done[j * chunk : (j + 1) * chunk])
                    inverses[ratio * g + j].append(inverted[j * chunk : (j + 1) * chunk])
        out[...] = jnp.concatenate([jnp.concatenate(head, axis=0) for head in heads], axis=1)
        for n, parts in enumerate(inverses):
            inverse[0, :, n : n + 1] = jnp.concatenate(parts, axis=0)

    return call_kernel(
        kernel,
        [joint_proj] * 3 + list(shared),
        blocks + shared_specs,
        [
            (pl.BlockSpec((row_total, pair), lambda i: (0, i)), ((row_total, steps * pair), low_type)),
            (
                pl.BlockSpec((1, row_total, 8), lambda i: (i, 0, 0)),
                ((steps, row_total, 8), jnp.float32),
            ),
        ],
        0,
        "attend",
        grid=(steps,),
    )


def attend_gradient(joint_proj, attended, inverse, grad, shared, first_step, steps):
    row_total = joint_proj.shape[0]
    ratio, chunk = HEADS // KV_HEADS, chunk_of(joint_proj.shape[0])
    pair, blocks, shared_specs = head_specs(row_total, first_step)
    scale = HEAD ** (-0.5)

    def kernel(
        query_ref,
        key_ref,
        value_ref,
        attended_ref,
        grad_ref,
        inverse_ref,
        query_gain,
        key_gain,
        cosine,
        sine,
        rows,
        columns,
        out_query,
        out_key,
        out_value,
        gains,
    ):
        step = pl.program_id(0)
        turns = (cosine[...], sine[...])

        @pl.when(step == 0)
        def _():
            gains[...] = jnp.zeros_like(gains)

        by_queries, by_keys, by_values = [], [], []
        for g in range(2):
            key_proj = head_of(key_ref[...], g)
            key = rotated_head(key_proj, key_gain[...], *turns)
            value = head_of(value_ref[...], g).astype(low_type)
            projs = [head_of(query_ref[...], ratio * g + j) for j in range(ratio)]
            queries = [rotated_head(proj, query_gain[...], *turns) for proj in projs]
            grads = [head_of(grad_ref[...], ratio * g + j) for j in range(ratio)]
            inners = [
                jnp.sum(
                    grads[j].astype(jnp.float32)
                    * head_of(attended_ref[...], ratio * g + j).astype(jnp.float32),
                    axis=-1,
                    keepdims=True,
                )
                for j in range(ratio)
            ]
            turned = [[] for _ in range(ratio)]
            by_key = by_value = None
            for start in range(row_total - chunk, -1, -chunk):
                end = start + chunk
                allowed = allowed_scores(rows[...], columns[...], start, chunk)
                stacked_heads = lambda parts: jnp.concatenate(
                    [part[start:end] for part in parts], axis=0
                )
                query_batch, grad_batch = stacked_heads(queries), stacked_heads(grads)
                inverted = jnp.concatenate(
                    [
                        inverse_ref[0, start:end, ratio * g + j : ratio * g + j + 1]
                        for j in range(ratio)
                    ],
                    axis=0,
                )
                weights = head_weights(
                    query_batch, key[:end], jnp.concatenate([allowed] * ratio, axis=0)
                )
                probs = weights * inverted
                grad_probs = product_with_transpose(grad_batch, value[:end])
                grad_scores = (probs * (grad_probs - stacked_heads(inners))).astype(low_type)
                by_batch = plain_product(grad_scores, key[:end]) * scale
                for j in range(ratio):
                    turned[j].insert(0, by_batch[j * chunk : (j + 1) * chunk])
                key_term = product_over_rows(grad_scores, query_batch) * scale
                value_term = product_over_rows(probs.astype(low_type), grad_batch)
                if by_key is None:
                    by_key, by_value = key_term, value_term
                else:
                    by_key = jnp.concatenate([by_key[:end] + key_term, by_key[end:]], axis=0)
                    by_value = jnp.concatenate([by_value[:end] + value_term, by_value[end:]], axis=0)
            for j in range(ratio):
                by_query, by_gain = head_gradient(
                    projs[j], query_gain[...], *turns, jnp.concatenate(turned[j], axis=0)
                )
                by_queries.append(by_query)
                gains[0:1, :] += by_gain
            by_key, by_gain = head_gradient(key_proj, key_gain[...], *turns, by_key)
            by_keys.append(by_key)
            by_values.append(by_value)
            gains[1:2, :] += by_gain
        for out, parts in ((out_query, by_queries), (out_key, by_keys), (out_value, by_values)):
            out[...] = jnp.concatenate(parts, axis=1).astype(low_type)

    columns = pl.BlockSpec((row_total, pair), lambda i: (0, first_step + i))
    out = lambda width: (
        pl.BlockSpec((row_total, width), lambda i: (0, i)),
        ((row_total, steps * width), low_type),
    )
    return call_kernel(
        kernel,
        [joint_proj] * 3 + [attended, grad, inverse] + list(shared),
        blocks
        + [
            columns,
            columns,
            pl.BlockSpec((1, row_total, 8), lambda i: (i, 0, 0)),
        ]
        + shared_specs,
        [
            out(pair),
            out(2 * HEAD),
            out(2 * HEAD),
            (resident((8, HEAD)), ((8, HEAD), jnp.float32)),
        ],
        40 * steps,
        "attend_gradient",
        grid=(steps,),
    )


def token_scratch(chips, rows, depth):
    return [pltpu.VMEM((chips * rows, depth), low_type), pltpu.SemaphoreType.DMA((chips,))]


def token_block(rows, width):
    return pl.BlockSpec((1, rows, width), lambda i, *_: (i, 0, 0))


def load_tokens(chips, rows, refs, target, sems):
    step = pl.program_id(0)

    @pl.when(step == 0)
    def _():
        for copy in piece_copies(piece_rows(chips, rows, len(refs)), refs, target, sems):
            copy.start()

    block = target.at[pl.ds(pl.multiple_of(step * rows, rows), rows)]
    pltpu.make_async_copy(block, block, sems.at[step]).wait()
    return block[...]


def times_blocks(x, blocks, columns):
    total, start = None, 0
    for block in blocks:
        rows = block.shape[0]
        term = plain_product(x[:, start : start + rows], block[:, columns])
        total = term if total is None else total + term
        start += rows
    return total


def gated_forward(tokens, joint_w, keep):
    chips = lax.axis_size("rep") // 2
    rows, depth = tokens[0].shape
    units = joint_w[0].shape[1] // 2
    count, blocks = len(tokens), len(joint_w)

    def kernel(*refs):
        weight = refs[count : count + blocks]
        act, to_gate, to_up = refs[count + blocks : count + blocks + 3]
        x = load_tokens(chips, rows, refs[:count], *refs[-2:])
        if keep:
            refs[count + blocks + 3][0] = x
        gate = times_blocks(x, weight, slice(0, units))
        upward = times_blocks(x, weight, slice(units, 2 * units))
        sig = 1.0 / (1.0 + jnp.exp(-gate))
        silu = gate * sig
        act[0] = (silu * upward).astype(low_type)
        to_gate[0] = (upward * sig * (1.0 + gate * (1.0 - sig))).astype(low_type)
        to_up[0] = silu.astype(low_type)

    out = (token_block(rows, units), ((chips, rows, units), low_type))
    kept = (token_block(rows, depth), ((chips, rows, depth), low_type))
    return call_kernel(
        kernel,
        [*tokens, *joint_w],
        [in_place] * count + [resident(block.shape) for block in joint_w],
        [out] * 3 + [kept] * keep,
        0,
        "gated_forward",
        grid=(chips,),
        scratch=token_scratch(chips, rows, depth),
    )


def gated_backward(tokens, halves, down_ws, joint_ws):
    chips, rows, units = halves[0][0].shape
    depth = tokens[0].shape[1]
    count = len(tokens)
    firsts = [0, len(joint_ws[0])]
    cuts = piece_rows(chips, rows, 5 if chips == 4 else chips)
    joint_flat = [*joint_ws[0], *joint_ws[1]]

    def kernel(*refs):
        factors, down_refs = refs[count : count + 4], refs[count + 4 : count + 6]
        joint_refs = refs[count + 6 : count + 6 + len(joint_flat)]
        outs, scratch = refs[count + 6 + len(joint_flat) : -2], refs[-2:]
        grads, outs = outs[:4], outs[4:]
        grad = load_tokens(chips, rows, refs[:count], *scratch)
        total = None
        for n in range(2):
            grad_act = product_with_transpose(grad, down_refs[n][...])
            gate = (grad_act * factors[2 * n][0].astype(jnp.float32)).astype(low_type)
            upward = (grad_act * factors[2 * n + 1][0].astype(jnp.float32)).astype(low_type)
            grads[2 * n][0] = gate
            grads[2 * n + 1][0] = upward
            term = jnp.concatenate(
                [
                    product_with_transpose(gate, block[:, :units])
                    + product_with_transpose(upward, block[:, units:])
                    for block in joint_refs[firsts[n] : firsts[n] + len(joint_ws[n])]
                ],
                axis=1,
            )
            total = term if total is None else total + term
        n = 0
        for i, group in enumerate(cuts):
            start = 0
            for size in group:

                @pl.when(pl.program_id(0) == i)
                def _(out=outs[n], start=start, size=size):
                    out[...] = total[start : start + size].astype(low_type)

                start += size
                n += 1

    narrow = token_block(rows, units)
    shapes = [(size, depth) for group in cuts for size in group]
    outs = call_kernel(
        kernel,
        [*tokens, *halves[0], *halves[1], *down_ws, *joint_flat],
        [in_place] * count
        + [narrow] * 4
        + [resident(w.shape) for w in (*down_ws, *joint_flat)],
        [(narrow, ((chips, rows, units), low_type))] * 4
        + [(resident(shape), (shape, low_type)) for shape in shapes],
        0,
        "gated_backward",
        grid=(chips,),
        scratch=token_scratch(chips, rows, depth),
    )
    return outs[:2], outs[2:4], as_groups(outs[4:], cuts)


def as_groups(pieces, cuts):
    groups, n = [], 0
    for group in cuts:
        groups.append(list(pieces[n : n + len(group)]))
        n += len(group)
    return groups


def down_forward(acts, down_ws):
    chips, rows, units = acts[0].shape
    depth = down_ws[0].shape[1]

    def kernel(*refs):
        total = plain_product(refs[0][0], refs[2][...]) + plain_product(refs[1][0], refs[3][...])
        for i, out in enumerate(refs[4:]):

            @pl.when(pl.program_id(0) == i)
            def _(out=out):
                out[...] = total.astype(low_type)

    act = token_block(rows, units)
    return call_kernel(
        kernel,
        [*acts, *down_ws],
        [act, act] + [resident((units, depth))] * 2,
        [(resident((rows, depth)), ((rows, depth), low_type))] * chips,
        0,
        "down_forward",
        grid=(chips,),
    )


def weight_gradient(xs, grads, steps):
    chips, rows, depth = xs[0].shape
    units = grads[0].shape[2]
    width = depth // steps

    def kernel(*refs):
        terms = [
            product_over_rows(
                refs[n][...].reshape(chips * rows, width),
                refs[2 + n][...].reshape(chips * rows, units),
            )
            for n in range(2)
        ]
        refs[4][...] = (terms[0] + terms[1]).astype(low_type)

    return call_kernel(
        kernel,
        [*xs, *grads],
        [pl.BlockSpec((chips, rows, width), lambda i: (0, 0, i))] * 2
        + [resident(grads[0].shape)] * 2,
        [(pl.BlockSpec((width, units), lambda i: (i, 0)), ((depth, units), low_type))],
        0,
        "weight_gradient",
        grid=(steps,),
    )[0]


def down_gradients(acts, grads, steps):
    chips, rows, units = acts[0].shape
    depth = grads[0].shape[1]
    width = depth // steps
    count = len(grads)

    def kernel(*refs):
        act_refs, outs, (own, sems) = refs[count : count + 2], refs[count + 2 : -2], refs[-2:]
        step = pl.program_id(0)

        @pl.when(step == 0)
        def _():
            for copy in piece_copies(piece_rows(chips, rows, count), refs[:count], own, sems):
                copy.start()
            for i in range(chips):
                block = own.at[pl.ds(i * rows, rows)]
                pltpu.make_async_copy(block, block, sems.at[i]).wait()

        right = own[:, pl.ds(pl.multiple_of(step * width, width), width)]
        for act, out in zip(act_refs, outs, strict=True):
            out[...] = product_over_rows(act[...].reshape(chips * rows, units), right).astype(
                low_type
            )

    out = (pl.BlockSpec((units, width), lambda i: (0, i)), ((units, depth), low_type))
    return call_kernel(
        kernel,
        [*grads, *acts],
        [in_place] * count + [resident(acts[0].shape)] * 2,
        [out] * 2,
        0,
        "down_gradients",
        grid=(steps,),
        scratch=token_scratch(chips, rows, depth),
    )


def plane_place():
    rep = lax.axis_index("rep")
    return jnp.stack([rep // 2, rep % 2]).astype(jnp.int32)


def both_cores(pieces):
    return pieces + [swap(stacked(pieces), 1)]


def plane_scratch(chips, rows, width):
    return [
        pltpu.VMEM((2, chips * rows, width), low_type),
        pltpu.SemaphoreType.DMA((2, chips)),
    ]


def load_plane(chips, rows, refs, target, sems):
    @pl.when(pl.program_id(0) == 0)
    def _():
        copies = piece_copies(
            piece_rows(chips, rows, len(refs) - 1), refs[:-1], target.at[0], sems.at[0]
        )
        copies.append(pltpu.make_async_copy(refs[-1], target.at[1], sems.at[1, 0]))
        for copy in copies:
            copy.start()
        for i in range(chips):
            block = target.at[0, pl.ds(i * rows, rows)]
            pltpu.make_async_copy(block, block, sems.at[0, i]).wait()
        pltpu.make_async_copy(target.at[1], target.at[1], sems.at[1, 0]).wait()


def whole_columns(pieces, share):
    size, chips = lax.axis_size("shard"), lax.axis_size("rep") // 2
    rows, width = pieces[0].shape
    step_rows = rows // 4

    def kernel(at, *refs):
        out, target, sems = refs[-3:]
        load_plane(chips, rows, refs[:-3], target, sems)
        step = pl.program_id(0)
        for j in range(2 * chips):
            start = (at[0] ^ (j // 2)) * rows + step * step_rows
            own = target[at[1] ^ (j % 2), pl.ds(pl.multiple_of(start, 16), step_rows), :]
            own = own.astype(jnp.float32)
            for z in range(size):
                first = (z * 2 * chips + j) * share
                out[:, first : first + share] = own[:, z * width // size :][:, :share]

    wide = 2 * chips * size * share
    return call_kernel(
        kernel,
        [plane_place(), *pieces],
        [in_place] * len(pieces),
        [(pl.BlockSpec((step_rows, wide), lambda i, at: (i, 0)), ((rows, wide), jnp.float32))],
        0,
        "whole_columns",
        grid=(4,),
        prefetch=1,
        scratch=plane_scratch(chips, rows, width),
    )[0]


def whole_rows(pieces, share):
    chips = lax.axis_size("rep") // 2
    rows, width = pieces[0].shape

    def kernel(at, *refs):
        out, target, sems = refs[-3:]
        load_plane(chips, rows, refs[:-3], target, sems)
        j = pl.program_id(0)
        start = pl.multiple_of((at[0] ^ (j // 2)) * rows, 32)
        own = target[at[1] ^ (j % 2), pl.ds(start, rows), :].astype(jnp.float32)
        out[0] = own[:share]

    shape = (2 * chips, share, width)
    return call_kernel(
        kernel,
        [plane_place(), *pieces],
        [in_place] * len(pieces),
        [(pl.BlockSpec((1, share, width), lambda j, at: (j, 0, 0)), (shape, jnp.float32))],
        0,
        "whole_rows",
        grid=(2 * chips,),
        prefetch=1,
        scratch=plane_scratch(chips, rows, width),
    )[0].reshape(2 * chips * share, width)


def rows_of(values, width):
    rows = -(-values.shape[0] // width)
    block = jnp.pad(values, (0, rows * width - values.shape[0])).reshape(rows, width)
    return jnp.pad(block, ((0, -rows % 16), (0, 0)))


def in_shard_order(parts):
    size, here = lax.axis_size("shard"), lax.axis_index("shard")
    twice = jnp.concatenate(parts + parts)
    run = parts[0].shape[0]
    return lax.dynamic_slice_in_dim(twice, (size - here) * run, size * run, 0)


def padded(share):
    return -(-share // 32) * 32


def own_columns(weight):
    size, reps = lax.axis_size("shard"), lax.axis_size("rep")
    run = weight.shape[1] // size
    share = run // reps
    rep = lax.axis_index("rep")
    none = jnp.zeros((weight.shape[0], padded(share) - share), weight.dtype)
    parts = []
    for z in range(size):
        parts += [lax.dynamic_slice_in_dim(weight, z * run + rep * share, share, 1), none]
    return jnp.concatenate(parts, axis=1)


def own_rows(weight):
    share = weight.shape[0] // lax.axis_size("rep")
    own = lax.dynamic_slice_in_dim(weight, lax.axis_index("rep") * share, share, 0)
    return jnp.pad(own, ((0, padded(share) - share), (0, 0)))


def scatter_group(partial):
    return lax.psum_scatter(partial, "shard", scatter_dimension=0, tiled=True)


def local(
    tokens,
    norm_gains,
    w_query,
    w_key,
    w_value,
    w_out,
    w_gate,
    w_up,
    w_down,
    seq_lengths,
    seq_device,
    cotangent,
):
    row_total = tokens.shape[0]
    size, reps = lax.axis_size("shard"), lax.axis_size("rep")
    chips = reps // 2
    rep = lax.axis_index("rep")
    device = rep * size + lax.axis_index("shard")
    query_width, key_width = HEADS * HEAD, KV_HEADS * HEAD

    w_joint = jnp.concatenate([w_query, w_key, w_value], axis=1)
    joint, outer = Tiles(w_joint), Tiles(w_out)
    joint_tile = jnp.concatenate([joint.own(w_joint), rows_of(norm_gains, joint.width)], axis=0)
    joint_slots = [from_ahead(joint_tile, k) for k in range(1, size)]
    gated_own = jnp.concatenate([own_columns(w_gate), own_columns(w_up)], axis=1)
    live, segment, position = layout(seq_lengths, seq_device, device, row_total)
    cotangent_live = jnp.where(live[:, None], cotangent, jnp.zeros_like(cotangent))
    gated_own, down_own, joint_slots, out_tile = fence(
        gated_own, own_rows(w_down), joint_slots, outer.own(w_out)
    )
    gather_shards = lambda own: lax.all_gather(own, "shard", axis=0, tiled=True)
    gated_w, down_w = gather_shards(gated_own), gather_shards(down_own)
    joint_tiles = jnp.concatenate([slot[: joint.part] for slot in joint_slots], axis=0)
    joint_near = near_groups(joint_tiles, joint.members)
    out_slots = [from_ahead(out_tile, k) for k in range(1, size)]
    gains = in_shard_order(
        [norm_gains]
        + [slot[joint.part :].reshape(-1)[: norm_gains.shape[0]] for slot in joint_slots]
    )
    joint_near, out_slots, gains = fence(joint_near, out_slots, gains)
    out_tiles = jnp.concatenate(out_slots, axis=0)
    joint_far = far_group(joint_near, joint.members)
    if joint_far:
        joint_far = [jnp.concatenate(joint_far, axis=0)]
    joint_pieces = joint.across([joint_tiles] + joint_near + joint_far)

    cosine, sine = rotary_tables(position, HEAD)
    gains = gains.astype(jnp.float32)[None]
    gain_in = gains[:, :D]
    gain_ff = gains[:, D + 2 * HEAD :]
    shared = (
        gains[:, D : D + HEAD],
        gains[:, D + HEAD : D + 2 * HEAD],
        jnp.concatenate([cosine, cosine], axis=1),
        jnp.concatenate([0.0 - sine, sine], axis=1),
        segment[:, None],
        segment[None, :],
    )
    joint_pieces, shared, out_tiles = fence(joint_pieces, shared, out_tiles)
    out_groups = all_groups(out_tiles, outer.members)
    joint_proj, normed_in = attention_input(joint, tokens, gain_in, w_joint, joint_pieces)

    joint_proj, normed_in = fence(joint_proj, normed_in)
    half_steps = KV_HEADS // 4
    attended_early, inverse_early = attend(joint_proj, shared, 0, half_steps)

    joint_proj, attended_early, out_groups, normed_in = fence(
        joint_proj, attended_early, out_groups, normed_in
    )
    out_pieces = outer.across(out_groups)
    normed_near = near_groups(normed_in, joint.members)
    attended_late, inverse_late = attend(joint_proj, shared, half_steps, half_steps)
    attended = jnp.concatenate([attended_early, attended_late], axis=1)

    attended, out_pieces = fence(attended, out_pieces)
    hidden, normed_ff = attention_output(outer, attended, tokens, gain_ff, w_out, out_pieces)

    normed_ff, normed_near = fence(normed_ff, normed_near)
    ff_near = near_groups(normed_ff, 2)

    ff_near, gated_w, cotangent_live = fence(ff_near, gated_w, cotangent_live)
    ff_far = far_group(ff_near, 2)
    grad_mixed = all_groups(cotangent_live, 2)
    half = gated_w.shape[0] // 2
    halves = (gated_w[:half], gated_w[half:])
    ff_far, gated_w, halves, normed_near = fence(ff_far, gated_w, halves, normed_near)
    ff_tokens = [normed_ff] + ff_near + ff_far
    gated_ws = ([gated_w], [swap(part, 1) for part in halves])
    *ours, group_tokens = gated_forward(ff_tokens, gated_ws[0], True)

    ours, gated_ws, group_tokens, attended = fence(ours, gated_ws, group_tokens, attended)
    attended_near = near_groups(attended, outer.members)
    theirs = gated_forward(ff_tokens, gated_ws[1], False)

    theirs, grad_mixed = fence(theirs, grad_mixed)
    grad_downs = down_gradients((ours[0], theirs[0]), grad_mixed, 2)

    grad_downs, down_w, attended_near = fence(grad_downs, down_w, attended_near)
    down_ws = (down_w, swap(down_w, 1))
    other_down = swap(grad_downs[1], 1)
    attended_far = far_group(attended_near, outer.members)

    down_ws, ours, theirs, normed_near = fence(down_ws, ours, theirs, normed_near)
    normed_far = far_group(normed_near, joint.members)
    down_parts = down_forward((ours[0], theirs[0]), down_ws)

    down_parts, other_down, attended_far, normed_far, group_tokens = fence(
        down_parts, other_down, attended_far, normed_far, group_tokens
    )
    attended_rows = [attended] + attended_near + attended_far
    normed_rows = [normed_in] + normed_near + normed_far
    all_tokens = (group_tokens, swap(group_tokens, 1))
    down_terms = sum_terms(down_parts, 2)
    grad_down = grad_downs[0].astype(jnp.float32) + other_down.astype(jnp.float32)
    grad_down = scatter_group(grad_down.astype(low_type))
    our_grads, their_grads, grad_x = gated_backward(
        grad_mixed, (ours[1:], theirs[1:]), down_ws, gated_ws
    )

    grad_x, our_grads, their_grads, all_tokens, down_terms = fence(
        grad_x, our_grads, their_grads, all_tokens, down_terms
    )
    grad_x_far = far_terms(grad_x, 2)
    their_grads = [swap(part, 1) for part in their_grads]
    grad_gate = weight_gradient(all_tokens, (our_grads[0], their_grads[0]), 4)

    grad_x_far, grad_gate, their_grads, down_terms, grad_down = fence(
        grad_x_far, grad_gate, their_grads, down_terms, grad_down
    )
    grad_terms = near_terms(grad_x, grad_x_far, 2)
    down_near = near_groups(grad_down, 2)
    grad_gate = scatter_group(grad_gate)
    grad_up = weight_gradient(all_tokens, (our_grads[1], their_grads[1]), 4)

    grad_terms, grad_up = fence(grad_terms, grad_up)
    grad_up = scatter_group(grad_up)
    grad_hidden, grad_gain_ff, grad_attended, *cuts = attention_output_gradient(
        outer, grad_terms, cotangent_live, hidden, gain_ff, w_out, out_pieces
    )

    cuts, grad_attended, down_near = fence(cuts, grad_attended, down_near)
    down_far = far_group(down_near, 2)
    out_runs = outer.group_columns(cuts)
    half_steps = KV_HEADS // 4
    early = attend_gradient(
        joint_proj, attended, inverse_early, grad_attended, shared, 0, half_steps
    )

    early, out_runs, down_far, grad_gate, grad_attended = fence(
        early, out_runs, down_far, grad_gate, grad_attended
    )
    gate_near = near_groups(grad_gate, 2)
    late = attend_gradient(
        joint_proj, attended, inverse_late, grad_attended, shared, half_steps, half_steps
    )

    early, late, gate_near = fence(early, late, gate_near)
    head_gains = early[3] + late[3]
    parts = [part for n in range(3) for part in (early[n], late[n])]
    grad_joint_low = jnp.concatenate(parts, axis=1)
    cuts, grad_joint_low = fence(joint.cut_columns(grad_joint_low), grad_joint_low)
    joint_runs = joint.group_columns(cuts)
    down_pieces = both_cores([grad_down] + down_near + down_far)
    grad_tokens, grad_gain_in = attention_input_gradient(
        joint, grad_joint_low, grad_hidden, tokens, gain_in, w_joint, joint_pieces
    )

    joint_runs, grad_gain_in, out_runs, down_pieces, gate_near = fence(
        joint_runs, grad_gain_in, out_runs, down_pieces, gate_near
    )
    gate_far = far_group(gate_near, 2)
    sums = outer.tile(attended_rows, out_runs)
    sums = joint.tile(normed_rows, joint_runs, sums)
    grad_gains = jnp.concatenate(
        [grad_gain_in, head_gains[0:1], head_gains[1:2], grad_gain_ff], axis=1
    )[0]
    extra = joint.extra_rows(grad_gains, sums[0].shape[1])

    sums, gate_far = fence(sums, gate_far)
    sums = sums[:1] + tuple(swap(part, h) for h, part in enumerate(sums) if h)
    gate_pieces = both_cores([grad_gate] + gate_near + gate_far)

    sums, down_pieces, gate_pieces, down_terms = fence(sums, down_pieces, gate_pieces, down_terms)
    own, sent = joint.send(sums, extra)
    up_near = near_groups(grad_up, 2)
    whole_down = whole_rows(down_pieces, w_down.shape[0] // reps)
    whole_gate = whole_columns(gate_pieces, w_down.shape[0] // reps)

    mixed_full = hidden
    for term in down_terms:
        mixed_full = mixed_full + term.astype(jnp.float32)
    mixed = jnp.where(live[:, None], mixed_full, jnp.zeros_like(mixed_full)).astype(jnp.bfloat16)

    whole_down, whole_gate, up_near, mixed = fence(whole_down, whole_gate, up_near, mixed)
    up_far = far_group(up_near, 2)

    own, sent, up_far = fence(own, sent, up_far)
    total = own
    for part in sent:
        total = total + part.astype(jnp.float32)
    total_groups = all_groups(total.astype(low_type), joint.members)
    up_pieces = both_cores([grad_up] + up_near + up_far)

    up_pieces = fence(*up_pieces)
    whole_up = whole_columns(up_pieces, w_down.shape[0] // reps)

    total_groups, whole_up = fence(total_groups, whole_up)
    whole_pieces = joint.across(total_groups)
    *grad_joint, grad_out_w, beneath = joint.whole(
        whole_pieces, ((query_width, key_width, key_width), (D,))
    )
    grad_gains = beneath.reshape(-1)[: norm_gains.shape[0]]
    share = w_down.shape[0] // reps
    return (
        mixed,
        grad_tokens,
        grad_gains,
        *grad_joint,
        grad_out_w,
        whole_gate,
        whole_up,
        whole_down,
    )


def solution(mesh):
    return jax.shard_map(
        local,
        mesh=mesh,
        in_specs=(
            P(("rep", "shard"), None),
            P("shard"),
            P("shard", None),
            P("shard", None),
            P("shard", None),
            P("shard", None),
            P("shard", None),
            P("shard", None),
            P("shard", None),
            P(),
            P(),
            P(("rep", "shard"), None),
        ),
        out_specs=(
            P(("rep", "shard"), None),
            P(("rep", "shard"), None),
            P("shard"),
            P("shard", None),
            P("shard", None),
            P("shard", None),
            P("shard", None),
            P("shard", None),
            P("shard", None),
            P("shard", None),
        ),
        check_vma=False,
    )
```
